32 devices in a mesh: rows: 8 (over y, x, core), heads: 4 (over z).
Axes of the slice: x: 2, y: 2, z: 4, core: 2. Of those that a mesh axis runs over, the one named last changes fastest.
Arguments:
- tokens: bfloat16 [32, 512, 1024], P('rows', 'heads'), may hold values from -6 to 6
- doc_lengths: int32 [32, 4], P('rows'), may hold values from 1 to 509, as said below
- cotangent: bfloat16 [32, 512, 1024], P('rows', 'heads'), may hold values from -6 to 6
- w_query: bfloat16 [1024, 1024], P('rows'), may hold values from -0.1875 to 0.1875
- w_key: bfloat16 [1024, 1024], P('rows'), may hold values from -0.1875 to 0.1875
- w_value: bfloat16 [1024, 1024], P('rows'), may hold values from -0.1875 to 0.1875
- w_gate: bfloat16 [1024, 1024], P('rows'), may hold values from -0.1875 to 0.1875
- w_out: bfloat16 [1024, 1024], P('rows'), may hold values from -0.3125 to 0.3125
- w_left: bfloat16 [1024, 2816], P('rows'), may hold values from -0.1875 to 0.1875
- w_right: bfloat16 [1024, 2816], P('rows'), may hold values from -0.1875 to 0.1875
- w_down: bfloat16 [2816, 1024], P('rows'), may hold values from -0.109375 to 0.109375
Outputs:
- activations: bfloat16 [32, 512, 1024], P('rows', 'heads')
- input_grad: float32 [32, 512, 1024], P('rows', 'heads')
- grad_query: float32 [1024, 1024], P('rows', 'heads')
- grad_key: float32 [1024, 1024], P('rows', 'heads')
- grad_value: float32 [1024, 1024], P('rows', 'heads')
- grad_gate: float32 [1024, 1024], P('rows', 'heads')
- grad_out: float32 [1024, 1024], P('rows', 'heads')
- grad_left: float32 [1024, 2816], P('rows', 'heads')
- grad_right: float32 [1024, 2816], P('rows', 'heads')
- grad_down: float32 [2816, 1024], P('rows', 'heads')
The draws below stay inside these ranges and needn't reach their ends.
Inputs may be any that keep to these rules, and one draw needn't show every extreme that they name: `doc_lengths`: each row holds 4 documents whose lengths sum to 512; in each group of 4 rows along heads, one row, drawn from the seed, holds a document of 509 tokens.
All inputs are finite; a program needn't handle non-finite values.
Results may differ from the reference program's by a relative error of at most 0.012.
Values may be sent and summed in bfloat16 or wider, within the bound.
No kernel may reach another device: no remote copies, remote signals or barrier semaphores. Data moves between devices by JAX's collectives and lax.ppermute only.
A program may use at most 256 MiB of HBM per device.

```python
import math
import jax
import jax.numpy as jnp
from jax import lax

D = 1024
HEADS = 8
HEAD_DIM = 128
FF = 2816
SEQS = 4
SEQ = 512
NSEQ = 32


def draw_doc_lengths(key, part):
    key = jax.random.fold_in(key, 11)
    groups = NSEQ // SEQS
    cut_key, pick_key = jax.random.split(key)
    raw = jnp.sort(jax.random.randint(cut_key, (NSEQ, 3), 1, SEQ - 2), axis=-1)
    cuts = raw + jnp.arange(3, dtype=jnp.int32)[None, :]
    first = cuts[:, 0]
    second = cuts[:, 1] - cuts[:, 0]
    third = cuts[:, 2] - cuts[:, 1]
    fourth = SEQ - cuts[:, 2]
    lengths = jnp.stack([first, second, third, fourth], axis=-1).astype(jnp.int32)
    chosen = jax.random.randint(pick_key, (groups,), 0, SEQS)
    row_ids = jnp.arange(NSEQ, dtype=jnp.int32)
    marked = row_ids % SEQS == chosen[row_ids // SEQS]
    longest = jnp.array([1, SEQ - 3, 1, 1], dtype=jnp.int32)
    return jnp.where(marked[:, None], longest[None, :], lengths).astype(jnp.int32)


def steps_of(rng, shape, pieces, least, largest):
    loudness = 1.0
    for axis_at, shards_of in pieces:
        draws = jax.random.uniform(jax.random.fold_in(jax.random.fold_in(rng, 6), axis_at), (shards_of,), jnp.float32, least / len(pieces), largest / len(pieces))
        loudness = loudness * jnp.repeat(jnp.exp(draws), shape[axis_at] // shards_of).reshape((-1,) + (1,) * (len(shape) - 1 - axis_at))
    return loudness


def bell_draw(rng, extent, scale, bound, cuts=(), held_as=jnp.bfloat16):
    result = scale * jax.random.normal(rng, extent, jnp.float32)
    if cuts:
        result = result * steps_of(rng, extent, cuts, -0.22, 0.18)
    return jnp.clip(result, -bound, bound).astype(held_as)


def setup_inputs(seed: int = 0) -> dict:
    seeds = jax.random.split(jax.random.key(seed), 12)
    tokens = bell_draw(seeds[0], (NSEQ, SEQ, D), 1.0, 6.0, ((0, 8), (1, 4)))
    doc_lengths = draw_doc_lengths(jax.random.fold_in(seeds[11], 71), 0)
    cotangent = bell_draw(seeds[2], (NSEQ, SEQ, D), 1.0, 6.0, ((0, 8), (1, 4)))
    w_query = bell_draw(seeds[3], (D, D), D ** -0.5, 0.1875, ((0, 8),))
    w_key = bell_draw(seeds[4], (D, D), D ** -0.5, 0.1875, ((0, 8),))
    w_value = bell_draw(seeds[5], (D, D), D ** -0.5, 0.1875, ((0, 8),))
    w_gate = bell_draw(seeds[6], (D, D), D ** -0.5, 0.1875, ((0, 8),))
    w_out = bell_draw(seeds[7], (D, D), (D // 3) ** -0.5, 0.3125, ((0, 8),))
    w_left = bell_draw(seeds[8], (D, FF), D ** -0.5, 0.1875, ((0, 8),))
    w_right = bell_draw(seeds[9], (D, FF), D ** -0.5, 0.1875, ((0, 8),))
    w_down = bell_draw(seeds[10], (FF, D), FF ** -0.5, 0.109375, ((0, 8),))
    return {"tokens": tokens, "doc_lengths": doc_lengths, "cotangent": cotangent, "w_query": w_query, "w_key": w_key, "w_value": w_value, "w_gate": w_gate, "w_out": w_out, "w_left": w_left, "w_right": w_right, "w_down": w_down}


EPS = 1e-06
HIGH = lax.Precision.HIGHEST

@jax.custom_vjp
def low(v):
    return lax.optimization_barrier(v.astype(jnp.bfloat16)).astype(jnp.float32)

@jax.custom_vjp
def low_back(v):
    return v

def low_keep(v):
    return (low(v), None)

def low_pass(kept, grad):
    return (grad,)

def back_keep(v):
    return (v, None)

def back_low(kept, grad):
    return (low(grad),)
low.defvjp(low_keep, low_pass)
low_back.defvjp(back_keep, back_low)

def srms(v):
    return v * lax.rsqrt(lax.optimization_barrier(jnp.mean(v * v, axis=-1, keepdims=True)) + EPS)

def project(a, w):
    return jnp.einsum('std,de->ste', a, w, precision=HIGH)

def document_ids(lengths, length):
    ends = jnp.cumsum(lengths, axis=-1, dtype=jnp.int32)[:, :-1]
    places = jnp.arange(length, dtype=jnp.int32)
    return lax.optimization_barrier(jnp.sum((places[None, :, None] >= ends[:, None, :]).astype(jnp.int32), axis=-1))

def rotate(a):
    width = a.shape[-1]
    places = jnp.arange(a.shape[1], dtype=jnp.float32)
    theta = jnp.exp(-math.log(10000.0) * jnp.arange(width, dtype=jnp.float32) / width)
    angle = places[:, None] * theta[None, :]
    cosine = jnp.cos(angle)[None, :, None, :]
    sine = jnp.sin(angle)[None, :, None, :]
    return jnp.concatenate([a * cosine, a * sine], axis=-1)

def head_mix(q_rot, k_rot, values, docs, slope):
    length = q_rot.shape[1]
    places = jnp.arange(length, dtype=jnp.int32)
    gap = places[:, None] - places[None, :]
    keep = (gap >= 0)[None] & (docs[:, :, None] == docs[:, None, :])
    spread = jnp.maximum(gap, 0).astype(jnp.float32)
    decay = jnp.where(keep, jnp.exp(-slope * spread)[None], jnp.float32(0.0))
    scores = jnp.einsum('sie,sje->sij', q_rot, k_rot, precision=HIGH)
    return jnp.einsum('sij,sje->sie', scores * decay, values, precision=HIGH)

def layer(xs, w_query, w_key, w_value, w_gate, w_out, w_left, w_right, w_down, docs):
    seqs, length = (xs.shape[0], xs.shape[1])
    h_in = low(srms(xs))
    q_pre = low_back(project(h_in, w_query))
    k_pre = low_back(project(h_in, w_key))
    v_pre = low_back(project(h_in, w_value))
    u_pre = low_back(project(h_in, w_gate))
    query = low_back(low(jax.nn.silu(q_pre)))
    key_part = low_back(low(jax.nn.silu(k_pre)))
    value = low_back(low(v_pre))
    gate = jax.nn.silu(u_pre)
    shape4 = (seqs, length, HEADS, HEAD_DIM)
    q_rot = rotate(query.reshape(shape4)).transpose(2, 0, 1, 3)
    k_rot = rotate(key_part.reshape(shape4)).transpose(2, 0, 1, 3)
    v_heads = value.reshape(shape4).transpose(2, 0, 1, 3)
    slopes = jnp.exp2(-8.0 * jnp.arange(1, HEADS + 1, dtype=jnp.float32) / HEADS)
    mapped = jax.checkpoint(head_mix)
    mixed = lax.map(lambda item: mapped(item[0], item[1], item[2], docs, item[3]), (q_rot, k_rot, v_heads, slopes))
    mixed = mixed.transpose(1, 2, 0, 3).reshape(seqs, length, D)
    mixed = low_back(low(mixed))
    gated = low(srms(mixed) * gate)
    branch = low_back(project(gated, w_out))
    x_mid = xs + branch
    h_mid = low(srms(x_mid))
    left = low_back(project(h_mid, w_left))
    right = low_back(project(h_mid, w_right))
    product = low(left * right)
    return x_mid + low_back(project(product, w_down))

def reference(tokens, doc_lengths, cotangent, w_query, w_key, w_value, w_gate, w_out, w_left, w_right, w_down):
    weights = tuple((w.astype(jnp.float32) for w in (w_query, w_key, w_value, w_gate, w_out, w_left, w_right, w_down)))
    groups = NSEQ // SEQS
    xs = tokens.astype(jnp.float32).reshape(groups, SEQS, SEQ, D)
    cs = cotangent.astype(jnp.float32).reshape(groups, SEQS, SEQ, D)
    ids = document_ids(doc_lengths, SEQ).reshape(groups, SEQS, SEQ)

    def step(totals, item):
        x_group, c_group, d_group = item
        out, back = jax.vjp(lambda xv, *ws: layer(xv, *ws, d_group), x_group, *weights)
        grads = back(c_group)
        return (tuple((t + g for t, g in zip(totals, grads[1:]))), (out, grads[0]))
    zeros = tuple((jnp.zeros_like(w) for w in weights))
    totals, (outs, dxs) = lax.scan(step, zeros, (xs, cs, ids))
    activations = outs.reshape(NSEQ, SEQ, D).astype(jnp.bfloat16)
    input_grad = dxs.reshape(NSEQ, SEQ, D)
    return (activations, input_grad, totals[0], totals[1], totals[2], totals[3], totals[4], totals[5], totals[6], totals[7])
```

```python
import functools
import math
import types

import jax
import jax.numpy as jnp
from jax import lax
from jax.experimental import pallas as pl
from jax.experimental.pallas import tpu as pltpu
from jax.sharding import PartitionSpec as P

HEADS = 8
HEAD_DIM = 128
EPS = 1e-06
F32 = jnp.float32
BF16 = jnp.bfloat16
VMEM_LIMIT = 48 << 20

BITS = (0, 2, 4, 6, 1, 3, 5, 7)
BITS_X = (0, 4, 2, 6, 1, 5, 3, 7)
BITS_Y = (0, 2, 4, 6, 1, 3, 5, 7)


def after(value, *others):
    return lax.optimization_barrier((value,) + others)[0]


def dot(a, b, dims, out=F32):
    return lax.dot_general(a, b, (dims, ((), ())), preferred_element_type=F32).astype(out)


NN = ((1,), (0,))
NT = ((1,), (1,))
TN = ((0,), (0,))


def swap(value, bit, size):
    return lax.ppermute(value, "rows", [(i, i ^ bit) for i in range(size)])


def place_body(rows, splits, order, *refs):
    pieces, outs, sems = refs[:10], refs[10 : 10 + len(splits)], refs[-1]
    half = sum(w for _, _, w in splits) // 2
    copies = []
    for i, (at, to, width) in enumerate(splits):
        for k in range(8):
            core, chip = k // 4, k % 4
            source = pieces[5 * core + chip]
            begin = at
            if chip == 3 and at >= half:
                source, begin = pieces[5 * core + 4], at - half
            copies.append(
                pltpu.make_async_copy(
                    source.at[:, begin : begin + width],
                    outs[i].at[at_block(order, BITS[k], rows), to : to + width],
                    sems.at[i, k],
                )
            )
    for copy in copies:
        copy.start()
    for copy in copies:
        copy.wait()


def pack_body(splits, order, *refs):
    count = len(splits)
    ins, out, sems = refs[:count], refs[count], refs[-1]
    copies = [
        pltpu.make_async_copy(
            ins[i].at[:, to : to + width], out.at[:, at : at + width], sems.at[i]
        )
        for i, (at, to, width) in enumerate(splits)
    ]
    for copy in copies:
        copy.start()
    for copy in copies:
        copy.wait()


def whole_spec(rows, width):
    return pl.BlockSpec((rows, width), lambda i, *_: (0, 0))


ANYWHERE = pl.BlockSpec(memory_space=pltpu.HBM)


def pack(splits, arrays, order):
    rows = arrays[0].shape[0]
    width = sum(w for _, _, w in splits)
    (out,) = call(
        functools.partial(pack_body, splits), (1,), order, [(a, ANYWHERE) for a in arrays],
        [((rows, width), BF16, whole_spec(rows, width))],
        scratch=[pltpu.SemaphoreType.DMA((len(splits),))],
    )
    return out


class Clock:
    def __init__(self, start):
        self.token = start

    def tick(self, *places):
        held = [getattr(o, n) for o, n in places]
        held, self.token = lax.optimization_barrier((held, self.token))
        for (o, n), value in zip(places, held):
            setattr(o, n, value)


class Gather:
    def __init__(self, piece, splits, owners, widths):
        self.piece, self.splits, self.owners, self.widths = piece, splits, owners, widths

    def first(self):
        self.near = [swap(self.piece, 2, 8), swap(self.piece, 4, 8)]

    def second(self):
        half = self.piece.shape[1] // 2
        self.far = [swap(self.near[0][:, :half], 4, 8), swap(self.near[1][:, half:], 2, 8)]

    def cross_first(self):
        self.other = [swap(p, 1, 8) for p in [self.piece] + self.near]

    def cross_second(self):
        self.other_far = [swap(p, 1, 8) for p in self.far]

    def whole(self, order):
        rows, splits, owners = self.piece.shape[0], self.splits, self.owners
        pieces = [self.piece] + self.near + self.far + self.other + self.other_far
        count = len(self.widths)

        def body(order, *refs):
            outs = refs[10 : 10 + count]
            place_body(rows, splits, order, *refs[:10], *[outs[o] for o in owners], refs[-1])

        return call(
            body, (1,), order, [(p, ANYWHERE) for p in pieces],
            [((8 * rows, w), BF16, whole_spec(8 * rows, w)) for w in self.widths],
            scratch=[pltpu.SemaphoreType.DMA((len(splits), 8))],
        )


def add(one, two, out=BF16):
    return (one.astype(F32) + two.astype(F32)).astype(out)


class Reduce:
    def __init__(self, sends, keeps, bits):
        self.sends, self.keeps, self.bits = list(sends), list(keeps), list(bits)

    def core(self):
        self.theirs = [swap(s, 1, 8) for s in self.sends]

    def join(self):
        self.totals = [k(t) for k, t in zip(self.keeps, self.theirs)]

    def first(self):
        self.got = [swap(t[t.shape[0] // 2 :], b, 8) for t, b in zip(self.totals, self.bits)]

    def join_first(self):
        self.parts = [add(t[: t.shape[0] // 2], g) for t, g in zip(self.totals, self.got)]

    def second(self):
        self.got_last = [swap(p[p.shape[0] // 2 :], 6 - b, 8) for p, b in zip(self.parts, self.bits)]

    def join_second(self):
        self.sums = [
            add(p[: p.shape[0] // 2], g, F32) for p, g in zip(self.parts, self.got_last)
        ]


def column_block(s, here, bit):
    width = s.shape[1] // 4
    return lax.dynamic_slice_in_dim(s, (here ^ bit) * width, width, axis=1)


class Settle:
    def __init__(self, sums, here):
        self.widths = [s.shape[1] // 4 for s in sums]
        self.own = [column_block(s, here, 0) for s in sums]
        self.far = [column_block(s, here, 2) for s in sums]
        near = [column_block(s, here, 1) for s in sums] + [column_block(s, here, 3) for s in sums]
        self.out = jnp.concatenate([n.astype(BF16) for n in near], axis=1)

    def pass_on(self, bit):
        self.got = lax.ppermute(self.out, "heads", [(i, i ^ bit) for i in range(4)])

    def split(self, at=0):
        pieces = []
        for w in self.widths:
            pieces.append(self.got[:, at : at + w].astype(F32))
            at += w
        return pieces

    def join(self):
        self.own = [o + g for o, g in zip(self.own, self.split())]
        far = [o + g for o, g in zip(self.far, self.split(sum(self.widths)))]
        self.out = jnp.concatenate([f.astype(BF16) for f in far], axis=1)

    def result(self):
        return [o + g for o, g in zip(self.own, self.split())]


def at_block(order_ref, index, width):
    return pl.ds(pl.multiple_of(order_ref[index] * width, width), width)


def sigmoid(v):
    return 1.0 / (1.0 + jnp.exp(-v))


def swish_slope(v):
    sig = sigmoid(v)
    return sig * (1.0 + v * (1.0 - sig))


def call(body, grid, order, ins, outs, scratch=(), flops=0):
    moved = sum(a.size * a.dtype.itemsize for a, _ in ins) + sum(
        math.prod(s) * jnp.dtype(t).itemsize for s, t, _ in outs
    )
    return pl.pallas_call(
        body,
        grid_spec=pltpu.PrefetchScalarGridSpec(
            num_scalar_prefetch=1,
            grid=grid,
            in_specs=[spec for _, spec in ins],
            out_specs=[spec for _, _, spec in outs],
            scratch_shapes=list(scratch),
        ),
        out_shape=[jax.ShapeDtypeStruct(s, t) for s, t, _ in outs],
        compiler_params=pltpu.CompilerParams(vmem_limit_bytes=VMEM_LIMIT),
        cost_estimate=pl.CostEstimate(flops=0, bytes_accessed=0, transcendentals=0),
    )(order, *[a for a, _ in ins])


def rows_spec(count, width, column=0):
    return pl.BlockSpec((count, width), lambda i, *_: (i, column))


def spread(order, blocks, h, outs):
    outs[0][...] = h
    width = h.shape[1] // blocks
    for out, bits in zip(outs[1:], (BITS_X, BITS_Y)):
        for k in range(blocks):
            source = at_block(order, bits[k], width)
            out[:, k * width : (k + 1) * width] = outs[0][:, source]


def norm_body(blocks, order, x_ref, *outs):
    x = x_ref[...].astype(F32)
    scale = lax.rsqrt(jnp.mean(x * x, axis=-1, keepdims=True) + EPS)
    spread(order, blocks, (x * scale).astype(BF16), outs)


def mid_body(blocks, order, x_ref, b_ref, mid_ref, *outs):
    mid = x_ref[...].astype(F32) + b_ref[...]
    mid_ref[...] = mid
    scale = lax.rsqrt(jnp.mean(mid * mid, axis=-1, keepdims=True) + EPS)
    spread(order, blocks, (mid * scale).astype(BF16), outs)


def norm_back_body(order, v_ref, base_ref, g_ref, *outs):
    v = v_ref[...].astype(F32)
    g = g_ref[...]
    scale = lax.rsqrt(jnp.mean(v * v, axis=-1, keepdims=True) + EPS)
    inner = jnp.mean(g * v, axis=-1, keepdims=True) * (scale * scale * scale)
    total = base_ref[...].astype(F32) + scale * g - v * inner
    outs[0][...] = total
    if len(outs) > 1:
        outs[1][...] = total.astype(BF16)


def ramp(rows, start, sign, slope):
    place = lax.broadcasted_iota(jnp.int32, (rows, HEAD_DIM), 0).astype(F32)
    return jnp.exp(-slope * (start + sign * place))


def decays(ids_col, ids_row, slope):
    rows = ids_col.shape[0]
    gap = (
        lax.broadcasted_iota(jnp.int32, (rows, rows), 0)
        - lax.broadcasted_iota(jnp.int32, (rows, rows), 1)
    ).astype(F32)
    keep = (gap >= 0.0) & (ids_col == ids_row)
    return jnp.where(keep, jnp.exp(-slope * jnp.maximum(gap, 0.0)), 0.0)


def slope_of(head):
    return 2.0 ** (-8.0 * (head + 1) / HEADS)


def columns(head):
    return slice(head * HEAD_DIM, (head + 1) * HEAD_DIM)


def turned(a, cos, sin):
    return jnp.concatenate([a * cos, a * sin], axis=1)


def rounded_swish(v):
    return (v * sigmoid(v)).astype(BF16).astype(F32)


def fresh_body(order, k_ref, v_ref, cos_ref, sin_ref, tail_ref, state_ref):
    rows = k_ref.shape[1]
    cos, sin = cos_ref[...], sin_ref[...]
    tail = tail_ref[0]
    for head in range(HEADS):
        key = rounded_swish(k_ref[0, :, columns(head)])
        key = key * (ramp(rows, rows - 1.0, -1.0, slope_of(head)) * tail)
        value = v_ref[0, :, columns(head)].astype(BF16)
        state_ref[0, head] = dot(turned(key, cos, sin).astype(BF16), value, TN, BF16)


def mix_body(
    order, q_ref, k_ref, v_ref, u_ref, cos_ref, sin_ref, col_ref, row_ref, link_ref, s_ref,
    mix_ref, gated_ref, *ordered_refs,
):
    rows = q_ref.shape[1]
    cos, sin = cos_ref[...], sin_ref[...]
    ids_col, ids_row = col_ref[0], row_ref[0]
    link = link_ref[0]
    power = jnp.zeros((rows, 1), F32)
    for head in range(HEADS):
        cols = columns(head)
        slope = slope_of(head)
        rq = turned(rounded_swish(q_ref[0, :, cols]), cos, sin).astype(BF16)
        rk = turned(rounded_swish(k_ref[0, :, cols]), cos, sin).astype(BF16)
        value = v_ref[0, :, cols].astype(BF16)
        weights = (dot(rq, rk, NT) * decays(ids_col, ids_row, slope)).astype(BF16)
        mixed = dot(weights, value, NN) + dot(rq, s_ref[0, head], NN) * (
            ramp(rows, 1.0, 1.0, slope) * link
        )
        mixed = mixed.astype(BF16)
        mix_ref[0, :, cols] = mixed
        mixed = mixed.astype(F32)
        power += jnp.sum(mixed * mixed, axis=-1, keepdims=True)
    scale = lax.rsqrt(power / (HEADS * HEAD_DIM) + EPS)
    for head in range(HEADS):
        cols = columns(head)
        u = u_ref[0, :, cols]
        gated_ref[0, :, cols] = (
            mix_ref[0, :, cols].astype(F32) * scale * (u * sigmoid(u))
        ).astype(BF16)
    for out in ordered_refs:
        for k in range(HEADS):
            out[0, :, columns(k)] = gated_ref[0, :, at_block(order, BITS_X[k], HEAD_DIM)]


def gate_back_body(
    order, q_ref, u_ref, mix_ref, dg_ref, cos_ref, sin_ref, link_ref, du_ref, dm_ref, state_ref
):
    rows = q_ref.shape[1]
    cos, sin = cos_ref[...], sin_ref[...]
    link = link_ref[0]
    mix = mix_ref[0].astype(F32)
    scale = lax.rsqrt(jnp.mean(mix * mix, axis=-1, keepdims=True) + EPS)
    inner = jnp.zeros((rows, 1), F32)
    for head in range(HEADS):
        cols = columns(head)
        u = u_ref[0, :, cols]
        part = mix_ref[0, :, cols].astype(F32)
        dg = dg_ref[0, :, cols]
        sig = sigmoid(u)
        inner += jnp.sum(dg * (u * sig) * part, axis=-1, keepdims=True)
        du_ref[0, :, cols] = (dg * part * scale * (sig * (1.0 + u * (1.0 - sig)))).astype(BF16)
    inner = inner * (scale * scale * scale) / (HEADS * HEAD_DIM)
    for head in range(HEADS):
        cols = columns(head)
        u = u_ref[0, :, cols]
        part = mix_ref[0, :, cols].astype(F32)
        dg = dg_ref[0, :, cols]
        d_mix = (scale * (dg * (u * sigmoid(u))) - part * inner).astype(BF16)
        dm_ref[0, :, cols] = d_mix
        query = rounded_swish(q_ref[0, :, cols]) * (
            ramp(rows, 1.0, 1.0, slope_of(head)) * link
        )
        state_ref[0, head] = dot(turned(query, cos, sin).astype(BF16), d_mix, TN, BF16)


def mix_back_body(
    order, q_ref, k_ref, v_ref, dm_ref, cos_ref, sin_ref, col_ref, row_ref, link_ref, s_ref,
    dq_ref, dk_ref, dv_ref,
):
    rows = q_ref.shape[1]
    cos, sin = cos_ref[...], sin_ref[...]
    ids_col, ids_row = col_ref[0], row_ref[0]
    link = link_ref[0]
    for head in range(HEADS):
        cols = columns(head)
        slope = slope_of(head)
        q_pre = q_ref[0, :, cols]
        rq = turned(rounded_swish(q_pre), cos, sin).astype(BF16)
        rk = turned(rounded_swish(k_ref[0, :, cols]), cos, sin).astype(BF16)
        value = v_ref[0, :, cols].astype(BF16)
        d_mix = dm_ref[0, :, cols]
        decay = decays(ids_col, ids_row, slope)
        weights = (dot(rq, rk, NT) * decay).astype(BF16)
        d_scores = (dot(d_mix, value, NT) * decay).astype(BF16)
        enter = ramp(rows, 1.0, 1.0, slope) * link
        d_rq = dot(d_scores, rk, NN) + dot(d_mix, s_ref[0, head], NT) * jnp.concatenate(
            [enter, enter], axis=1
        )
        d_query = d_rq[:, :HEAD_DIM] * cos + d_rq[:, HEAD_DIM:] * sin
        dq_ref[0, :, cols] = (
            d_query.astype(BF16).astype(F32) * swish_slope(q_pre)
        ).astype(BF16)
        d_rk = dot(d_scores, rq, TN)
        dk_ref[0, :, cols] = d_rk[:, :HEAD_DIM] * cos + d_rk[:, HEAD_DIM:] * sin
        dv_ref[0, :, cols] = dot(weights, d_mix, TN)


def state_back_body(
    order, k_ref, v_ref, dk_ref, dv_ref, cos_ref, sin_ref, tail_ref, s_ref, dko_ref, dvo_ref
):
    rows = k_ref.shape[1]
    cos, sin = cos_ref[...], sin_ref[...]
    tail = tail_ref[0]
    for head in range(HEADS):
        cols = columns(head)
        k_pre = k_ref[0, :, cols]
        leave = ramp(rows, rows - 1.0, -1.0, slope_of(head)) * tail
        key = rounded_swish(k_pre) * leave
        rk = turned(key, cos, sin).astype(BF16)
        value = v_ref[0, :, cols].astype(BF16)
        state = s_ref[0, head]
        d_rk = dot(value, state, NT) * jnp.concatenate([leave, leave], axis=1)
        d_key = dk_ref[0, :, cols] + d_rk[:, :HEAD_DIM] * cos + d_rk[:, HEAD_DIM:] * sin
        dko_ref[0, :, cols] = (d_key.astype(BF16).astype(F32) * swish_slope(k_pre)).astype(BF16)
        dvo_ref[0, :, cols] = (dv_ref[0, :, cols] + dot(rk, state, NN)).astype(BF16)


class Chain:
    def __init__(self, fresh, factor, forward, parts):
        self.fresh, self.factor, self.forward, self.parts = fresh, factor, forward, parts
        self.seqs = fresh.shape[0]
        self.now = [fresh[s] for s in range(self.seqs)]
        self.got = [[] for _ in range(self.seqs)]
        self.turns = self.seqs + parts - 2

    def pass_on(self, s, hop):
        pair = (hop - 1, hop) if self.forward else (self.parts - hop, self.parts - hop - 1)
        self.got[s].append(lax.ppermute(self.now[s], "heads", [pair]))

    def begin(self):
        for s in range(self.seqs):
            self.pass_on(s, 1)

    def at(self, turn):
        return [(s, turn - s) for s in range(self.seqs) if 1 <= turn - s < self.parts]

    def arrivals(self, turn):
        self.new = [self.got[s][hop - 1] for s, hop in self.at(turn)]
        return self, "new"

    def go_on(self, turn):
        for (s, hop), new in zip(self.at(turn), self.new):
            self.got[s][hop - 1] = new
            if hop + 1 < self.parts:
                arrived = new.astype(F32) * self.factor[s][:, None, None]
                self.now[s] = (self.fresh[s].astype(F32) + arrived).astype(BF16)
                self.pass_on(s, hop + 1)

    def result(self):
        return jnp.stack([functools.reduce(lambda a, b: a + b, g) for g in self.got])


class Layer:
    def __init__(self, tokens, doc_lengths, cotangent, by_hand):
        seqs, length, width = tokens.shape
        self.seqs, self.length, self.width, self.count = seqs, length, width, seqs * length
        self.by_hand = by_hand
        self.here = lax.axis_index("rows")
        self.place = lax.axis_index("heads")
        self.order = jnp.stack([self.here ^ b for b in range(8)]).astype(jnp.int32)
        self.x = tokens.reshape(self.count, width)
        self.dy = cotangent.reshape(self.count, width)

        ends = jnp.cumsum(doc_lengths, axis=-1, dtype=jnp.int32)[:, :-1]

        def ids_at(where):
            return jnp.sum((where[None, :, None] >= ends[:, None, :]).astype(jnp.int32), axis=-1)

        start = self.place * length
        positions = start + jnp.arange(length, dtype=jnp.int32)
        ids = ids_at(positions)
        before = jnp.where(self.place > 0, ids_at(jnp.reshape(start - 1, (1,))), -1)
        final = ids[:, -1:]
        link = (ids == before).astype(F32)[:, :, None]
        tail = (ids == final).astype(F32)[:, :, None]
        slopes = jnp.array([slope_of(h) for h in range(HEADS)], F32)
        self.factor = (final == before).astype(F32) * jnp.exp(-slopes * length)[None, :]
        theta = jnp.exp(-math.log(10000.0) * jnp.arange(HEAD_DIM, dtype=F32) / HEAD_DIM)
        angle = positions.astype(F32)[:, None] * theta[None, :]

        table = pl.BlockSpec((length, HEAD_DIM), lambda s, *_: (0, 0))
        one_col = pl.BlockSpec((1, length, 1), lambda s, *_: (s, 0, 0))
        one_row = pl.BlockSpec((1, 1, length), lambda s, *_: (s, 0, 0))
        self.turn = [(jnp.cos(angle), table), (jnp.sin(angle), table)]
        self.link = link, one_col
        self.tail = tail, one_col
        self.masks = [(ids[:, :, None], one_col), (ids[:, None, :], one_row), self.link]
        self.seq = pl.BlockSpec((1, length, width), lambda s, *_: (s, 0, 0))
        self.state = pl.BlockSpec(
            (1, HEADS, 2 * HEAD_DIM, HEAD_DIM), lambda s, *_: (s, 0, 0, 0)
        )
        self.states = (seqs, HEADS, 2 * HEAD_DIM, HEAD_DIM), BF16, self.state
        step = min(self.count, 256)
        self.grid = (self.count // step,)
        self.wide = rows_spec(step, width)

    def rows(self, body, ins, types, order=None):
        return call(
            body, self.grid, self.order, [(a, self.wide) for a in ins],
            [((self.count, self.width), t, self.wide) for t in types],
        )

    def seqwise(self, body, ins, outs):
        shape = (self.seqs, self.length, self.width)
        ins = [i if isinstance(i, tuple) else (i.reshape(shape), self.seq) for i in ins]
        outs = [o if isinstance(o, tuple) else (shape, o, self.seq) for o in outs]
        got = call(body, (self.seqs,), self.order, ins, outs)
        return [g.reshape(self.count, self.width) if g.shape == shape else g for g in got]

    def copies(self):
        return [BF16] * (3 if self.by_hand else 1)

    def norm(self):
        blocks = 8 if self.by_hand else 1
        return self.rows(functools.partial(norm_body, blocks), [self.x], self.copies())

    def fresh(self, k_pre, v_pre):
        return self.seqwise(fresh_body, [k_pre, v_pre] + self.turn + [self.tail], [self.states])[0]

    def mix(self, q_pre, k_pre, v_pre, u_pre, state_in):
        ins = [q_pre, k_pre, v_pre, u_pre] + self.turn + self.masks + [(state_in, self.state)]
        return self.seqwise(mix_body, ins, [BF16] + self.copies())

    def mid(self, branch):
        blocks = 8 if self.by_hand else 1
        return self.rows(
            functools.partial(mid_body, blocks), [self.x, branch], [F32] + self.copies()
        )

    def mid_back(self, x_mid, grad):
        return self.rows(norm_back_body, [x_mid, self.dy, grad], [F32, BF16])

    def in_back(self, d_mid, grad):
        return self.rows(norm_back_body, [self.x, d_mid, grad], [F32])[0]

    def gate_back(self, q_pre, u_pre, mix, d_gated):
        ins = [q_pre, u_pre, mix, d_gated] + self.turn + [self.link]
        return self.seqwise(gate_back_body, ins, [BF16, BF16, self.states])

    def mix_back(self, q_pre, k_pre, v_pre, d_mix, state_in):
        ins = [q_pre, k_pre, v_pre, d_mix] + self.turn + self.masks + [(state_in, self.state)]
        return self.seqwise(mix_back_body, ins, [BF16, F32, F32])

    def state_back(self, k_pre, v_pre, dk_near, dv_near, d_state):
        ins = [k_pre, v_pre, dk_near, dv_near] + self.turn + [self.tail, (d_state, self.state)]
        return self.seqwise(state_back_body, ins, [BF16, BF16])


def plainly(layer, heads_count, weights):
    w_query, w_key, w_value, w_gate, w_out, w_left, w_right, w_down = (
        lax.all_gather(w, "rows", axis=0, tiled=True) for w in weights
    )

    def carried(fresh, forward):
        chain = Chain(fresh, layer.factor, forward, heads_count)
        chain.begin()
        for turn in range(1, chain.turns + 1):
            chain.arrivals(turn)
            chain.go_on(turn)
        return chain.result()

    def gradient(lhs, d):
        total = lax.psum_scatter(dot(lhs, d, TN, BF16), "rows", scatter_dimension=0, tiled=True)
        return lax.psum_scatter(total, "heads", scatter_dimension=1, tiled=True).astype(F32)

    (h_in,) = layer.norm()
    q_pre, k_pre, v_pre, u_pre = (
        dot(h_in, w, NN) for w in (w_query, w_key, w_value, w_gate)
    )
    state_in = carried(layer.fresh(k_pre, v_pre), True)
    mix, gated = layer.mix(q_pre, k_pre, v_pre, u_pre, state_in)
    x_mid, h_mid = layer.mid(dot(gated, w_out, NN))
    left, right = dot(h_mid, w_left, NN), dot(h_mid, w_right, NN)
    product = (left * right).astype(BF16)
    activations = (x_mid + dot(product, w_down, NN)).astype(BF16)
    grad_product = dot(layer.dy, w_down, NT)
    d_left = (grad_product * right).astype(BF16)
    d_right = (grad_product * left).astype(BF16)
    d_mid, d_branch = layer.mid_back(
        x_mid, dot(d_left, w_left, NT) + dot(d_right, w_right, NT)
    )
    d_u, d_mix, d_fresh = layer.gate_back(q_pre, u_pre, mix, dot(d_branch, w_out, NT))
    d_state = carried(d_fresh, False)
    d_q, dk_near, dv_near = layer.mix_back(q_pre, k_pre, v_pre, d_mix, state_in)
    d_k, d_v = layer.state_back(k_pre, v_pre, dk_near, dv_near, d_state)
    grad_in = (
        dot(d_q, w_query, NT) + dot(d_u, w_gate, NT) + dot(d_k, w_key, NT) + dot(d_v, w_value, NT)
    )
    input_grad = layer.in_back(d_mid, grad_in)
    pairs = (
        (h_in, d_q), (h_in, d_k), (h_in, d_v), (h_in, d_u), (gated, d_branch),
        (h_mid, d_left), (h_mid, d_right), (product, layer.dy),
    )
    return (activations, input_grad) + tuple(gradient(lhs, d) for lhs, d in pairs)


def reducing(terms):
    sends, keeps = [], []
    for lhs, d, _ in terms:
        half = lhs.shape[1] // 2
        sends.append(dot(lhs[:, half:], d, TN, BF16))

        def keep(theirs, lhs=lhs, d=d, half=half):
            return (dot(lhs[:, :half], d, TN) + theirs.astype(F32)).astype(BF16)

        keeps.append(keep)
    return Reduce(sends, keeps, [b for _, _, b in terms])


def reducing_rows(whole, here):
    rows, half = whole.shape[0] // 8, whole.shape[1] // 2

    def block(side, bits):
        cut = whole[:, side * half : (side + 1) * half]
        return jnp.concatenate(
            [lax.dynamic_slice_in_dim(cut, (here ^ b) * rows, rows, axis=0) for b in bits], axis=0
        )

    sends, keeps = [], []
    for side, bits in enumerate((BITS_X, BITS_Y)):
        sends.append(block(side, bits[4:]))

        def keep(theirs, side=side, bits=bits):
            return add(block(side, bits[:4]), theirs)

        keeps.append(keep)
    return Reduce(sends, keeps, [2, 4])


def stepwise(layer, heads_count, weights):
    w_query, w_key, w_value, w_gate, w_out, w_left, w_right, w_down = weights
    width, inner = layer.width, w_left.shape[1]
    half = width // 2
    order, here, place = layer.order, layer.here, layer.place
    v = types.SimpleNamespace()
    clock = Clock(order)
    tick = clock.tick

    pair = [(0, 0, width), (width, 0, width)]
    triple = [
        (0, 0, width), (width, 0, half), (width + half, 0, width), (2 * width + half, half, half),
    ]
    kv = Gather(pack(pair, [w_key, w_value], order), pair, (0, 1), (width, width))
    kv.first()
    v.h = layer.norm()
    v.qu = pack(triple, [w_query, w_out, w_gate, w_out], order)
    ff_pair = [(0, 0, inner), (inner, 0, inner)]
    v.ff = pack(ff_pair, [w_left, w_right], order)
    tick((kv, "near"), (v, "qu"), (v, "ff"), (v, "h"))
    kv.second()
    qu = Gather(v.qu, triple, (0, 2, 1, 2), (width, width, width))
    qu.first()
    ff = Gather(v.ff, ff_pair, (0, 1), (inner, inner))
    ff.first()
    kv.cross_first()
    tick((kv, "far"))
    kv.cross_second()
    full_k, full_v = kv.whole(order)
    h_in = v.h[0]
    k_pre, v_pre = dot(h_in, full_k, NN), dot(h_in, full_v, NN)
    v.fresh = layer.fresh(k_pre, v_pre)
    tick((v, "fresh"))
    forward = Chain(v.fresh, layer.factor, True, heads_count)
    forward.begin()

    tick(forward.arrivals(1), (qu, "near"))
    forward.go_on(1)
    qu.second()
    v.down = w_down
    down = Gather(v.down, [(0, 0, half), (half, half, half)], (0, 0), (width,))
    tick((down, "piece"))
    down.first()
    qu.cross_first()
    tick(forward.arrivals(2))
    forward.go_on(2)
    tick(forward.arrivals(3), (ff, "near"))
    forward.go_on(3)
    ff.second()
    ff.cross_first()
    tick(forward.arrivals(4), (qu, "far"))
    forward.go_on(4)
    qu.cross_second()
    full_q, full_u, full_out = qu.whole(order)
    v.q_pre, v.u_pre = dot(h_in, full_q, NN), dot(h_in, full_u, NN)
    tick(forward.arrivals(5), (down, "near"), (v, "q_pre"), (v, "u_pre"))
    forward.go_on(5)
    down.second()
    down.cross_first()
    tick(forward.arrivals(6))
    forward.go_on(6)
    state_in = forward.result()
    v.mix, *v.gated = layer.mix(v.q_pre, k_pre, v_pre, v.u_pre, state_in)
    tick((v, "mix"), (v, "gated"), (ff, "far"))
    ff.cross_second()
    branch = dot(v.gated[0], full_out, NN)
    v.x_mid, *v.h_mid = layer.mid(branch)
    full_left, full_right = ff.whole(order)
    tick((v, "x_mid"), (v, "h_mid"), (down, "far"))
    down.cross_second()

    h_mid = v.h_mid[0]
    v.left, v.right = dot(h_mid, full_left, NN), dot(h_mid, full_right, NN)
    v.product = (v.left * v.right).astype(BF16)
    tick((v, "left"), (v, "right"), (v, "product"))
    (full_down,) = down.whole(order)
    r_down = reducing_rows(dot(v.product, layer.dy, TN, BF16), here)
    tick((r_down, "sends"))
    r_down.core()
    grad_product = dot(layer.dy, full_down, NT)
    v.d_left = (grad_product * v.right).astype(BF16)
    v.d_right = (grad_product * v.left).astype(BF16)
    tick((v, "d_left"), (v, "d_right"), (r_down, "theirs"))
    r_down.join()
    tick((r_down, "totals"), (v, "d_left"), (v, "d_right"))
    r_down.first()
    v.d_mid, v.d_branch = layer.mid_back(
        v.x_mid, dot(v.d_left, full_left, NT) + dot(v.d_right, full_right, NT)
    )
    v.d_u, v.d_mix, v.d_fresh = layer.gate_back(
        v.q_pre, v.u_pre, v.mix, dot(v.d_branch, full_out, NT)
    )
    tick((v, "d_fresh"), (v, "d_u"), (v, "d_mix"), (v, "d_branch"), (v, "d_mid"), (v, "d_left"), (v, "d_right"))

    backward = Chain(v.d_fresh, layer.factor, False, heads_count)
    backward.begin()
    r_ff = reducing([(v.h_mid[1], v.d_left, 2), (v.h_mid[2], v.d_right, 4)])
    tick((r_ff, "sends"), (r_down, "got"))
    r_ff.core()
    r_down.join_first()
    tick(backward.arrivals(1), (r_down, "parts"), (v, "d_mix"))
    backward.go_on(1)
    r_down.second()
    v.d_q, v.dk_near, v.dv_near = layer.mix_back(v.q_pre, k_pre, v_pre, v.d_mix, state_in)
    tick(backward.arrivals(2), (r_ff, "theirs"), (v, "d_q"), (v, "dk_near"), (v, "dv_near"), (v, "d_u"))
    backward.go_on(2)
    r_ff.join()
    tick((r_ff, "totals"))
    r_ff.first()
    tick(backward.arrivals(3), (v, "d_branch"), (v, "d_u"))
    backward.go_on(3)
    r_out = reducing([(v.gated[1], v.d_branch, 2), (v.h[2], v.d_u, 4)])
    tick((r_out, "sends"), (r_down, "got_last"))
    r_out.core()
    r_down.join_second()
    s_down = Settle([jnp.concatenate(r_down.sums, axis=1)], place)
    tick(backward.arrivals(4), (r_out, "theirs"), (v, "d_q"))
    backward.go_on(4)
    r_out.join()
    r_query = reducing([(v.h[2], v.d_q, 4)])
    tick((r_out, "totals"), (r_query, "sends"))
    r_out.first()
    r_query.core()
    tick(backward.arrivals(5), (r_query, "theirs"), (v, "product"))
    backward.go_on(5)
    r_query.join()
    tick((r_query, "totals"))
    r_query.first()
    v.activations = (v.x_mid + dot(v.product, full_down, NN)).astype(BF16)
    tick(backward.arrivals(6), (v, "activations"), (r_ff, "got"))
    backward.go_on(6)
    d_state = backward.result()
    r_ff.join_first()
    v.d_k, v.d_v = layer.state_back(k_pre, v_pre, v.dk_near, v.dv_near, d_state)
    tick((r_ff, "parts"), (v, "d_k"), (v, "d_v"))
    r_ff.second()
    r_key = reducing([(v.h[1], v.d_k, 2), (v.h[2], v.d_v, 4)])
    tick((r_key, "sends"), (r_out, "got"))
    r_key.core()
    r_out.join_first()
    tick((r_key, "theirs"), (r_out, "parts"))
    r_out.second()
    r_key.join()
    tick((r_key, "totals"), (r_query, "got"), (v, "d_q"))
    r_key.first()
    r_query.join_first()
    tick((r_query, "parts"), (v, "d_q"), (s_down, "out"))
    r_query.second()
    s_down.pass_on(1)
    v.grad_in = (
        dot(v.d_q, full_q, NT) + dot(v.d_u, full_u, NT)
        + dot(v.d_k, full_k, NT) + dot(v.d_v, full_v, NT)
    )
    tick((v, "grad_in"), (r_ff, "got_last"), (s_down, "got"))
    r_ff.join_second()
    s_ff = Settle(r_ff.sums, place)
    s_down.join()
    tick((s_ff, "out"), (s_ff, "own"), (s_down, "out"))
    s_ff.pass_on(1)
    s_down.pass_on(2)
    v.input_grad = layer.in_back(v.d_mid, v.grad_in)
    tick((v, "input_grad"), (r_out, "got_last"), (r_query, "got_last"))
    r_out.join_second()
    r_query.join_second()
    s_out = Settle(r_out.sums + r_query.sums, place)
    tick((s_out, "out"), (r_key, "got"))
    s_out.pass_on(1)
    r_key.join_first()
    tick((r_key, "parts"), (s_ff, "got"))
    r_key.second()
    s_ff.join()
    tick((s_ff, "out"), (s_out, "got"))
    s_ff.pass_on(2)
    s_out.join()
    tick((s_out, "out"), (r_key, "got_last"))
    s_out.pass_on(2)
    r_key.join_second()
    s_key = Settle(r_key.sums, place)
    tick((s_key, "out"))
    s_key.pass_on(1)
    tick((s_key, "got"), (s_down, "got"), (s_ff, "got"))
    s_key.join()
    tick((s_key, "out"), (s_out, "got"))
    s_key.pass_on(2)
    (g_down,) = s_down.result()
    g_left, g_right = s_ff.result()
    g_out, g_gate, g_query = s_out.result()
    g_key, g_value = s_key.result()
    return (
        v.activations, v.input_grad, g_query, g_key, g_value, g_gate, g_out, g_left, g_right, g_down
    )


def on_device(rows_count, heads_count, tokens, doc_lengths, cotangent, *weights):
    by_hand = rows_count == 8 and heads_count == 4
    layer = Layer(tokens, doc_lengths, cotangent, by_hand)
    run = stepwise if by_hand else plainly
    activations, input_grad, *grads = run(layer, heads_count, weights)
    return (activations.reshape(tokens.shape), input_grad.reshape(tokens.shape), *grads)


def solution(mesh):
    sizes = dict(mesh.shape)
    tokens = P("rows", "heads", None)
    weights = P("rows", None)
    grads = P("rows", "heads")
    return jax.shard_map(
        functools.partial(on_device, sizes["rows"], sizes["heads"]),
        mesh=mesh,
        in_specs=(tokens, weights, tokens) + (weights,) * 8,
        out_specs=(tokens, tokens) + (grads,) * 8,
        check_vma=False,
    )
```

```python
import functools
import math
import types

import jax
import jax.numpy as jnp
from jax import lax
from jax.experimental import pallas as pl
from jax.experimental.pallas import tpu as pltpu
from jax.sharding import PartitionSpec as P

HEADS = 8
HEAD_DIM = 128
EPS = 1e-06
F32 = jnp.float32
BF16 = jnp.bfloat16
VMEM_LIMIT = 60 << 20

BITS = (0, 2, 4, 6, 1, 3, 5, 7)
BITS_X = (0, 4, 2, 6, 1, 5, 3, 7)
BITS_Y = (0, 2, 4, 6, 1, 3, 5, 7)


def after(value, *others):
    return lax.optimization_barrier((value,) + others)[0]


def dot(a, b, dims, out=F32):
    return lax.dot_general(a, b, (dims, ((), ())), preferred_element_type=F32).astype(out)


NN = ((1,), (0,))
NT = ((1,), (1,))
TN = ((0,), (0,))


def swap(value, bit, size):
    return lax.ppermute(value, "rows", [(i, i ^ bit) for i in range(size)])


def swap_heads(value, bit):
    return lax.ppermute(value, "heads", [(i, i ^ bit) for i in range(4)])


HBM = pl.BlockSpec(memory_space=pltpu.HBM)


def whole_spec(rows, width):
    return pl.BlockSpec((rows, width), lambda i, *_: (0, 0))


def run_copies(copies):
    for copy in copies:
        copy.start()
    for copy in copies:
        copy.wait()


def pack(order, arrays, lists):
    rows = arrays[0].shape[0]
    widths = [sum(w for _, _, w in parts) for parts in lists]
    most = max(len(parts) for parts in lists)

    def body(order, *refs):
        ins, outs, sems = refs[: len(arrays)], refs[len(arrays) : -1], refs[-1]
        copies = []
        for j, parts in enumerate(lists):
            at = 0
            for i, (which, begin, width) in enumerate(parts):
                copies.append(
                    pltpu.make_async_copy(
                        ins[which].at[:, begin : begin + width],
                        outs[j].at[:, at : at + width],
                        sems.at[j, i],
                    )
                )
                at += width
        run_copies(copies)

    return call(
        body, (1,), order, [(a, HBM) for a in arrays],
        [((rows, w), BF16, whole_spec(rows, w)) for w in widths],
        scratch=[pltpu.SemaphoreType.DMA((len(lists), most))],
    )


class Clock:
    def __init__(self, start):
        self.token = start

    def tick(self, *places):
        held = [getattr(o, n) for o, n in places]
        held, self.token = lax.optimization_barrier((held, self.token))
        for (o, n), value in zip(places, held):
            setattr(o, n, value)


def places(here, head):
    return jnp.stack([here ^ b for b in range(8)] + [head ^ b for b in range(4)]).astype(jnp.int32)


class Gather:
    def __init__(self, pieces):
        self.pieces = list(pieces)

    def first(self):
        self.near_x = [swap(p, 2, 8) for p in self.pieces]
        self.near_y = [swap(p, 4, 8) for p in self.pieces]

    def second(self):
        self.far = [swap(self.near_x[0], 4, 8), swap(self.near_y[1], 2, 8)]

    def cross(self, *names):
        for name in names:
            setattr(self, name + "_other", [swap(p, 1, 8) for p in getattr(self, name)])

    def all(self, half):
        names = ("pieces", "near_x", "near_y", "far")
        return [getattr(self, n + core)[half] for core in ("", "_other") for n in names]


def add(one, two, out=BF16):
    return (one.astype(F32) + two.astype(F32)).astype(out)


def added(order, outs):
    steps = 2
    ins, results, counts = [], [], []
    for terms, rows, dtype in outs:
        size = rows // steps
        width = terms[0][0].shape[1]
        for array, first in terms:
            ins.append((array, pl.BlockSpec((size, width), lambda i, *_, f=first // size: (f + i, 0))))
        results.append(((rows, width), dtype, pl.BlockSpec((size, width), lambda i, *_: (i, 0))))
        counts.append(len(terms))

    def body(order, *refs):
        at = 0
        for out, count in zip(refs[len(ins) :], counts):
            total = refs[at][...].astype(F32)
            for ref in refs[at + 1 : at + count]:
                total += ref[...].astype(F32)
            out[...] = total.astype(out.dtype)
            at += count

    return call(body, (steps,), order, ins, results)


class Reduce:
    def __init__(self, order, sends, keeps, bits):
        self.order, self.sends, self.keeps, self.bits = order, list(sends), list(keeps), list(bits)

    def core(self):
        self.theirs = [swap(s, 1, 8) for s in self.sends]

    def join(self):
        half = self.keeps[0].shape[0] // 2
        pairs = zip(self.keeps, self.theirs)
        self.totals = added(self.order, [([(k, half), (t, half)], half, BF16) for k, t in pairs])

    def first(self):
        self.got = [swap(t, b, 8) for t, b in zip(self.totals, self.bits)]

    def join_first(self):
        rows = self.keeps[0].shape[0] // 4
        outs = []
        for at in (0, rows):
            for k, t, g in zip(self.keeps, self.theirs, self.got):
                outs.append(([(k, at), (t, at), (g, at)], rows, BF16))
        parts = added(self.order, outs)
        count = len(self.keeps)
        self.own, self.parts = parts[:count], parts[count:]

    def second(self):
        self.got_last = [swap(p, 6 - b, 8) for p, b in zip(self.parts, self.bits)]

    def join_second(self):
        self.sums = [add(p, g, F32) for p, g in zip(self.own, self.got_last)]


def column_block(s, here, bit):
    width = s.shape[1] // 4
    return lax.dynamic_slice_in_dim(s, (here ^ bit) * width, width, axis=1)


class Settle:
    def __init__(self, sums, here):
        self.widths = [s.shape[1] // 4 for s in sums]
        self.own = [column_block(s, here, 0) for s in sums]
        self.far = [column_block(s, here, 2) for s in sums]
        near = [column_block(s, here, 1) for s in sums] + [column_block(s, here, 3) for s in sums]
        self.out = jnp.concatenate([n.astype(BF16) for n in near], axis=1)

    def pass_on(self, bit):
        self.got = lax.ppermute(self.out, "heads", [(i, i ^ bit) for i in range(4)])

    def split(self, at=0):
        pieces = []
        for w in self.widths:
            pieces.append(self.got[:, at : at + w].astype(F32))
            at += w
        return pieces

    def join(self):
        self.own = [o + g for o, g in zip(self.own, self.split())]
        far = [o + g for o, g in zip(self.far, self.split(sum(self.widths)))]
        self.out = jnp.concatenate([f.astype(BF16) for f in far], axis=1)

    def result(self):
        return [o + g for o, g in zip(self.own, self.split())]


class SettleWide:
    def __init__(self, order, parts, got):
        self.order, self.count = order, len(parts)
        rows, width = parts[0].shape
        self.rows, self.block = rows, width // 4
        count, block = self.count, self.block

        def body(order, *refs):
            own, out, held = refs[2 * count], refs[2 * count + 1], refs[2 * count + 2]
            for i in range(count):
                held[...] = refs[2 * i][...].astype(F32) + refs[2 * i + 1][...].astype(F32)
                for j, bit in enumerate((0, 2)):
                    at = (2 * i + j) * block
                    own[:, at : at + block] = held[:, at_block(order, 8 + bit, block)]
                    out[:, at : at + block] = held[:, at_block(order, 9 + bit, block)].astype(BF16)

        spec = whole_spec(rows, width)
        wide = whole_spec(rows, 2 * count * block)
        shape = rows, 2 * count * block
        ins = [(a, spec) for pair in zip(parts, got) for a in pair]
        self.own, self.out = call(
            body, (1,), order, ins, [(shape, F32, wide), (shape, BF16, wide)],
            scratch=[pltpu.VMEM((rows, width), F32)],
        )

    def pass_on(self, bit):
        self.got = lax.ppermute(self.out, "heads", [(i, i ^ bit) for i in range(4)])

    def join(self):
        rows, count, block = self.rows, self.count, self.block

        def body(order, own_ref, got_ref, mine, out):
            for i in range(count):
                at = 2 * i * block
                both = own_ref[:, at : at + 2 * block] + got_ref[:, at : at + 2 * block].astype(F32)
                mine[:, i * block : (i + 1) * block] = both[:, :block]
                out[:, i * block : (i + 1) * block] = both[:, block:].astype(BF16)

        wide, narrow = whole_spec(rows, 2 * count * block), whole_spec(rows, count * block)
        shape = rows, count * block
        self.own, self.out = call(
            body, (1,), self.order, [(self.own, wide), (self.got, wide)],
            [(shape, F32, narrow), (shape, BF16, narrow)],
        )

    def result(self):
        rows, count, block = self.rows, self.count, self.block

        def body(order, own_ref, got_ref, *outs):
            for i, out in enumerate(outs):
                cols = slice(i * block, (i + 1) * block)
                out[...] = own_ref[:, cols] + got_ref[:, cols].astype(F32)

        narrow = whole_spec(rows, count * block)
        return call(
            body, (1,), self.order, [(self.own, narrow), (self.got, narrow)],
            [((rows, block), F32, whole_spec(rows, block))] * count,
        )


def at_block(order_ref, index, width):
    return pl.ds(pl.multiple_of(order_ref[index] * width, width), width)


def sigmoid(v):
    return 1.0 / (1.0 + jnp.exp(-v))


def swish_slope(v):
    sig = sigmoid(v)
    return sig * (1.0 + v * (1.0 - sig))


def call(body, grid, order, ins, outs, scratch=(), flops=0):
    moved = sum(a.size * a.dtype.itemsize for a, _ in ins) + sum(
        math.prod(s) * jnp.dtype(t).itemsize for s, t, _ in outs
    )
    return pl.pallas_call(
        body,
        grid_spec=pltpu.PrefetchScalarGridSpec(
            num_scalar_prefetch=1,
            grid=grid,
            in_specs=[spec for _, spec in ins],
            out_specs=[spec for _, _, spec in outs],
            scratch_shapes=list(scratch),
        ),
        out_shape=[jax.ShapeDtypeStruct(s, t) for s, t, _ in outs],
        compiler_params=pltpu.CompilerParams(vmem_limit_bytes=VMEM_LIMIT),
        cost_estimate=pl.CostEstimate(flops=flops // 32, bytes_accessed=moved // 32, transcendentals=0),
    )(order, *[a for a, _ in ins])


def rows_spec(count, width, column=0):
    return pl.BlockSpec((count, width), lambda i, *_: (i, column))


def norm_body(order, x_ref, h_ref):
    x = x_ref[...].astype(F32)
    scale = lax.rsqrt(jnp.mean(x * x, axis=-1, keepdims=True) + EPS)
    h_ref[...] = (x * scale).astype(BF16)


def mid_body(order, x_ref, b_ref, mid_ref, h_ref):
    mid = x_ref[...].astype(F32) + b_ref[...]
    mid_ref[...] = mid
    scale = lax.rsqrt(jnp.mean(mid * mid, axis=-1, keepdims=True) + EPS)
    h_ref[...] = (mid * scale).astype(BF16)


def norm_back_body(order, v_ref, base_ref, g_ref, *outs):
    v = v_ref[...].astype(F32)
    g = g_ref[...]
    scale = lax.rsqrt(jnp.mean(v * v, axis=-1, keepdims=True) + EPS)
    inner = jnp.mean(g * v, axis=-1, keepdims=True) * (scale * scale * scale)
    total = base_ref[...].astype(F32) + scale * g - v * inner
    outs[0][...] = total
    if len(outs) > 1:
        outs[1][...] = total.astype(BF16)


def ramp(rows, start, sign, slope):
    place = lax.broadcasted_iota(jnp.int32, (rows, HEAD_DIM), 0).astype(F32)
    return jnp.exp(-slope * (start + sign * place))


def decays(ids_col, ids_row, slope):
    rows = ids_col.shape[0]
    gap = (
        lax.broadcasted_iota(jnp.int32, (rows, rows), 0)
        - lax.broadcasted_iota(jnp.int32, (rows, rows), 1)
    ).astype(F32)
    keep = (gap >= 0.0) & (ids_col == ids_row)
    return jnp.where(keep, jnp.exp(-slope * jnp.maximum(gap, 0.0)), 0.0)


def slope_of(head):
    return 2.0 ** (-8.0 * (head + 1) / HEADS)


def columns(head):
    return slice(head * HEAD_DIM, (head + 1) * HEAD_DIM)


def turned(a, cos, sin):
    return jnp.concatenate([a * cos, a * sin], axis=1)


def rounded_swish(v):
    return (v * sigmoid(v)).astype(BF16).astype(F32)


def fresh_body(order, k_ref, v_ref, cos_ref, sin_ref, tail_ref, state_ref):
    rows = k_ref.shape[1]
    cos, sin = cos_ref[...], sin_ref[...]
    tail = tail_ref[0]
    for head in range(HEADS):
        key = rounded_swish(k_ref[0, :, columns(head)])
        key = key * (ramp(rows, rows - 1.0, -1.0, slope_of(head)) * tail)
        value = v_ref[0, :, columns(head)].astype(BF16)
        state_ref[0, head] = dot(turned(key, cos, sin).astype(BF16), value, TN, BF16)


def mix_body(
    order, q_ref, k_ref, v_ref, u_ref, cos_ref, sin_ref, col_ref, row_ref, link_ref, s_ref,
    mix_ref, gated_ref,
):
    rows = q_ref.shape[1]
    cos, sin = cos_ref[...], sin_ref[...]
    ids_col, ids_row = col_ref[0], row_ref[0]
    link = link_ref[0]
    power = jnp.zeros((rows, 1), F32)
    for head in range(HEADS):
        cols = columns(head)
        slope = slope_of(head)
        rq = turned(rounded_swish(q_ref[0, :, cols]), cos, sin).astype(BF16)
        rk = turned(rounded_swish(k_ref[0, :, cols]), cos, sin).astype(BF16)
        value = v_ref[0, :, cols].astype(BF16)
        weights = (dot(rq, rk, NT) * decays(ids_col, ids_row, slope)).astype(BF16)
        mixed = dot(weights, value, NN) + dot(rq, s_ref[0, head], NN) * (
            ramp(rows, 1.0, 1.0, slope) * link
        )
        mixed = mixed.astype(BF16)
        mix_ref[0, :, cols] = mixed
        mixed = mixed.astype(F32)
        power += jnp.sum(mixed * mixed, axis=-1, keepdims=True)
    scale = lax.rsqrt(power / (HEADS * HEAD_DIM) + EPS)
    for head in range(HEADS):
        cols = columns(head)
        u = u_ref[0, :, cols]
        gated_ref[0, :, cols] = (
            mix_ref[0, :, cols].astype(F32) * scale * (u * sigmoid(u))
        ).astype(BF16)


def gate_back_body(
    order, q_ref, u_ref, mix_ref, dg_ref, cos_ref, sin_ref, link_ref, du_ref, dm_ref, state_ref
):
    rows = q_ref.shape[1]
    cos, sin = cos_ref[...], sin_ref[...]
    link = link_ref[0]
    mix = mix_ref[0].astype(F32)
    scale = lax.rsqrt(jnp.mean(mix * mix, axis=-1, keepdims=True) + EPS)
    inner = jnp.zeros((rows, 1), F32)
    for head in range(HEADS):
        cols = columns(head)
        u = u_ref[0, :, cols]
        part = mix_ref[0, :, cols].astype(F32)
        dg = dg_ref[0, :, cols]
        sig = sigmoid(u)
        inner += jnp.sum(dg * (u * sig) * part, axis=-1, keepdims=True)
        du_ref[0, :, cols] = (dg * part * scale * (sig * (1.0 + u * (1.0 - sig)))).astype(BF16)
    inner = inner * (scale * scale * scale) / (HEADS * HEAD_DIM)
    for head in range(HEADS):
        cols = columns(head)
        u = u_ref[0, :, cols]
        part = mix_ref[0, :, cols].astype(F32)
        dg = dg_ref[0, :, cols]
        d_mix = (scale * (dg * (u * sigmoid(u))) - part * inner).astype(BF16)
        dm_ref[0, :, cols] = d_mix
        query = rounded_swish(q_ref[0, :, cols]) * (
            ramp(rows, 1.0, 1.0, slope_of(head)) * link
        )
        state_ref[0, head] = dot(turned(query, cos, sin).astype(BF16), d_mix, TN, BF16)


def mix_back_body(
    order, q_ref, k_ref, v_ref, dm_ref, cos_ref, sin_ref, col_ref, row_ref, link_ref, s_ref,
    dq_ref, dk_ref, dv_ref,
):
    rows = q_ref.shape[1]
    cos, sin = cos_ref[...], sin_ref[...]
    ids_col, ids_row = col_ref[0], row_ref[0]
    link = link_ref[0]
    for head in range(HEADS):
        cols = columns(head)
        slope = slope_of(head)
        q_pre = q_ref[0, :, cols]
        rq = turned(rounded_swish(q_pre), cos, sin).astype(BF16)
        rk = turned(rounded_swish(k_ref[0, :, cols]), cos, sin).astype(BF16)
        value = v_ref[0, :, cols].astype(BF16)
        d_mix = dm_ref[0, :, cols]
        decay = decays(ids_col, ids_row, slope)
        weights = (dot(rq, rk, NT) * decay).astype(BF16)
        d_scores = (dot(d_mix, value, NT) * decay).astype(BF16)
        enter = ramp(rows, 1.0, 1.0, slope) * link
        d_rq = dot(d_scores, rk, NN) + dot(d_mix, s_ref[0, head], NT) * jnp.concatenate(
            [enter, enter], axis=1
        )
        d_query = d_rq[:, :HEAD_DIM] * cos + d_rq[:, HEAD_DIM:] * sin
        dq_ref[0, :, cols] = (
            d_query.astype(BF16).astype(F32) * swish_slope(q_pre)
        ).astype(BF16)
        d_rk = dot(d_scores, rq, TN)
        dk_ref[0, :, cols] = d_rk[:, :HEAD_DIM] * cos + d_rk[:, HEAD_DIM:] * sin
        dv_ref[0, :, cols] = dot(weights, d_mix, TN)


def state_back_body(
    order, k_ref, v_ref, dk_ref, dv_ref, cos_ref, sin_ref, tail_ref, s_ref, dko_ref, dvo_ref
):
    rows = k_ref.shape[1]
    cos, sin = cos_ref[...], sin_ref[...]
    tail = tail_ref[0]
    for head in range(HEADS):
        cols = columns(head)
        k_pre = k_ref[0, :, cols]
        leave = ramp(rows, rows - 1.0, -1.0, slope_of(head)) * tail
        key = rounded_swish(k_pre) * leave
        rk = turned(key, cos, sin).astype(BF16)
        value = v_ref[0, :, cols].astype(BF16)
        state = s_ref[0, head]
        d_rk = dot(value, state, NT) * jnp.concatenate([leave, leave], axis=1)
        d_key = dk_ref[0, :, cols] + d_rk[:, :HEAD_DIM] * cos + d_rk[:, HEAD_DIM:] * sin
        dko_ref[0, :, cols] = (d_key.astype(BF16).astype(F32) * swish_slope(k_pre)).astype(BF16)
        dvo_ref[0, :, cols] = (dv_ref[0, :, cols] + dot(rk, state, NN)).astype(BF16)


ORDERS = (BITS_Y, BITS_X)


def spread(order, h_ref, outs):
    width = h_ref.shape[1] // 8
    for out, bits in zip(outs, ORDERS):
        for k in range(8):
            out[:, k * width : (k + 1) * width] = h_ref[:, at_block(order, bits[k], width)]


def row_norm_body(order, x_ref, *refs):
    x = x_ref[...].astype(F32)
    scale = lax.rsqrt(jnp.mean(x * x, axis=-1, keepdims=True) + EPS)
    refs[-1][...] = (x * scale).astype(BF16)
    spread(order, refs[-1], refs[:-1])


def head_slope(head):
    return jnp.exp2(-8.0 * (head.astype(F32) + 1.0) / HEADS)


def block_decay(ids_col, ids_row, i, j, size, slope):
    gap = (
        (i - j) * size
        + lax.broadcasted_iota(jnp.int32, (size, size), 0)
        - lax.broadcasted_iota(jnp.int32, (size, size), 1)
    ).astype(F32)
    same = ids_col[i * size : (i + 1) * size] == ids_row[:, j * size : (j + 1) * size]
    keep = same if i > j else same & (gap >= 0.0)
    return jnp.where(keep, jnp.exp(-slope * jnp.maximum(gap, 0.0)), 0.0)


def row_mix_body(size, order, q_ref, k_ref, v_ref, cos_ref, sin_ref, col_ref, row_ref, mix_ref):
    cos, sin = cos_ref[...], sin_ref[...]
    col, row = col_ref[...], row_ref[...]
    each = q_ref.shape[1] // HEAD_DIM
    for part in range(each):
        cols = columns(part)
        slope = head_slope(pl.program_id(0) * each + part)
        rq = turned(rounded_swish(q_ref[:, cols]), cos, sin).astype(BF16)
        rk = turned(rounded_swish(k_ref[:, cols]), cos, sin).astype(BF16)
        value = v_ref[:, cols].astype(BF16)
        for i in range(rq.shape[0] // size):
            here = slice(i * size, (i + 1) * size)
            mixed = jnp.zeros((size, HEAD_DIM), F32)
            for j in range(i + 1):
                there = slice(j * size, (j + 1) * size)
                scores = dot(rq[here], rk[there], NT) * block_decay(col, row, i, j, size, slope)
                mixed += dot(scores.astype(BF16), value[there], NN)
            mix_ref[here, cols] = mixed.astype(BF16)


def row_mix_back_body(
    size, order, q_ref, k_ref, v_ref, dm_ref, cos_ref, sin_ref, col_ref, row_ref,
    dq_ref, dk_ref, dv_ref,
):
    cos, sin = cos_ref[...], sin_ref[...]
    col, row = col_ref[...], row_ref[...]
    each = q_ref.shape[1] // HEAD_DIM
    count = q_ref.shape[0] // size
    cut = [slice(i * size, (i + 1) * size) for i in range(count)]

    def back(d_turned, pre, at):
        d = d_turned[:, :HEAD_DIM] * cos[at] + d_turned[:, HEAD_DIM:] * sin[at]
        return (d.astype(BF16).astype(F32) * swish_slope(pre[at])).astype(BF16)

    for part in range(each):
        cols = columns(part)
        slope = head_slope(pl.program_id(0) * each + part)
        q_pre, k_pre = q_ref[:, cols], k_ref[:, cols]
        rq = turned(rounded_swish(q_pre), cos, sin).astype(BF16)
        rk = turned(rounded_swish(k_pre), cos, sin).astype(BF16)
        value = v_ref[:, cols].astype(BF16)
        d_mix = dm_ref[:, cols]
        d_rq = [0.0] * count
        d_rk = [0.0] * count
        d_value = [0.0] * count
        for i in range(count):
            for j in range(i + 1):
                decay = block_decay(col, row, i, j, size, slope)
                scores = (dot(rq[cut[i]], rk[cut[j]], NT) * decay).astype(BF16)
                d_scores = (dot(d_mix[cut[i]], value[cut[j]], NT) * decay).astype(BF16)
                d_value[j] += dot(scores, d_mix[cut[i]], TN)
                d_rq[i] += dot(d_scores, rk[cut[j]], NN)
                d_rk[j] += dot(d_scores, rq[cut[i]], TN)
        for i in range(count):
            dq_ref[cut[i], cols] = back(d_rq[i], q_pre, cut[i])
            dk_ref[cut[i], cols] = back(d_rk[i], k_pre, cut[i])
            dv_ref[cut[i], cols] = d_value[i].astype(BF16)


def stacked(refs):
    return jnp.concatenate([r[...] for r in refs], axis=0)


def restored(order, value, out):
    width = value.shape[1] // 8
    for k, at in enumerate(BITS_Y):
        out[:, at_block(order, at, width)] = value[:, k * width : (k + 1) * width]


def project_body(order, h_ref, *refs):
    h = h_ref[...]
    refs[16][...] = dot(h, stacked(refs[:8]), NN)
    refs[17][...] = dot(h, stacked(refs[8:16]), NN)


def out_mid_body(order, mix_ref, u_ref, x_ref, *refs):
    gated_ref, mid_ref, plain = refs[16], refs[17], refs[-1]
    mix = mix_ref[...].astype(F32)
    u = u_ref[...]
    scale = lax.rsqrt(jnp.mean(mix * mix, axis=-1, keepdims=True) + EPS)
    plain[...] = (mix * scale * (u * sigmoid(u))).astype(BF16)
    spread(order, plain, (refs[-2], gated_ref))
    gated = refs[-2][...]
    half = x_ref.shape[1] // 2
    low = x_ref[:, :half].astype(F32) + dot(gated, stacked(refs[:8]), NN)
    high = x_ref[:, half:].astype(F32) + dot(gated, stacked(refs[8:16]), NN)
    mid_ref[:, :half] = low
    mid_ref[:, half:] = high
    power = jnp.sum(low * low, axis=-1, keepdims=True) + jnp.sum(high * high, axis=-1, keepdims=True)
    scale = lax.rsqrt(power / x_ref.shape[1] + EPS)
    plain[:, :half] = (low * scale).astype(BF16)
    plain[:, half:] = (high * scale).astype(BF16)
    spread(order, plain, refs[18:20])


def left_right_body(order, h_ref, *refs):
    left_ref, right_ref, product_ref = refs[16:19]
    h = h_ref[...]
    left = dot(h, stacked(refs[:8]), NN)
    right = dot(h, stacked(refs[8:16]), NN)
    left_ref[...] = left.astype(BF16)
    right_ref[...] = right.astype(BF16)
    product_ref[...] = (left * right).astype(BF16)


def down_grad_body(rows, order, product_ref, c_ref, *refs):
    outs, held, sems = refs[:4], refs[4], refs[5]
    step = pl.program_id(0)
    size = product_ref.shape[1]
    held[pl.ds(pl.multiple_of(step * size, size), size), :] = dot(
        product_ref[...], c_ref[...], TN, BF16
    )

    @pl.when(step == pl.num_programs(0) - 1)
    def _():
        half = held.shape[1] // 2
        copies = []
        for side, bits in enumerate((BITS_X, BITS_Y)):
            for k, bit in enumerate(bits):
                copies.append(
                    pltpu.make_async_copy(
                        held.at[at_block(order, bit, rows), side * half : (side + 1) * half],
                        outs[2 * (k // 4) + side].at[(k % 4) * rows : (k % 4 + 1) * rows, :],
                        sems.at[side, k],
                    )
                )
        run_copies(copies)


def feed_back_body(
    rows, order, left_ref, right_ref, product_ref, hx_ref, hy_ref, c_ref, mid_ref, *refs
):
    weights, downs = refs[:16], refs[16:32]
    keep_l, send_l, keep_r, send_r, d_mid_ref, d_branch_ref, act_ref = refs[32:39]
    down, grad, total, held_l, held_r, sems = refs[39:]
    step = pl.program_id(0)

    @pl.when(step == 0)
    def _():
        half = down.shape[1] // 2
        run_copies(
            [
                pltpu.make_async_copy(
                    downs[8 * side + k],
                    down.at[at_block(order, at, rows), side * half : (side + 1) * half],
                    sems.at[side, k],
                )
                for side in range(2)
                for k, at in enumerate(BITS_Y)
            ]
        )
        held_l[...] = jnp.zeros_like(held_l)
        held_r[...] = jnp.zeros_like(held_r)

    size = left_ref.shape[1]
    last = pl.num_programs(0) - 2

    def down_rows(block):
        return down[pl.ds(pl.multiple_of(block * size, size), size), :]

    d_left, d_right = held_l[...], held_r[...]
    half = hx_ref.shape[1] // 2
    g_left = dot(hx_ref[...], d_left, TN, BF16)
    keep_l[...] = g_left[:half]
    send_l[...] = g_left[half:]
    g_right = dot(hy_ref[...], d_right, TN, BF16)
    keep_r[...] = g_right[:half]
    send_r[...] = g_right[half:]
    total[...] += dot(product_ref[...], down_rows(jnp.maximum(step - 1, 0)), NN)
    grad[...] += dot(d_left, stacked(weights[:8]), NT) + dot(d_right, stacked(weights[8:]), NT)

    grad_product = dot(c_ref[...], down_rows(jnp.minimum(step, last)), NT)
    held_l[...] = (grad_product * right_ref[...].astype(F32)).astype(BF16)
    held_r[...] = (grad_product * left_ref[...].astype(F32)).astype(BF16)

    @pl.when(step == 0)
    def _():
        grad[...] = jnp.zeros_like(grad)
        total[...] = jnp.zeros_like(total)

    @pl.when(step == pl.num_programs(0) - 1)
    def _():
        mid = mid_ref[...]
        act_ref[...] = (mid + total[...]).astype(BF16)
        restored(order, grad[...], total)
        g = total[...]
        scale = lax.rsqrt(jnp.mean(mid * mid, axis=-1, keepdims=True) + EPS)
        inner = jnp.mean(g * mid, axis=-1, keepdims=True) * (scale * scale * scale)
        d_mid = c_ref[...].astype(F32) + scale * g - mid * inner
        d_mid_ref[...] = d_mid
        d_branch_ref[...] = d_mid.astype(BF16)


def gate_out_back_body(order, d_ref, mix_ref, u_ref, *refs):
    du_ref, dm_ref, held = refs[16:]
    half = d_ref.shape[1] // 2
    d = d_ref[...]
    restored(
        order, dot(d[:, :half], stacked(refs[:8]), NT) + dot(d[:, half:], stacked(refs[8:16]), NT), held
    )
    dg = held[...]
    mix = mix_ref[...].astype(F32)
    u = u_ref[...]
    sig = sigmoid(u)
    scale = lax.rsqrt(jnp.mean(mix * mix, axis=-1, keepdims=True) + EPS)
    du_ref[...] = (dg * mix * scale * (sig * (1.0 + u * (1.0 - sig)))).astype(BF16)
    dn = dg * (u * sig)
    inner = jnp.mean(dn * mix, axis=-1, keepdims=True) * (scale * scale * scale)
    dm_ref[...] = (scale * dn - mix * inner).astype(BF16)


def in_back_body(order, x_ref, d_mid_ref, *refs):
    ds, weights, out, grad, held = refs[:4], refs[4:36], refs[36], refs[37], refs[38]
    step = pl.program_id(0)
    value = dot(ds[0][...], stacked(weights[:8]), NT)
    for i in (1, 2, 3):
        value += dot(ds[i][...], stacked(weights[8 * i : 8 * i + 8]), NT)

    @pl.when(step == 0)
    def _():
        grad[...] = value

    @pl.when(step > 0)
    def _():
        grad[...] += value

    @pl.when(step == pl.num_programs(0) - 1)
    def _():
        restored(order, grad[...], held)
        g = held[...]
        x = x_ref[...].astype(F32)
        scale = lax.rsqrt(jnp.mean(x * x, axis=-1, keepdims=True) + EPS)
        inner = jnp.mean(g * x, axis=-1, keepdims=True) * (scale * scale * scale)
        out[...] = d_mid_ref[...] + scale * g - x * inner


def weight_grads_body(count, order, *refs):
    for i in range(count):
        g = dot(refs[2 * i][...], refs[2 * i + 1][...], TN, BF16)
        half = g.shape[0] // 2
        refs[2 * count + 2 * i][...] = g[:half]
        refs[2 * count + 2 * i + 1][...] = g[half:]


class Chain:
    def __init__(self, fresh, factor, forward, parts):
        self.fresh, self.factor, self.forward, self.parts = fresh, factor, forward, parts
        self.seqs = fresh.shape[0]
        self.now = [fresh[s] for s in range(self.seqs)]
        self.got = [[] for _ in range(self.seqs)]
        self.turns = self.seqs + parts - 2

    def pass_on(self, s, hop):
        pair = (hop - 1, hop) if self.forward else (self.parts - hop, self.parts - hop - 1)
        self.got[s].append(lax.ppermute(self.now[s], "heads", [pair]))

    def begin(self):
        for s in range(self.seqs):
            self.pass_on(s, 1)

    def at(self, turn):
        return [(s, turn - s) for s in range(self.seqs) if 1 <= turn - s < self.parts]

    def arrivals(self, turn):
        self.new = [self.got[s][hop - 1] for s, hop in self.at(turn)]
        return self, "new"

    def go_on(self, turn):
        for (s, hop), new in zip(self.at(turn), self.new):
            self.got[s][hop - 1] = new
            if hop + 1 < self.parts:
                arrived = new.astype(F32) * self.factor[s][:, None, None]
                self.now[s] = (self.fresh[s].astype(F32) + arrived).astype(BF16)
                self.pass_on(s, hop + 1)

    def result(self):
        return jnp.stack([functools.reduce(lambda a, b: a + b, g) for g in self.got])


class Layer:
    def __init__(self, tokens, doc_lengths, cotangent):
        seqs, length, width = tokens.shape
        self.seqs, self.length, self.width, self.count = seqs, length, width, seqs * length
        self.here = lax.axis_index("rows")
        self.place = lax.axis_index("heads")
        self.order = places(self.here, self.place)
        self.x = tokens.reshape(self.count, width)
        self.dy = cotangent.reshape(self.count, width)

        ends = jnp.cumsum(doc_lengths, axis=-1, dtype=jnp.int32)[:, :-1]

        def ids_at(where):
            return jnp.sum((where[None, :, None] >= ends[:, None, :]).astype(jnp.int32), axis=-1)

        start = self.place * length
        positions = start + jnp.arange(length, dtype=jnp.int32)
        ids = ids_at(positions)
        before = jnp.where(self.place > 0, ids_at(jnp.reshape(start - 1, (1,))), -1)
        final = ids[:, -1:]
        link = (ids == before).astype(F32)[:, :, None]
        tail = (ids == final).astype(F32)[:, :, None]
        slopes = jnp.array([slope_of(h) for h in range(HEADS)], F32)
        self.factor = (final == before).astype(F32) * jnp.exp(-slopes * length)[None, :]
        theta = jnp.exp(-math.log(10000.0) * jnp.arange(HEAD_DIM, dtype=F32) / HEAD_DIM)
        angle = positions.astype(F32)[:, None] * theta[None, :]

        table = pl.BlockSpec((length, HEAD_DIM), lambda s, *_: (0, 0))
        one_col = pl.BlockSpec((1, length, 1), lambda s, *_: (s, 0, 0))
        one_row = pl.BlockSpec((1, 1, length), lambda s, *_: (s, 0, 0))
        self.turn = [(jnp.cos(angle), table), (jnp.sin(angle), table)]
        self.link = link, one_col
        self.tail = tail, one_col
        self.masks = [(ids[:, :, None], one_col), (ids[:, None, :], one_row), self.link]
        self.seq = pl.BlockSpec((1, length, width), lambda s, *_: (s, 0, 0))
        self.state = pl.BlockSpec(
            (1, HEADS, 2 * HEAD_DIM, HEAD_DIM), lambda s, *_: (s, 0, 0, 0)
        )
        self.states = (seqs, HEADS, 2 * HEAD_DIM, HEAD_DIM), BF16, self.state
        step = min(self.count, 256)
        self.grid = (self.count // step,)
        self.wide = rows_spec(step, width)

    def rows(self, body, ins, types, order=None):
        return call(
            body, self.grid, self.order, [(a, self.wide) for a in ins],
            [((self.count, self.width), t, self.wide) for t in types],
        )

    def seqwise(self, body, ins, outs):
        shape = (self.seqs, self.length, self.width)
        ins = [i if isinstance(i, tuple) else (i.reshape(shape), self.seq) for i in ins]
        outs = [o if isinstance(o, tuple) else (shape, o, self.seq) for o in outs]
        got = call(body, (self.seqs,), self.order, ins, outs)
        return [g.reshape(self.count, self.width) if g.shape == shape else g for g in got]

    def norm(self):
        return self.rows(norm_body, [self.x], [BF16])

    def fresh(self, k_pre, v_pre):
        return self.seqwise(fresh_body, [k_pre, v_pre] + self.turn + [self.tail], [self.states])[0]

    def mix(self, q_pre, k_pre, v_pre, u_pre, state_in):
        ins = [q_pre, k_pre, v_pre, u_pre] + self.turn + self.masks + [(state_in, self.state)]
        return self.seqwise(mix_body, ins, [BF16, BF16])

    def mid(self, branch):
        return self.rows(mid_body, [self.x, branch], [F32, BF16])

    def mid_back(self, x_mid, grad):
        return self.rows(norm_back_body, [x_mid, self.dy, grad], [F32, BF16])

    def in_back(self, d_mid, grad):
        return self.rows(norm_back_body, [self.x, d_mid, grad], [F32])[0]

    def gate_back(self, q_pre, u_pre, mix, d_gated):
        ins = [q_pre, u_pre, mix, d_gated] + self.turn + [self.link]
        return self.seqwise(gate_back_body, ins, [BF16, BF16, self.states])

    def mix_back(self, q_pre, k_pre, v_pre, d_mix, state_in):
        ins = [q_pre, k_pre, v_pre, d_mix] + self.turn + self.masks + [(state_in, self.state)]
        return self.seqwise(mix_back_body, ins, [BF16, F32, F32])

    def state_back(self, k_pre, v_pre, dk_near, dv_near, d_state):
        ins = [k_pre, v_pre, dk_near, dv_near] + self.turn + [self.tail, (d_state, self.state)]
        return self.seqwise(state_back_body, ins, [BF16, BF16])


def plainly(layer, heads_count, weights):
    w_query, w_key, w_value, w_gate, w_out, w_left, w_right, w_down = (
        lax.all_gather(w, "rows", axis=0, tiled=True) for w in weights
    )

    def carried(fresh, forward):
        chain = Chain(fresh, layer.factor, forward, heads_count)
        chain.begin()
        for turn in range(1, chain.turns + 1):
            chain.arrivals(turn)
            chain.go_on(turn)
        return chain.result()

    def gradient(lhs, d):
        total = lax.psum_scatter(dot(lhs, d, TN, BF16), "rows", scatter_dimension=0, tiled=True)
        return lax.psum_scatter(total, "heads", scatter_dimension=1, tiled=True).astype(F32)

    (h_in,) = layer.norm()
    q_pre, k_pre, v_pre, u_pre = (
        dot(h_in, w, NN) for w in (w_query, w_key, w_value, w_gate)
    )
    state_in = carried(layer.fresh(k_pre, v_pre), True)
    mix, gated = layer.mix(q_pre, k_pre, v_pre, u_pre, state_in)
    x_mid, h_mid = layer.mid(dot(gated, w_out, NN))
    left, right = dot(h_mid, w_left, NN), dot(h_mid, w_right, NN)
    product = (left * right).astype(BF16)
    activations = (x_mid + dot(product, w_down, NN)).astype(BF16)
    grad_product = dot(layer.dy, w_down, NT)
    d_left = (grad_product * right).astype(BF16)
    d_right = (grad_product * left).astype(BF16)
    d_mid, d_branch = layer.mid_back(
        x_mid, dot(d_left, w_left, NT) + dot(d_right, w_right, NT)
    )
    d_u, d_mix, d_fresh = layer.gate_back(q_pre, u_pre, mix, dot(d_branch, w_out, NT))
    d_state = carried(d_fresh, False)
    d_q, dk_near, dv_near = layer.mix_back(q_pre, k_pre, v_pre, d_mix, state_in)
    d_k, d_v = layer.state_back(k_pre, v_pre, dk_near, dv_near, d_state)
    grad_in = (
        dot(d_q, w_query, NT) + dot(d_u, w_gate, NT) + dot(d_k, w_key, NT) + dot(d_v, w_value, NT)
    )
    input_grad = layer.in_back(d_mid, grad_in)
    pairs = (
        (h_in, d_q), (h_in, d_k), (h_in, d_v), (h_in, d_u), (gated, d_branch),
        (h_mid, d_left), (h_mid, d_right), (product, layer.dy),
    )
    return (activations, input_grad) + tuple(gradient(lhs, d) for lhs, d in pairs)


class Row:
    def __init__(self, doc_lengths, length, width, here, head):
        self.length, self.width = length, width
        self.order = places(here, head)
        lengths = lax.dynamic_index_in_dim(doc_lengths, head, 0, keepdims=False)
        ends = jnp.cumsum(lengths, dtype=jnp.int32)[:-1]
        positions = jnp.arange(length, dtype=jnp.int32)
        ids = jnp.sum((positions[:, None] >= ends[None, :]).astype(jnp.int32), axis=-1)
        theta = jnp.exp(-math.log(10000.0) * jnp.arange(HEAD_DIM, dtype=F32) / HEAD_DIM)
        angle = positions.astype(F32)[:, None] * theta[None, :]

        def whole(rows, cols):
            return pl.BlockSpec((rows, cols), lambda *_: (0, 0))

        table = whole(length, HEAD_DIM)
        self.extra = [
            (jnp.cos(angle), table), (jnp.sin(angle), table),
            (ids[:, None], whole(length, 1)), (ids[None, :], whole(1, length)),
        ]
        self.heads = pl.BlockSpec((length, 2 * HEAD_DIM), lambda h, *_: (0, h))
        self.wide = rows_spec(min(length, 256), width)
        self.all = whole(length, width)
        self.block = math.gcd(length, 256)
        self.flops = 2 * length * width * width

    def norm(self, x):
        return self.by_rows(row_norm_body, [(x, self.wide)], [], [BF16, BF16], [BF16])

    def pieces(self, group, half, width, column=None, offset=0):
        rows = group.pieces[0].shape[0]
        if column is None:
            spec = pl.BlockSpec((rows, width), lambda i, *_: (0, offset + i))
        else:
            spec = pl.BlockSpec((rows, width), lambda *_: (0, column))
        return [(a, spec) for a in group.all(half)]

    def project(self, h, att):
        half = self.width // 2
        out = (self.length, 2 * self.width), F32, pl.BlockSpec((self.length, half), lambda i, *_: (0, i))
        return call(
            project_body, (4,), self.order,
            [(h, self.all)] + self.pieces(att, 0, half) + self.pieces(att, 1, half), [out, out],
            flops=4 * self.flops,
        )

    def column(self, block, offset=0):
        return pl.BlockSpec((self.length, block), lambda i, *_: (0, offset + i))

    def mix(self, qk, vu):
        ins = [(qk, self.heads), (qk, self.column(2 * HEAD_DIM, HEADS // 2)), (vu, self.heads)]
        return call(
            functools.partial(row_mix_body, self.block), (HEADS // 2,), self.order, ins + self.extra,
            [((self.length, self.width), BF16, self.heads)], flops=self.flops * 3 // 8,
        )[0]

    def mix_back(self, qk, vu, d_mix):
        ins = [(qk, self.heads), (qk, self.column(2 * HEAD_DIM, HEADS // 2)), (vu, self.heads)]
        return call(
            functools.partial(row_mix_back_body, self.block), (HEADS // 2,), self.order,
            ins + [(d_mix, self.heads)] + self.extra,
            [((self.length, self.width), BF16, self.heads)] * 3, flops=self.flops,
        )

    def out_weights(self, att):
        half = self.width // 2
        return self.pieces(att, 0, half, 4) + self.pieces(att, 1, half, 4)

    def by_rows(self, body, ins, weights, types, scratch):
        step = self.wide.block_shape[0]
        return call(
            body, (self.length // step,), self.order, ins + weights,
            [((self.length, self.width), t, self.wide) for t in types],
            scratch=[pltpu.VMEM((step, self.width), t) for t in scratch], flops=self.flops,
        )

    def gate_spec(self):
        return pl.BlockSpec(self.wide.block_shape, lambda i, *_: (i, 1))

    def out_mid(self, mix, vu, x, att):
        return self.by_rows(
            out_mid_body, [(mix, self.wide), (vu, self.gate_spec()), (x, self.wide)],
            self.out_weights(att), [BF16, F32, BF16, BF16], [BF16, BF16],
        )

    def gate_out_back(self, d_branch, mix, vu, att):
        return self.by_rows(
            gate_out_back_body, [(d_branch, self.wide), (mix, self.wide), (vu, self.gate_spec())],
            self.out_weights(att), [BF16, BF16], [F32],
        )

    def left_right(self, h, ff):
        inner = ff.pieces[0].shape[1]
        block = math.gcd(inner, 1408)
        return call(
            left_right_body, (inner // block,), self.order,
            [(h, self.all)] + self.pieces(ff, 0, block) + self.pieces(ff, 1, block),
            [((self.length, inner), BF16, self.column(block))] * 3,
            flops=2 * self.flops * inner // self.width,
        )

    def down_grad(self, product, c):
        inner, half = product.shape[1], self.width // 2
        block = math.gcd(inner, 1408)
        rows = inner // 8
        got = call(
            functools.partial(down_grad_body, rows), (inner // block,), self.order,
            [(product, self.column(block)), (c, self.all)], [((4 * rows, half), BF16, HBM)] * 4,
            scratch=[pltpu.VMEM((inner, self.width), BF16), pltpu.SemaphoreType.DMA((2, 8))],
            flops=self.flops * inner // self.width,
        )
        return Reduce(self.order, got[2:], got[:2], [2, 4])

    def feed_back(self, left, right, product, h_x, h_y, c, x_mid, ff, down):
        inner, rows = ff.pieces[0].shape[1], down.pieces[0].shape[0]
        block = math.gcd(inner, 256)
        steps = inner // block

        def now(rows):
            return pl.BlockSpec((rows, block), lambda i, *_: (0, jnp.minimum(i, steps - 1)))

        def before(rows):
            return pl.BlockSpec((rows, block), lambda i, *_: (0, jnp.maximum(i - 1, 0)))

        full = (self.length, self.width)
        weights = [
            (a, before(ff.pieces[0].shape[0])) for a in ff.all(0) + ff.all(1)
        ]
        return call(
            functools.partial(feed_back_body, rows), (steps + 1,), self.order,
            [(left, now(self.length)), (right, now(self.length)), (product, before(self.length))]
            + [(a, self.all) for a in (h_x, h_y, c, x_mid)]
            + weights + [(a, HBM) for a in down.all(0) + down.all(1)],
            [((self.width // 2, inner), BF16, before(self.width // 2))] * 4
            + [(full, F32, self.all), (full, BF16, self.all), (full, BF16, self.all)],
            scratch=[pltpu.VMEM((inner, self.width), BF16)] + [pltpu.VMEM(full, F32)] * 2
            + [pltpu.VMEM((self.length, block), BF16)] * 2 + [pltpu.SemaphoreType.DMA((2, 8))],
            flops=6 * self.flops * inner // self.width,
        )

    def in_back(self, x, d_mid, ds, att):
        half = self.width // 2
        weights = []
        for which, offset in ((0, 0), (0, 2), (1, 0), (1, 2)):
            weights += self.pieces(att, which, half, offset=offset)
        full = (self.length, self.width)
        return call(
            in_back_body, (2,), self.order,
            [(x, self.all), (d_mid, self.all)] + [(d, self.column(half)) for d in ds] + weights,
            [(full, F32, self.all)], scratch=[pltpu.VMEM(full, F32)] * 2, flops=4 * self.flops,
        )[0]

    def weight_grads(self, pairs, bits):
        half = self.width // 2
        tall = pl.BlockSpec((half, half), lambda i, *_: (0, i))
        ins = []
        for lhs, d in pairs:
            ins += [(lhs, self.all), (d, self.column(half))]
        got = call(
            functools.partial(weight_grads_body, len(pairs)), (2,), self.order, ins,
            [((half, self.width), BF16, tall)] * (2 * len(pairs)), flops=len(pairs) * self.flops,
        )
        return Reduce(self.order, got[1::2], got[::2], bits)


def stepwise(tokens, doc_lengths, cotangent, weights):
    w_query, w_key, w_value, w_gate, w_out, w_left, w_right, w_down = weights
    size, width = tokens.shape[1:]
    length, half = 4 * size, width // 2
    here, head = lax.axis_index("rows"), lax.axis_index("heads")
    row = Row(doc_lengths, length, width, here, head)
    order = row.order
    v = types.SimpleNamespace()
    clock = Clock(order)
    tick = clock.tick

    def exchanged(a):
        return lax.all_to_all(a.reshape(4, size, width), "heads", 0, 0, tiled=True)

    def whole_row(a):
        return exchanged(a).reshape(length, width)

    att = Gather(
        pack(
            order, [w_query, w_key, w_value, w_gate, w_out],
            [[(0, 0, width), (1, 0, width), (4, 0, half)], [(2, 0, width), (3, 0, width), (4, half, half)]],
        )
    )
    att.first()
    v.x = whole_row(tokens)
    v.down = pack(order, [w_down], [[(0, 0, half)], [(0, half, half)]])
    v.ff = [w_left, w_right]
    att.cross("pieces")
    tick((v, "x"), (v, "down"), (att, "pieces_other"))
    v.h = row.norm(v.x)
    tick((att, "near_x"), (att, "near_y"), (v, "ff"), (v, "down"), (v, "h"))
    att.second()
    ff = Gather(v.ff)
    ff.first()
    att.cross("near_x", "near_y")
    tick((att, "far"), (att, "near_x_other"), (att, "near_y_other"))
    att.cross("far")
    tick((att, "far_other"), (v, "h"))
    v.qk, v.vu = row.project(v.h[0], att)
    tick((v, "qk"), (v, "vu"))
    v.c = cotangent
    tick((v, "c"))
    v.c = whole_row(v.c)
    v.mix = row.mix(v.qk, v.vu)
    tick((v, "mix"), (ff, "near_x"), (ff, "near_y"), (ff, "pieces"), (v, "down"))
    ff.second()
    ff.cross("pieces", "near_x", "near_y")
    down = Gather(v.down)
    down.first()
    gated, v.x_mid, *v.h_mid = row.out_mid(v.mix, v.vu, v.x, att)
    tick((v, "x_mid"), (v, "h_mid"), (v, "c"), (ff, "far"))
    ff.cross("far")
    tick((v, "c"), (ff, "far_other"), (v, "h_mid"))

    v.left, v.right, v.product = row.left_right(v.h_mid[0], ff)
    tick((v, "left"), (v, "right"), (v, "product"), (down, "near_x"), (down, "near_y"), (down, "pieces"))
    down.second()
    down.cross("pieces", "near_x", "near_y")
    r_down = row.down_grad(v.product, v.c)
    tick((r_down, "sends"), (down, "far"), (v, "left"))
    r_down.core()
    down.cross("far")
    tick((r_down, "theirs"), (down, "far_other"), (v, "left"))
    r_down.join()
    tick((r_down, "totals"), (v, "left"))
    r_down.first()
    keep_l, send_l, keep_r, send_r, v.d_mid, v.d_branch, v.act = row.feed_back(
        v.left, v.right, v.product, v.h_mid[1], v.h_mid[0], v.c, v.x_mid, ff, down
    )
    r_ff = Reduce(order, [send_l, send_r], [keep_l, keep_r], [2, 4])
    tick((r_ff, "sends"), (v, "d_mid"), (v, "d_branch"), (v, "act"), (r_down, "got"))
    r_ff.core()
    r_down.join_first()
    tick((r_down, "parts"), (v, "d_branch"), (v, "act"))
    r_down.second()
    v.act = exchanged(v.act)
    v.d_u, v.d_mix = row.gate_out_back(v.d_branch, v.mix, v.vu, att)
    tick((r_ff, "theirs"), (v, "d_u"), (v, "d_mix"), (r_down, "got_last"))
    r_ff.join()
    tick((r_ff, "totals"), (v, "d_mix"))
    r_ff.first()
    v.d_q, v.d_k, v.d_v = row.mix_back(v.qk, v.vu, v.d_mix)
    tick((v, "d_q"), (v, "d_k"), (v, "d_v"), (v, "act"), (r_down, "own"), (r_down, "got_last"))
    s_down = SettleWide(order, [jnp.concatenate(r_down.own, axis=1)], [jnp.concatenate(r_down.got_last, axis=1)])
    tick((s_down, "out"), (s_down, "own"), (v, "d_q"))
    s_down.pass_on(1)
    r_att = row.weight_grads(
        [(v.h[1], v.d_q), (v.h[0], v.d_k), (v.h[1], v.d_v), (v.h[0], v.d_u), (gated, v.d_branch)],
        [2, 4, 2, 4, 2],
    )
    tick((r_att, "sends"), (r_ff, "got"), (s_down, "got"))
    r_att.core()
    r_ff.join_first()
    tick((r_ff, "parts"), (r_att, "theirs"), (s_down, "got"))
    r_ff.second()
    r_att.join()
    s_down.join()
    tick((r_att, "totals"), (s_down, "out"), (v, "d_q"))
    r_att.first()
    s_down.pass_on(2)
    v.input_grad = row.in_back(v.x, v.d_mid, [v.d_q, v.d_k, v.d_v, v.d_u], att)
    tick((v, "input_grad"), (r_ff, "got_last"), (s_down, "got"))
    r_ff.join_second()
    s_ff = Settle(r_ff.sums, head)
    tick((s_ff, "out"), (s_ff, "own"), (v, "input_grad"))
    s_ff.pass_on(1)
    tick((r_att, "got"), (v, "input_grad"))
    r_att.join_first()
    tick((r_att, "parts"), (s_ff, "got"), (v, "input_grad"))
    r_att.second()
    s_ff.join()
    (g_down,) = s_down.result()
    tick((s_ff, "out"), (v, "input_grad"))
    s_ff.pass_on(2)
    back = exchanged(v.input_grad.astype(BF16))
    tick((r_att, "got_last"), (r_att, "own"))
    s_att = SettleWide(order, r_att.own, r_att.got_last)
    tick((s_att, "out"), (s_att, "own"))
    s_att.pass_on(1)
    tick((s_att, "got"), (s_ff, "got"))
    s_att.join()
    tick((s_att, "out"))
    s_att.pass_on(2)
    g_left, g_right = s_ff.result()
    g_query, g_key, g_value, g_gate, g_out = s_att.result()
    return (
        v.act, back.astype(F32), g_query, g_key, g_value, g_gate, g_out, g_left, g_right, g_down
    )


def on_device(rows_count, heads_count, tokens, doc_lengths, cotangent, *weights):
    if rows_count == 8 and heads_count == 4 and tokens.shape[0] == 4:
        return stepwise(tokens, doc_lengths, cotangent, weights)
    layer = Layer(tokens, doc_lengths, cotangent)
    activations, input_grad, *grads = plainly(layer, heads_count, weights)
    return (activations.reshape(tokens.shape), input_grad.reshape(tokens.shape), *grads)


def solution(mesh):
    sizes = dict(mesh.shape)
    tokens = P("rows", "heads", None)
    weights = P("rows", None)
    grads = P("rows", "heads")
    return jax.shard_map(
        functools.partial(on_device, sizes["rows"], sizes["heads"]),
        mesh=mesh,
        in_specs=(tokens, weights, tokens) + (weights,) * 8,
        out_specs=(tokens, tokens) + (grads,) * 8,
        check_vma=False,
    )
```

```python
import functools
import math
import types

import jax
import jax.numpy as jnp
from jax import lax
from jax.experimental import pallas as pl
from jax.experimental.pallas import tpu as pltpu
from jax.sharding import PartitionSpec as P

HEADS = 8
HEAD_DIM = 128
EPS = 1e-06
F32 = jnp.float32
BF16 = jnp.bfloat16
VMEM_LIMIT = 60 << 20

BITS = (0, 2, 4, 6, 1, 3, 5, 7)
BITS_X = (0, 4, 2, 6, 1, 5, 3, 7)
BITS_Y = (0, 2, 4, 6, 1, 3, 5, 7)


def after(value, *others):
    return lax.optimization_barrier((value,) + others)[0]


def dot(a, b, dims, out=F32):
    return lax.dot_general(a, b, (dims, ((), ())), preferred_element_type=F32).astype(out)


NN = ((1,), (0,))
NT = ((1,), (1,))
TN = ((0,), (0,))


def swap(value, bit, size):
    return lax.ppermute(value, "rows", [(i, i ^ bit) for i in range(size)])


def swap_heads(value, bit):
    return lax.ppermute(value, "heads", [(i, i ^ bit) for i in range(4)])


HBM = pl.BlockSpec(memory_space=pltpu.HBM)


def whole_spec(rows, width):
    return pl.BlockSpec((rows, width), lambda i, *_: (0, 0))


def run_copies(copies):
    for copy in copies:
        copy.start()
    for copy in copies:
        copy.wait()


def pack(order, arrays, lists):
    rows = arrays[0].shape[0]
    widths = [sum(w for _, _, w in parts) for parts in lists]
    most = max(len(parts) for parts in lists)

    def body(order, *refs):
        ins, outs, sems = refs[: len(arrays)], refs[len(arrays) : -1], refs[-1]
        copies = []
        for j, parts in enumerate(lists):
            at = 0
            for i, (which, begin, width) in enumerate(parts):
                copies.append(
                    pltpu.make_async_copy(
                        ins[which].at[:, begin : begin + width],
                        outs[j].at[:, at : at + width],
                        sems.at[j, i],
                    )
                )
                at += width
        run_copies(copies)

    return call(
        body, (1,), order, [(a, HBM) for a in arrays],
        [((rows, w), BF16, whole_spec(rows, w)) for w in widths],
        scratch=[pltpu.SemaphoreType.DMA((len(lists), most))],
    )


class Clock:
    def __init__(self, start):
        self.token = start

    def tick(self, *places):
        held = [getattr(o, n) for o, n in places]
        held, self.token = lax.optimization_barrier((held, self.token))
        for (o, n), value in zip(places, held):
            setattr(o, n, value)


def places(here, head):
    return jnp.stack([here ^ b for b in range(8)] + [head ^ b for b in range(4)]).astype(jnp.int32)


class Gather:
    def __init__(self, pieces):
        self.pieces = list(pieces)
        self.near_x, self.near_y = [None, None], [None, None]

    def first(self, *halves):
        for half in halves or (0, 1):
            self.near_x[half] = swap(self.pieces[half], 2, 8)
            self.near_y[half] = swap(self.pieces[half], 4, 8)

    def second(self):
        self.far = [swap(self.near_x[0], 4, 8), swap(self.near_y[1], 2, 8)]

    def cross(self, *names):
        for name in names:
            setattr(self, name + "_other", [swap(p, 1, 8) for p in getattr(self, name)])

    def all(self, half):
        names = ("pieces", "near_x", "near_y", "far")
        return [getattr(self, n + core)[half] for core in ("", "_other") for n in names]


def added(*terms):
    return functools.reduce(lambda a, b: a + b, [t.astype(F32) for t in terms]).astype(BF16)


class Reduce:
    def __init__(self, order, sends, keeps, bits):
        self.order, self.sends, self.keeps, self.bits = order, list(sends), list(keeps), list(bits)

    def core(self):
        self.theirs = [swap(s, 1, 8) for s in self.sends]

    def join(self):
        half = self.keeps[0].shape[0] // 2
        self.totals = [added(k[half:], t[half:]) for k, t in zip(self.keeps, self.theirs)]

    def first(self):
        self.got = [swap(t, b, 8) for t, b in zip(self.totals, self.bits)]

    def join_first(self):
        rows = self.keeps[0].shape[0] // 4
        self.own, self.parts = (
            [
                added(k[at : at + rows], t[at : at + rows], g[at : at + rows])
                for k, t, g in zip(self.keeps, self.theirs, self.got)
            ]
            for at in (0, rows)
        )

    def second(self):
        self.got_last = [swap(p, 6 - b, 8) for p, b in zip(self.parts, self.bits)]

    def settle(self, block, starts):
        return Settle(self.order, self.own, self.got_last, block, starts)


class Settle:
    def __init__(self, order, parts, got, block, starts):
        self.order, self.block, self.count = order, block, len(starts)
        rows = self.rows = parts[0].shape[0]
        widths = [p.shape[1] for p in parts]
        each = 2 if got else 1

        def body(order, *refs):
            own, out, held = refs[each * len(parts) :]
            at = 0
            for i, width in enumerate(widths):
                total = refs[each * i][...].astype(F32)
                if got:
                    total += refs[each * i + 1][...].astype(F32)
                held[:, at : at + width] = total
                at += width
            for z in range(4):

                @pl.when(order[8] == z)
                def _(z=z):
                    for i, start in enumerate(starts):
                        for j in range(2):
                            mine, theirs = start(z ^ (2 * j)), start(z ^ (2 * j + 1))
                            own[2 * i + j] = held[:, mine : mine + block]
                            out[2 * i + j] = held[:, theirs : theirs + block].astype(BF16)

        self.own, self.out = call(
            body, (1,), order,
            [(a, whole_spec(*a.shape)) for terms in zip(parts, *([got] if got else [])) for a in terms],
            [self.entry(2 * self.count, F32), self.entry(2 * self.count, BF16)],
            scratch=[pltpu.VMEM((rows, sum(widths)), F32)],
        )

    def entry(self, count, dtype):
        shape = (count, self.rows, self.block)
        return shape, dtype, pl.BlockSpec(shape, lambda *_: (0, 0, 0))

    def given(self):
        return [(a, pl.BlockSpec(a.shape, lambda *_: (0, 0, 0))) for a in (self.own, self.got)]

    def pass_on(self, bit):
        self.got = lax.ppermute(self.out, "heads", [(i, i ^ bit) for i in range(4)])

    def join(self):
        count = self.count

        def body(order, own_ref, got_ref, mine, out):
            for i in range(count):
                mine[i] = own_ref[2 * i] + got_ref[2 * i].astype(F32)
                out[i] = (own_ref[2 * i + 1] + got_ref[2 * i + 1].astype(F32)).astype(BF16)

        self.own, self.out = call(
            body, (1,), self.order, self.given(), [self.entry(count, F32), self.entry(count, BF16)]
        )

    def result(self):
        def body(order, own_ref, got_ref, *outs):
            for i, out in enumerate(outs):
                out[...] = own_ref[i] + got_ref[i].astype(F32)

        shape = (self.rows, self.block)
        return call(
            body, (1,), self.order, self.given(), [(shape, F32, whole_spec(*shape))] * self.count
        )


def at_block(order_ref, index, width):
    return pl.ds(pl.multiple_of(order_ref[index] * width, width), width)


def sigmoid(v):
    return 1.0 / (1.0 + jnp.exp(-v))


def swish_slope(v):
    sig = sigmoid(v)
    return sig * (1.0 + v * (1.0 - sig))


def call(body, grid, order, ins, outs, scratch=(), flops=0):
    moved = sum(a.size * a.dtype.itemsize for a, _ in ins) + sum(
        math.prod(s) * jnp.dtype(t).itemsize for s, t, _ in outs
    )
    return pl.pallas_call(
        body,
        grid_spec=pltpu.PrefetchScalarGridSpec(
            num_scalar_prefetch=1,
            grid=grid,
            in_specs=[spec for _, spec in ins],
            out_specs=[spec for _, _, spec in outs],
            scratch_shapes=list(scratch),
        ),
        out_shape=[jax.ShapeDtypeStruct(s, t) for s, t, _ in outs],
        compiler_params=pltpu.CompilerParams(vmem_limit_bytes=VMEM_LIMIT),
        cost_estimate=pl.CostEstimate(flops=flops // 4, bytes_accessed=moved // 4, transcendentals=0),
    )(order, *[a for a, _ in ins])


def rows_spec(count, width, column=0):
    return pl.BlockSpec((count, width), lambda i, *_: (i, column))


def norm_body(order, x_ref, h_ref):
    x = x_ref[...].astype(F32)
    scale = lax.rsqrt(jnp.mean(x * x, axis=-1, keepdims=True) + EPS)
    h_ref[...] = (x * scale).astype(BF16)


def mid_body(order, x_ref, b_ref, mid_ref, h_ref):
    mid = x_ref[...].astype(F32) + b_ref[...]
    mid_ref[...] = mid
    scale = lax.rsqrt(jnp.mean(mid * mid, axis=-1, keepdims=True) + EPS)
    h_ref[...] = (mid * scale).astype(BF16)


def norm_back_body(order, v_ref, base_ref, g_ref, *outs):
    v = v_ref[...].astype(F32)
    g = g_ref[...]
    scale = lax.rsqrt(jnp.mean(v * v, axis=-1, keepdims=True) + EPS)
    inner = jnp.mean(g * v, axis=-1, keepdims=True) * (scale * scale * scale)
    total = base_ref[...].astype(F32) + scale * g - v * inner
    outs[0][...] = total
    if len(outs) > 1:
        outs[1][...] = total.astype(BF16)


def ramp(rows, start, sign, slope):
    place = lax.broadcasted_iota(jnp.int32, (rows, HEAD_DIM), 0).astype(F32)
    return jnp.exp(-slope * (start + sign * place))


def decays(ids_col, ids_row, slope):
    rows = ids_col.shape[0]
    gap = (
        lax.broadcasted_iota(jnp.int32, (rows, rows), 0)
        - lax.broadcasted_iota(jnp.int32, (rows, rows), 1)
    ).astype(F32)
    keep = (gap >= 0.0) & (ids_col == ids_row)
    return jnp.where(keep, jnp.exp(-slope * jnp.maximum(gap, 0.0)), 0.0)


def slope_of(head):
    return 2.0 ** (-8.0 * (head + 1) / HEADS)


def columns(head):
    return slice(head * HEAD_DIM, (head + 1) * HEAD_DIM)


def turned(a, cos, sin):
    return jnp.concatenate([a * cos, a * sin], axis=1)


def rounded_swish(v):
    return (v * sigmoid(v)).astype(BF16).astype(F32)


def fresh_body(order, k_ref, v_ref, cos_ref, sin_ref, tail_ref, state_ref):
    rows = k_ref.shape[1]
    cos, sin = cos_ref[...], sin_ref[...]
    tail = tail_ref[0]
    for head in range(HEADS):
        key = rounded_swish(k_ref[0, :, columns(head)])
        key = key * (ramp(rows, rows - 1.0, -1.0, slope_of(head)) * tail)
        value = v_ref[0, :, columns(head)].astype(BF16)
        state_ref[0, head] = dot(turned(key, cos, sin).astype(BF16), value, TN, BF16)


def mix_body(
    order, q_ref, k_ref, v_ref, u_ref, cos_ref, sin_ref, col_ref, row_ref, link_ref, s_ref,
    mix_ref, gated_ref,
):
    rows = q_ref.shape[1]
    cos, sin = cos_ref[...], sin_ref[...]
    ids_col, ids_row = col_ref[0], row_ref[0]
    link = link_ref[0]
    power = jnp.zeros((rows, 1), F32)
    for head in range(HEADS):
        cols = columns(head)
        slope = slope_of(head)
        rq = turned(rounded_swish(q_ref[0, :, cols]), cos, sin).astype(BF16)
        rk = turned(rounded_swish(k_ref[0, :, cols]), cos, sin).astype(BF16)
        value = v_ref[0, :, cols].astype(BF16)
        weights = (dot(rq, rk, NT) * decays(ids_col, ids_row, slope)).astype(BF16)
        mixed = dot(weights, value, NN) + dot(rq, s_ref[0, head], NN) * (
            ramp(rows, 1.0, 1.0, slope) * link
        )
        mixed = mixed.astype(BF16)
        mix_ref[0, :, cols] = mixed
        mixed = mixed.astype(F32)
        power += jnp.sum(mixed * mixed, axis=-1, keepdims=True)
    scale = lax.rsqrt(power / (HEADS * HEAD_DIM) + EPS)
    for head in range(HEADS):
        cols = columns(head)
        u = u_ref[0, :, cols]
        gated_ref[0, :, cols] = (
            mix_ref[0, :, cols].astype(F32) * scale * (u * sigmoid(u))
        ).astype(BF16)


def gate_back_body(
    order, q_ref, u_ref, mix_ref, dg_ref, cos_ref, sin_ref, link_ref, du_ref, dm_ref, state_ref
):
    rows = q_ref.shape[1]
    cos, sin = cos_ref[...], sin_ref[...]
    link = link_ref[0]
    mix = mix_ref[0].astype(F32)
    scale = lax.rsqrt(jnp.mean(mix * mix, axis=-1, keepdims=True) + EPS)
    inner = jnp.zeros((rows, 1), F32)
    for head in range(HEADS):
        cols = columns(head)
        u = u_ref[0, :, cols]
        part = mix_ref[0, :, cols].astype(F32)
        dg = dg_ref[0, :, cols]
        sig = sigmoid(u)
        inner += jnp.sum(dg * (u * sig) * part, axis=-1, keepdims=True)
        du_ref[0, :, cols] = (dg * part * scale * (sig * (1.0 + u * (1.0 - sig)))).astype(BF16)
    inner = inner * (scale * scale * scale) / (HEADS * HEAD_DIM)
    for head in range(HEADS):
        cols = columns(head)
        u = u_ref[0, :, cols]
        part = mix_ref[0, :, cols].astype(F32)
        dg = dg_ref[0, :, cols]
        d_mix = (scale * (dg * (u * sigmoid(u))) - part * inner).astype(BF16)
        dm_ref[0, :, cols] = d_mix
        query = rounded_swish(q_ref[0, :, cols]) * (
            ramp(rows, 1.0, 1.0, slope_of(head)) * link
        )
        state_ref[0, head] = dot(turned(query, cos, sin).astype(BF16), d_mix, TN, BF16)


def mix_back_body(
    order, q_ref, k_ref, v_ref, dm_ref, cos_ref, sin_ref, col_ref, row_ref, link_ref, s_ref,
    dq_ref, dk_ref, dv_ref,
):
    rows = q_ref.shape[1]
    cos, sin = cos_ref[...], sin_ref[...]
    ids_col, ids_row = col_ref[0], row_ref[0]
    link = link_ref[0]
    for head in range(HEADS):
        cols = columns(head)
        slope = slope_of(head)
        q_pre = q_ref[0, :, cols]
        rq = turned(rounded_swish(q_pre), cos, sin).astype(BF16)
        rk = turned(rounded_swish(k_ref[0, :, cols]), cos, sin).astype(BF16)
        value = v_ref[0, :, cols].astype(BF16)
        d_mix = dm_ref[0, :, cols]
        decay = decays(ids_col, ids_row, slope)
        weights = (dot(rq, rk, NT) * decay).astype(BF16)
        d_scores = (dot(d_mix, value, NT) * decay).astype(BF16)
        enter = ramp(rows, 1.0, 1.0, slope) * link
        d_rq = dot(d_scores, rk, NN) + dot(d_mix, s_ref[0, head], NT) * jnp.concatenate(
            [enter, enter], axis=1
        )
        d_query = d_rq[:, :HEAD_DIM] * cos + d_rq[:, HEAD_DIM:] * sin
        dq_ref[0, :, cols] = (
            d_query.astype(BF16).astype(F32) * swish_slope(q_pre)
        ).astype(BF16)
        d_rk = dot(d_scores, rq, TN)
        dk_ref[0, :, cols] = d_rk[:, :HEAD_DIM] * cos + d_rk[:, HEAD_DIM:] * sin
        dv_ref[0, :, cols] = dot(weights, d_mix, TN)


def state_back_body(
    order, k_ref, v_ref, dk_ref, dv_ref, cos_ref, sin_ref, tail_ref, s_ref, dko_ref, dvo_ref
):
    rows = k_ref.shape[1]
    cos, sin = cos_ref[...], sin_ref[...]
    tail = tail_ref[0]
    for head in range(HEADS):
        cols = columns(head)
        k_pre = k_ref[0, :, cols]
        leave = ramp(rows, rows - 1.0, -1.0, slope_of(head)) * tail
        key = rounded_swish(k_pre) * leave
        rk = turned(key, cos, sin).astype(BF16)
        value = v_ref[0, :, cols].astype(BF16)
        state = s_ref[0, head]
        d_rk = dot(value, state, NT) * jnp.concatenate([leave, leave], axis=1)
        d_key = dk_ref[0, :, cols] + d_rk[:, :HEAD_DIM] * cos + d_rk[:, HEAD_DIM:] * sin
        dko_ref[0, :, cols] = (d_key.astype(BF16).astype(F32) * swish_slope(k_pre)).astype(BF16)
        dvo_ref[0, :, cols] = (dv_ref[0, :, cols] + dot(rk, state, NN)).astype(BF16)


ORDERS = (BITS_Y, BITS_X)


def spread(order, h_ref, outs):
    width = h_ref.shape[1] // 8
    for out, bits in zip(outs, ORDERS):
        for k in range(8):
            out[:, k * width : (k + 1) * width] = h_ref[:, at_block(order, bits[k], width)]


def row_norm_body(order, x_ref, *refs):
    x = x_ref[...].astype(F32)
    scale = lax.rsqrt(jnp.mean(x * x, axis=-1, keepdims=True) + EPS)
    refs[-1][...] = (x * scale).astype(BF16)
    spread(order, refs[-1], refs[:-1])


def head_slope(head):
    return jnp.exp2(-8.0 * (head.astype(F32) + 1.0) / HEADS)


def block_decay(ids_col, ids_row, i, j, size, slope):
    gap = (
        (i - j) * size
        + lax.broadcasted_iota(jnp.int32, (size, size), 0)
        - lax.broadcasted_iota(jnp.int32, (size, size), 1)
    ).astype(F32)
    same = ids_col[i * size : (i + 1) * size] == ids_row[:, j * size : (j + 1) * size]
    keep = same if i > j else same & (gap >= 0.0)
    return jnp.where(keep, jnp.exp(-slope * jnp.maximum(gap, 0.0)), 0.0)


def row_mix_body(size, order, q_ref, k_ref, v_ref, cos_ref, sin_ref, col_ref, row_ref, mix_ref):
    q_ref, k_ref, v_ref = q_ref.at[0], k_ref.at[0], v_ref.at[0]
    cos, sin = cos_ref[...], sin_ref[...]
    col, row = col_ref[...], row_ref[...]
    each = q_ref.shape[1] // HEAD_DIM
    for part in range(each):
        cols = columns(part)
        slope = head_slope(pl.program_id(0) * each + part)
        rq = turned(rounded_swish(q_ref[:, cols]), cos, sin).astype(BF16)
        rk = turned(rounded_swish(k_ref[:, cols]), cos, sin).astype(BF16)
        value = v_ref[:, cols].astype(BF16)
        for i in range(rq.shape[0] // size):
            here = slice(i * size, (i + 1) * size)
            mixed = jnp.zeros((size, HEAD_DIM), F32)
            for j in range(i + 1):
                there = slice(j * size, (j + 1) * size)
                scores = dot(rq[here], rk[there], NT) * block_decay(col, row, i, j, size, slope)
                mixed += dot(scores.astype(BF16), value[there], NN)
            mix_ref[here, cols] = mixed.astype(BF16)


def row_mix_back_body(
    size, order, q_ref, k_ref, v_ref, dm_ref, cos_ref, sin_ref, col_ref, row_ref,
    d_ref,
):
    q_ref, k_ref, v_ref = q_ref.at[0], k_ref.at[0], v_ref.at[0]
    dq_ref, dk_ref, dv_ref = d_ref.at[0, 0], d_ref.at[0, 1], d_ref.at[0, 2]
    cos, sin = cos_ref[...], sin_ref[...]
    col, row = col_ref[...], row_ref[...]
    each = q_ref.shape[1] // HEAD_DIM
    count = q_ref.shape[0] // size
    cut = [slice(i * size, (i + 1) * size) for i in range(count)]

    def back(d_turned, pre, at):
        d = d_turned[:, :HEAD_DIM] * cos[at] + d_turned[:, HEAD_DIM:] * sin[at]
        return (d.astype(BF16).astype(F32) * swish_slope(pre[at])).astype(BF16)

    for part in range(each):
        cols = columns(part)
        slope = head_slope(pl.program_id(0) * each + part)
        q_pre, k_pre = q_ref[:, cols], k_ref[:, cols]
        rq = turned(rounded_swish(q_pre), cos, sin).astype(BF16)
        rk = turned(rounded_swish(k_pre), cos, sin).astype(BF16)
        value = v_ref[:, cols].astype(BF16)
        d_mix = dm_ref[:, cols]
        d_rq = [0.0] * count
        d_rk = [0.0] * count
        d_value = [0.0] * count
        for i in range(count):
            for j in range(i + 1):
                decay = block_decay(col, row, i, j, size, slope)
                scores = (dot(rq[cut[i]], rk[cut[j]], NT) * decay).astype(BF16)
                d_scores = (dot(d_mix[cut[i]], value[cut[j]], NT) * decay).astype(BF16)
                d_value[j] += dot(scores, d_mix[cut[i]], TN)
                d_rq[i] += dot(d_scores, rk[cut[j]], NN)
                d_rk[j] += dot(d_scores, rq[cut[i]], TN)
        for i in range(count):
            dq_ref[cut[i], cols] = back(d_rq[i], q_pre, cut[i])
            dk_ref[cut[i], cols] = back(d_rk[i], k_pre, cut[i])
            dv_ref[cut[i], cols] = d_value[i].astype(BF16)


def stacked(refs):
    return jnp.concatenate([r[...] for r in refs], axis=0)


def restored(order, value, out):
    width = value.shape[1] // 8
    for k, at in enumerate(BITS_Y):
        out[:, at_block(order, at, width)] = value[:, k * width : (k + 1) * width]


def project_body(order, h_ref, *refs):
    h = h_ref[...]
    refs[16][0] = dot(h, stacked(refs[:8]), NN)
    refs[16][1] = dot(h, stacked(refs[8:16]), NN)


def out_mid_body(order, mix_ref, h_in_ref, x_ref, *refs):
    u_ref, gated_ref, gated_x_ref, mid_ref = refs[16:20]
    held = refs[-1]
    mix = mix_ref[...].astype(F32)
    u = dot(h_in_ref[...], stacked(refs[:8]), NN)
    u_ref[...] = u
    scale = lax.rsqrt(jnp.mean(mix * mix, axis=-1, keepdims=True) + EPS)
    held[...] = (mix * scale * (u * sigmoid(u))).astype(BF16)
    spread(order, held, (gated_ref, gated_x_ref))
    mid = x_ref[...].astype(F32) + dot(gated_ref[...], stacked(refs[8:16]), NN)
    mid_ref[...] = mid
    scale = lax.rsqrt(jnp.mean(mid * mid, axis=-1, keepdims=True) + EPS)
    held[...] = (mid * scale).astype(BF16)
    spread(order, held, refs[20:22])


def left_right_body(order, h_ref, *refs):
    left_ref, right_ref, product_ref = refs[16:]
    h = h_ref[...]
    left = dot(h, stacked(refs[:8]), NN)
    right = dot(h, stacked(refs[8:16]), NN)
    left_ref[...] = left.astype(BF16)
    right_ref[...] = right.astype(BF16)
    product_ref[...] = (left * right).astype(BF16)


def down_grad_body(rows, order, product_ref, c_ref, *refs):
    outs, held, sems = refs[:4], refs[4], refs[5]
    step = pl.program_id(0)
    size = product_ref.shape[1]
    held[pl.ds(pl.multiple_of(step * size, size), size), :] = dot(
        product_ref[...], c_ref[...], TN, BF16
    )

    @pl.when(step == pl.num_programs(0) - 1)
    def _():
        half = held.shape[1] // 2
        copies = []
        for side, bits in enumerate((BITS_X, BITS_Y)):
            for k, bit in enumerate(bits):
                copies.append(
                    pltpu.make_async_copy(
                        held.at[at_block(order, bit, rows), side * half : (side + 1) * half],
                        outs[2 * (k // 4) + side].at[(k % 4) * rows : (k % 4 + 1) * rows, :],
                        sems.at[side, k],
                    )
                )
        run_copies(copies)


def feed_back_body(
    rows, order, left_ref, right_ref, product_ref, hx_ref, hy_ref, c_ref, mid_ref, *refs
):
    weights, downs = refs[:16], refs[16:32]
    keep_l, send_l, keep_r, send_r, d_mid_ref, d_branch_ref, act_ref = refs[32:39]
    down, grad, total, held_l, held_r, sems = refs[39:]
    step = pl.program_id(0)

    @pl.when(step == 0)
    def _():
        half = down.shape[1] // 2
        run_copies(
            [
                pltpu.make_async_copy(
                    downs[8 * side + k],
                    down.at[at_block(order, at, rows), side * half : (side + 1) * half],
                    sems.at[side, k],
                )
                for side in range(2)
                for k, at in enumerate(BITS_Y)
            ]
        )
        held_l[...] = jnp.zeros_like(held_l)
        held_r[...] = jnp.zeros_like(held_r)

    size = left_ref.shape[1]
    last = pl.num_programs(0) - 2

    def down_rows(block):
        return down[pl.ds(pl.multiple_of(block * size, size), size), :]

    d_left, d_right = held_l[...], held_r[...]
    half = hx_ref.shape[1] // 2
    g_left = dot(hx_ref[...], d_left, TN, BF16)
    keep_l[...] = g_left[:half]
    send_l[...] = g_left[half:]
    g_right = dot(hy_ref[...], d_right, TN, BF16)
    keep_r[...] = g_right[:half]
    send_r[...] = g_right[half:]
    total[...] += dot(product_ref[...], down_rows(jnp.maximum(step - 1, 0)), NN)
    grad[...] += dot(d_left, stacked(weights[:8]), NT) + dot(d_right, stacked(weights[8:]), NT)

    grad_product = dot(c_ref[...], down_rows(jnp.minimum(step, last)), NT)
    held_l[...] = (grad_product * right_ref[...].astype(F32)).astype(BF16)
    held_r[...] = (grad_product * left_ref[...].astype(F32)).astype(BF16)

    @pl.when(step == 0)
    def _():
        grad[...] = jnp.zeros_like(grad)
        total[...] = jnp.zeros_like(total)

    @pl.when(step == pl.num_programs(0) - 1)
    def _():
        mid = mid_ref[...]
        act_ref[...] = (mid + total[...]).astype(BF16)
        restored(order, grad[...], total)
        g = total[...]
        scale = lax.rsqrt(jnp.mean(mid * mid, axis=-1, keepdims=True) + EPS)
        inner = jnp.mean(g * mid, axis=-1, keepdims=True) * (scale * scale * scale)
        d_mid = c_ref[...].astype(F32) + scale * g - mid * inner
        d_mid_ref[...] = d_mid
        d_branch_ref[...] = d_mid.astype(BF16)


def gate_out_back_body(order, d_ref, mix_ref, u_ref, *refs):
    du_ref, dm_ref, held = refs[8:]
    restored(order, dot(d_ref[...], stacked(refs[:8]), NT), held)
    dg = held[...]
    mix = mix_ref[...].astype(F32)
    u = u_ref[...]
    sig = sigmoid(u)
    scale = lax.rsqrt(jnp.mean(mix * mix, axis=-1, keepdims=True) + EPS)
    du_ref[...] = (dg * mix * scale * (sig * (1.0 + u * (1.0 - sig)))).astype(BF16)
    dn = dg * (u * sig)
    inner = jnp.mean(dn * mix, axis=-1, keepdims=True) * (scale * scale * scale)
    dm_ref[...] = (scale * dn - mix * inner).astype(BF16)


def in_back_body(order, x_ref, d_mid_ref, du_ref, d_ref, *refs):
    low, high, gates, (out, grad, held) = refs[:8], refs[8:16], refs[16:24], refs[24:]
    step = pl.program_id(0)

    @pl.when(step == 0)
    def _():
        grad[...] = dot(du_ref[...], stacked(gates), NT)

    grad[...] += dot(d_ref[0, 0], stacked(low), NT) + dot(d_ref[1, 0], stacked(high), NT)

    @pl.when(step == pl.num_programs(0) - 1)
    def _():
        restored(order, grad[...], held)
        g = held[...]
        x = x_ref[...].astype(F32)
        scale = lax.rsqrt(jnp.mean(x * x, axis=-1, keepdims=True) + EPS)
        inner = jnp.mean(g * x, axis=-1, keepdims=True) * (scale * scale * scale)
        out[...] = (d_mid_ref[...] + scale * g - x * inner).astype(BF16)


def weight_grads_body(order, hx_ref, hy_ref, gx_ref, gy_ref, d_ref, du, db, *outs):
    held, sems = outs[4:8], outs[8]
    step = pl.program_id(0)
    half = hx_ref.shape[1] // 2

    def copies(side):
        return [
            pltpu.make_async_copy(held[2 * side + i], outs[2 * side + i], sems.at[2 * side + i])
            for i in range(2)
        ]

    def run(side, h, gated):
        keep, send = held[2 * side], held[2 * side + 1]
        terms = [(h, d_ref.at[0, i]) for i in range(3)] + [(h, du), (gated, db)]
        for i, (lhs, d) in enumerate(terms):
            g = dot(lhs[...], d[...], TN, BF16)
            cols = slice(i * g.shape[1], (i + 1) * g.shape[1])
            keep[:, cols] = g[:half]
            send[:, cols] = g[half:]
        for copy in copies(side):
            copy.start()

    @pl.when(step == 0)
    def _():
        run(0, hx_ref, gx_ref)

    @pl.when(step == 1)
    def _():
        run(1, hy_ref, gy_ref)
        for copy in copies(0) + copies(1):
            copy.wait()


class Chain:
    def __init__(self, fresh, factor, forward, parts):
        self.fresh, self.factor, self.forward, self.parts = fresh, factor, forward, parts
        self.seqs = fresh.shape[0]
        self.now = [fresh[s] for s in range(self.seqs)]
        self.got = [[] for _ in range(self.seqs)]
        self.turns = self.seqs + parts - 2

    def pass_on(self, s, hop):
        pair = (hop - 1, hop) if self.forward else (self.parts - hop, self.parts - hop - 1)
        self.got[s].append(lax.ppermute(self.now[s], "heads", [pair]))

    def begin(self):
        for s in range(self.seqs):
            self.pass_on(s, 1)

    def at(self, turn):
        return [(s, turn - s) for s in range(self.seqs) if 1 <= turn - s < self.parts]

    def arrivals(self, turn):
        self.new = [self.got[s][hop - 1] for s, hop in self.at(turn)]
        return self, "new"

    def go_on(self, turn):
        for (s, hop), new in zip(self.at(turn), self.new):
            self.got[s][hop - 1] = new
            if hop + 1 < self.parts:
                arrived = new.astype(F32) * self.factor[s][:, None, None]
                self.now[s] = (self.fresh[s].astype(F32) + arrived).astype(BF16)
                self.pass_on(s, hop + 1)

    def result(self):
        return jnp.stack([functools.reduce(lambda a, b: a + b, g) for g in self.got])


class Layer:
    def __init__(self, tokens, doc_lengths, cotangent):
        seqs, length, width = tokens.shape
        self.seqs, self.length, self.width, self.count = seqs, length, width, seqs * length
        self.here = lax.axis_index("rows")
        self.place = lax.axis_index("heads")
        self.order = places(self.here, self.place)
        self.x = tokens.reshape(self.count, width)
        self.dy = cotangent.reshape(self.count, width)

        ends = jnp.cumsum(doc_lengths, axis=-1, dtype=jnp.int32)[:, :-1]

        def ids_at(where):
            return jnp.sum((where[None, :, None] >= ends[:, None, :]).astype(jnp.int32), axis=-1)

        start = self.place * length
        positions = start + jnp.arange(length, dtype=jnp.int32)
        ids = ids_at(positions)
        before = jnp.where(self.place > 0, ids_at(jnp.reshape(start - 1, (1,))), -1)
        final = ids[:, -1:]
        link = (ids == before).astype(F32)[:, :, None]
        tail = (ids == final).astype(F32)[:, :, None]
        slopes = jnp.array([slope_of(h) for h in range(HEADS)], F32)
        self.factor = (final == before).astype(F32) * jnp.exp(-slopes * length)[None, :]
        theta = jnp.exp(-math.log(10000.0) * jnp.arange(HEAD_DIM, dtype=F32) / HEAD_DIM)
        angle = positions.astype(F32)[:, None] * theta[None, :]

        table = pl.BlockSpec((length, HEAD_DIM), lambda s, *_: (0, 0))
        one_col = pl.BlockSpec((1, length, 1), lambda s, *_: (s, 0, 0))
        one_row = pl.BlockSpec((1, 1, length), lambda s, *_: (s, 0, 0))
        self.turn = [(jnp.cos(angle), table), (jnp.sin(angle), table)]
        self.link = link, one_col
        self.tail = tail, one_col
        self.masks = [(ids[:, :, None], one_col), (ids[:, None, :], one_row), self.link]
        self.seq = pl.BlockSpec((1, length, width), lambda s, *_: (s, 0, 0))
        self.state = pl.BlockSpec(
            (1, HEADS, 2 * HEAD_DIM, HEAD_DIM), lambda s, *_: (s, 0, 0, 0)
        )
        self.states = (seqs, HEADS, 2 * HEAD_DIM, HEAD_DIM), BF16, self.state
        step = min(self.count, 256)
        self.grid = (self.count // step,)
        self.wide = rows_spec(step, width)

    def rows(self, body, ins, types, order=None):
        return call(
            body, self.grid, self.order, [(a, self.wide) for a in ins],
            [((self.count, self.width), t, self.wide) for t in types],
        )

    def seqwise(self, body, ins, outs):
        shape = (self.seqs, self.length, self.width)
        ins = [i if isinstance(i, tuple) else (i.reshape(shape), self.seq) for i in ins]
        outs = [o if isinstance(o, tuple) else (shape, o, self.seq) for o in outs]
        got = call(body, (self.seqs,), self.order, ins, outs)
        return [g.reshape(self.count, self.width) if g.shape == shape else g for g in got]

    def norm(self):
        return self.rows(norm_body, [self.x], [BF16])

    def fresh(self, k_pre, v_pre):
        return self.seqwise(fresh_body, [k_pre, v_pre] + self.turn + [self.tail], [self.states])[0]

    def mix(self, q_pre, k_pre, v_pre, u_pre, state_in):
        ins = [q_pre, k_pre, v_pre, u_pre] + self.turn + self.masks + [(state_in, self.state)]
        return self.seqwise(mix_body, ins, [BF16, BF16])

    def mid(self, branch):
        return self.rows(mid_body, [self.x, branch], [F32, BF16])

    def mid_back(self, x_mid, grad):
        return self.rows(norm_back_body, [x_mid, self.dy, grad], [F32, BF16])

    def in_back(self, d_mid, grad):
        return self.rows(norm_back_body, [self.x, d_mid, grad], [F32])[0]

    def gate_back(self, q_pre, u_pre, mix, d_gated):
        ins = [q_pre, u_pre, mix, d_gated] + self.turn + [self.link]
        return self.seqwise(gate_back_body, ins, [BF16, BF16, self.states])

    def mix_back(self, q_pre, k_pre, v_pre, d_mix, state_in):
        ins = [q_pre, k_pre, v_pre, d_mix] + self.turn + self.masks + [(state_in, self.state)]
        return self.seqwise(mix_back_body, ins, [BF16, F32, F32])

    def state_back(self, k_pre, v_pre, dk_near, dv_near, d_state):
        ins = [k_pre, v_pre, dk_near, dv_near] + self.turn + [self.tail, (d_state, self.state)]
        return self.seqwise(state_back_body, ins, [BF16, BF16])


def plainly(layer, heads_count, weights):
    w_query, w_key, w_value, w_gate, w_out, w_left, w_right, w_down = (
        lax.all_gather(w, "rows", axis=0, tiled=True) for w in weights
    )

    def carried(fresh, forward):
        chain = Chain(fresh, layer.factor, forward, heads_count)
        chain.begin()
        for turn in range(1, chain.turns + 1):
            chain.arrivals(turn)
            chain.go_on(turn)
        return chain.result()

    def gradient(lhs, d):
        total = lax.psum_scatter(dot(lhs, d, TN, BF16), "rows", scatter_dimension=0, tiled=True)
        return lax.psum_scatter(total, "heads", scatter_dimension=1, tiled=True).astype(F32)

    (h_in,) = layer.norm()
    q_pre, k_pre, v_pre, u_pre = (
        dot(h_in, w, NN) for w in (w_query, w_key, w_value, w_gate)
    )
    state_in = carried(layer.fresh(k_pre, v_pre), True)
    mix, gated = layer.mix(q_pre, k_pre, v_pre, u_pre, state_in)
    x_mid, h_mid = layer.mid(dot(gated, w_out, NN))
    left, right = dot(h_mid, w_left, NN), dot(h_mid, w_right, NN)
    product = (left * right).astype(BF16)
    activations = (x_mid + dot(product, w_down, NN)).astype(BF16)
    grad_product = dot(layer.dy, w_down, NT)
    d_left = (grad_product * right).astype(BF16)
    d_right = (grad_product * left).astype(BF16)
    d_mid, d_branch = layer.mid_back(
        x_mid, dot(d_left, w_left, NT) + dot(d_right, w_right, NT)
    )
    d_u, d_mix, d_fresh = layer.gate_back(q_pre, u_pre, mix, dot(d_branch, w_out, NT))
    d_state = carried(d_fresh, False)
    d_q, dk_near, dv_near = layer.mix_back(q_pre, k_pre, v_pre, d_mix, state_in)
    d_k, d_v = layer.state_back(k_pre, v_pre, dk_near, dv_near, d_state)
    grad_in = (
        dot(d_q, w_query, NT) + dot(d_u, w_gate, NT) + dot(d_k, w_key, NT) + dot(d_v, w_value, NT)
    )
    input_grad = layer.in_back(d_mid, grad_in)
    pairs = (
        (h_in, d_q), (h_in, d_k), (h_in, d_v), (h_in, d_u), (gated, d_branch),
        (h_mid, d_left), (h_mid, d_right), (product, layer.dy),
    )
    return (activations, input_grad) + tuple(gradient(lhs, d) for lhs, d in pairs)


class Row:
    def __init__(self, doc_lengths, length, width, here, head):
        self.length, self.width = length, width
        self.order = places(here, head)
        lengths = lax.dynamic_index_in_dim(doc_lengths, head, 0, keepdims=False)
        ends = jnp.cumsum(lengths, dtype=jnp.int32)[:-1]
        positions = jnp.arange(length, dtype=jnp.int32)
        ids = jnp.sum((positions[:, None] >= ends[None, :]).astype(jnp.int32), axis=-1)
        theta = jnp.exp(-math.log(10000.0) * jnp.arange(HEAD_DIM, dtype=F32) / HEAD_DIM)
        angle = positions.astype(F32)[:, None] * theta[None, :]

        def whole(rows, cols):
            return pl.BlockSpec((rows, cols), lambda *_: (0, 0))

        table = whole(length, HEAD_DIM)
        self.extra = [
            (jnp.cos(angle), table), (jnp.sin(angle), table),
            (ids[:, None], whole(length, 1)), (ids[None, :], whole(1, length)),
        ]
        self.heads = pl.BlockSpec((length, 2 * HEAD_DIM), lambda h, *_: (0, h))
        self.wide = rows_spec(min(length, 256), width)
        self.all = whole(length, width)
        self.block = math.gcd(length, 256)
        self.flops = 2 * length * width * width

    def norm(self, x):
        return self.by_rows(row_norm_body, [(x, self.wide)], [], [BF16, BF16], [BF16])

    def pieces(self, group, half, width=None):
        rows, whole = group.pieces[half].shape
        spec = pl.BlockSpec((rows, width or whole), lambda i, *_: (0, i if width else 0))
        return [(a, spec) for a in group.all(half)]

    def thirds(self, which=None, dtype=F32):
        half = self.width // 2
        if which is None:
            return pl.BlockSpec((2, self.length, half), lambda i, *_: (0, 0, i))
        pair = 2 * HEAD_DIM
        each = half // pair
        return pl.BlockSpec(
            (1, self.length, pair), lambda i, *_: (i // each, 0, which * each + i % each)
        )

    def project(self, h, qkv):
        half = self.width // 2
        return call(
            project_body, (3,), self.order,
            [(h, self.all)] + self.pieces(qkv, 0, half) + self.pieces(qkv, 1, half),
            [((2, self.length, 3 * half), F32, self.thirds())], flops=3 * self.flops,
        )[0]

    def column(self, block, offset=0):
        return pl.BlockSpec((self.length, block), lambda i, *_: (0, offset + i))

    def mix(self, pre):
        return call(
            functools.partial(row_mix_body, self.block), (HEADS // 2,), self.order,
            [(pre, self.thirds(i)) for i in range(3)] + self.extra,
            [((self.length, self.width), BF16, self.heads)], flops=self.flops * 3 // 8,
        )[0]

    def mix_back(self, pre, d_mix):
        pair, half = 2 * HEAD_DIM, self.width // 2
        each = half // pair
        spec = pl.BlockSpec((1, 3, self.length, pair), lambda i, *_: (i // each, 0, 0, i % each))
        return call(
            functools.partial(row_mix_back_body, self.block), (HEADS // 2,), self.order,
            [(pre, self.thirds(i)) for i in range(3)] + [(d_mix, self.heads)] + self.extra,
            [((2, 3, self.length, half), BF16, spec)], flops=self.flops,
        )[0]

    def by_rows(self, body, ins, weights, types, scratch):
        step = self.wide.block_shape[0]
        return call(
            body, (self.length // step,), self.order, ins + weights,
            [((self.length, self.width), t, self.wide) for t in types],
            scratch=[pltpu.VMEM((step, self.width), t) for t in scratch], flops=self.flops,
        )

    def out_mid(self, mix, h, x, uo):
        return self.by_rows(
            out_mid_body, [(mix, self.wide), (h, self.wide), (x, self.wide)],
            self.pieces(uo, 0) + self.pieces(uo, 1),
            [F32, BF16, BF16, F32, BF16, BF16], [BF16],
        )

    def gate_out_back(self, d_branch, mix, u_pre, uo):
        return self.by_rows(
            gate_out_back_body, [(d_branch, self.wide), (mix, self.wide), (u_pre, self.wide)],
            self.pieces(uo, 1), [BF16, BF16], [F32],
        )

    def left_right(self, h, ff):
        inner = ff.pieces[0].shape[1]
        block = math.gcd(inner, 1408)
        return call(
            left_right_body, (inner // block,), self.order,
            [(h, self.all)] + self.pieces(ff, 0, block) + self.pieces(ff, 1, block),
            [((self.length, inner), BF16, self.column(block))] * 3,
            flops=2 * self.flops * inner // self.width,
        )

    def down_grad(self, product, c):
        inner, half = product.shape[1], self.width // 2
        block = math.gcd(inner, 1408)
        rows = inner // 8
        got = call(
            functools.partial(down_grad_body, rows), (inner // block,), self.order,
            [(product, self.column(block)), (c, self.all)], [((4 * rows, half), BF16, HBM)] * 4,
            scratch=[pltpu.VMEM((inner, self.width), BF16), pltpu.SemaphoreType.DMA((2, 8))],
            flops=self.flops * inner // self.width,
        )
        return Reduce(self.order, got[2:], got[:2], [2, 4])

    def feed_back(self, left, right, product, h_x, h_y, c, x_mid, ff, down):
        inner, rows = ff.pieces[0].shape[1], down.pieces[0].shape[0]
        block = math.gcd(inner, 256)
        steps = inner // block

        def now(rows):
            return pl.BlockSpec((rows, block), lambda i, *_: (0, jnp.minimum(i, steps - 1)))

        def before(rows):
            return pl.BlockSpec((rows, block), lambda i, *_: (0, jnp.maximum(i - 1, 0)))

        full = (self.length, self.width)
        weights = [
            (a, before(ff.pieces[0].shape[0])) for a in ff.all(0) + ff.all(1)
        ]
        return call(
            functools.partial(feed_back_body, rows), (steps + 1,), self.order,
            [(left, now(self.length)), (right, now(self.length)), (product, before(self.length))]
            + [(a, self.all) for a in (h_x, h_y, c, x_mid)]
            + weights + [(a, HBM) for a in down.all(0) + down.all(1)],
            [((self.width // 2, inner), BF16, before(self.width // 2))] * 4
            + [(full, F32, self.all), (full, BF16, self.all), (full, BF16, self.all)],
            scratch=[pltpu.VMEM((inner, self.width), BF16)] + [pltpu.VMEM(full, F32)] * 2
            + [pltpu.VMEM((self.length, block), BF16)] * 2 + [pltpu.SemaphoreType.DMA((2, 8))],
            flops=6 * self.flops * inner // self.width,
        )

    def in_back(self, x, d_mid, d, d_u, qkv, uo):
        half = self.width // 2
        full = (self.length, self.width)
        third = pl.BlockSpec((2, 1, self.length, half), lambda i, *_: (0, i, 0, 0))
        return call(
            in_back_body, (3,), self.order,
            [(x, self.all), (d_mid, self.all), (d_u, self.all), (d, third)]
            + self.pieces(qkv, 0, half) + self.pieces(qkv, 1, half) + self.pieces(uo, 0),
            [(full, BF16, self.all)], scratch=[pltpu.VMEM(full, F32)] * 2, flops=4 * self.flops,
        )[0]

    def weight_grads(self, h_x, h_y, gated_x, gated_y, d, d_u, d_branch):
        half = self.width // 2
        shape = (half, 5 * half)
        thirds = pl.BlockSpec((1, 3, self.length, half), lambda i, *_: (i, 0, 0, 0))
        got = call(
            weight_grads_body, (2,), self.order,
            [(a, self.all) for a in (h_x, h_y, gated_x, gated_y)]
            + [(d, thirds), (d_u, self.column(half)), (d_branch, self.column(half))],
            [(shape, BF16, HBM)] * 4,
            scratch=[pltpu.VMEM(shape, BF16)] * 4 + [pltpu.SemaphoreType.DMA((4,))],
            flops=5 * self.flops,
        )
        return Reduce(self.order, got[1::2], got[::2], [2, 4])


def stepwise(tokens, doc_lengths, cotangent, weights):
    w_query, w_key, w_value, w_gate, w_out, w_left, w_right, w_down = weights
    size, width = tokens.shape[1:]
    length, half = 4 * size, width // 2
    here, head = lax.axis_index("rows"), lax.axis_index("heads")
    row = Row(doc_lengths, length, width, here, head)
    order = row.order
    v = types.SimpleNamespace()
    clock = Clock(order)
    tick = clock.tick

    def exchanged(a):
        return lax.all_to_all(a.reshape(4, size, width), "heads", 0, 0, tiled=True)

    def whole_row(a):
        return exchanged(a).reshape(length, width)

    inner = w_left.shape[1]
    uo = Gather([w_gate, w_out])
    uo.first()
    qkv = Gather(
        pack(order, [w_query, w_key, w_value], [[(i, at, half) for i in range(3)] for at in (0, half)])
    )
    qkv.first()
    v.x = whole_row(tokens)
    v.extra = [a for a, _ in row.extra]
    ff = Gather([w_left, w_right])
    v.c = cotangent
    tick((v, "x"), (qkv, "near_x"), (qkv, "near_y"), (uo, "near_x"), (uo, "near_y"), (uo, "pieces"), (v, "c"), (v, "extra"))
    row.extra = [(a, spec) for a, (_, spec) in zip(v.extra, row.extra)]
    qkv.second()
    uo.second()
    qkv.cross("pieces", "near_x", "near_y")
    uo.cross("pieces", "near_x", "near_y")
    v.h = row.norm(v.x)
    tick((qkv, "far"), (uo, "far"), (v, "h"), (ff, "pieces"))
    ff.first()
    ff.cross("pieces")
    qkv.cross("far")
    uo.cross("far")
    v.pre = row.project(v.h[0], qkv)
    v.mix = row.mix(v.pre)
    v.u_pre, v.gated, v.gated_x, v.x_mid, *v.h_mid = row.out_mid(v.mix, v.h[0], v.x, uo)
    v.down = w_down
    tick((v, "x_mid"), (v, "h_mid"), (ff, "near_x"), (ff, "near_y"), (v, "down"), (v, "c"))
    ff.second()
    v.c = whole_row(v.c)
    ff.cross("near_x", "near_y")
    v.down = pack(order, [v.down], [[(0, 0, half)], [(0, half, half)]])
    tick((ff, "far"), (v, "down"))
    down = Gather(v.down)
    ff.cross("far")
    down.first()
    down.cross("pieces")
    h_y, h_x = v.h_mid

    v.left, v.right, v.product = row.left_right(h_y, ff)
    tick((v, "left"), (v, "right"), (v, "product"), (down, "near_x"), (down, "near_y"), (v, "c"))
    down.second()
    down.cross("near_x", "near_y")
    v.g_down = dot(v.product, v.c, TN, BF16)
    tick((v, "g_down"), (down, "far"), (v, "left"))
    v.sum_down = lax.psum_scatter(v.g_down, "rows", scatter_dimension=0, tiled=True)
    down.cross("far")
    tick((down, "far_other"), (v, "left"))
    keep_l, send_l, keep_r, send_r, v.d_mid, v.d_branch, v.act = row.feed_back(
        v.left, v.right, v.product, h_x, h_y, v.c, v.x_mid, ff, down
    )
    r_ff = Reduce(order, [send_l, send_r], [keep_l, keep_r], [2, 4])
    tick((r_ff, "sends"), (v, "d_mid"), (v, "d_branch"), (v, "act"))
    r_ff.core()
    v.d_u, v.d_mix = row.gate_out_back(v.d_branch, v.mix, v.u_pre, uo)
    tick((r_ff, "theirs"), (v, "d_u"), (v, "d_mix"))
    r_ff.join()
    tick((r_ff, "totals"), (v, "act"), (v, "d_mix"))
    r_ff.first()
    v.act = exchanged(v.act)
    v.d = row.mix_back(v.pre, v.d_mix)
    tick((v, "d"), (v, "sum_down"))
    s_down = Settle(order, [v.sum_down], None, half // 2, [lambda z: z * (half // 2)])
    tick((v, "d"), (s_down, "out"))
    s_down.pass_on(1)
    r_att = row.weight_grads(v.h[1], v.h[0], v.gated_x, v.gated, v.d, v.d_u, v.d_branch)
    tick((r_att, "sends"), (r_ff, "got"), (v, "act"), (v, "d"))
    r_att.core()
    r_ff.join_first()
    tick((r_att, "theirs"), (r_ff, "parts"), (v, "d"), (s_down, "got"))
    r_ff.second()
    s_down.join()
    tick((s_down, "out"), (r_att, "theirs"), (v, "d"))
    s_down.pass_on(2)
    r_att.join()
    v.back = row.in_back(v.x, v.d_mid, v.d, v.d_u, qkv, uo)
    tick((r_att, "totals"), (r_ff, "got_last"), (r_ff, "own"), (v, "back"), (s_down, "got"))
    r_att.first()
    v.back = exchanged(v.back)
    quarter = inner // 4
    s_ff = r_ff.settle(quarter, [lambda z: z * quarter, lambda z: inner + z * quarter])
    tick((s_ff, "out"))
    s_ff.pass_on(1)
    (v.g_down,) = s_down.result()
    tick((r_att, "got"), (v, "g_down"))
    r_att.join_first()
    tick((r_att, "parts"), (s_ff, "got"), (v, "back"))
    r_att.second()
    s_ff.join()
    v.back = v.back.astype(F32)
    tick((s_ff, "out"), (v, "back"))
    s_ff.pass_on(2)
    tick((r_att, "got_last"), (r_att, "own"))
    s_att = r_att.settle(
        half // 2,
        [
            lambda z, i=i: (z // 2) * 5 * half + i * half + (z % 2) * (half // 2)
            for i in range(5)
        ],
    )
    tick((s_att, "out"), (s_ff, "got"))
    s_att.pass_on(1)
    v.g_ff = s_ff.result()
    tick((s_att, "got"), (v, "g_ff"))
    s_att.join()
    tick((s_att, "out"))
    s_att.pass_on(2)
    g_query, g_key, g_value, g_gate, g_out = s_att.result()
    g_left, g_right = v.g_ff
    return (
        v.act, v.back, g_query, g_key, g_value, g_gate, g_out, g_left, g_right, v.g_down
    )


def on_device(rows_count, heads_count, tokens, doc_lengths, cotangent, *weights):
    if rows_count == 8 and heads_count == 4 and tokens.shape[0] == 4:
        return stepwise(tokens, doc_lengths, cotangent, weights)
    layer = Layer(tokens, doc_lengths, cotangent)
    activations, input_grad, *grads = plainly(layer, heads_count, weights)
    return (activations.reshape(tokens.shape), input_grad.reshape(tokens.shape), *grads)


def solution(mesh):
    sizes = dict(mesh.shape)
    tokens = P("rows", "heads", None)
    weights = P("rows", None)
    grads = P("rows", "heads")
    return jax.shard_map(
        functools.partial(on_device, sizes["rows"], sizes["heads"]),
        mesh=mesh,
        in_specs=(tokens, weights, tokens) + (weights,) * 8,
        out_specs=(tokens, tokens) + (grads,) * 8,
        check_vma=False,
    )
```

```python
import functools
import math
import types

import jax
import jax.numpy as jnp
from jax import lax
from jax.experimental import pallas as pl
from jax.experimental.pallas import tpu as pltpu
from jax.sharding import PartitionSpec as P

HEADS = 8
HEAD_DIM = 128
EPS = 1e-06
F32 = jnp.float32
BF16 = jnp.bfloat16
VMEM_LIMIT = 60 << 20

BITS = (0, 2, 4, 6, 1, 3, 5, 7)
BITS_X = (0, 4, 2, 6, 1, 5, 3, 7)
BITS_Y = (0, 2, 4, 6, 1, 3, 5, 7)


def after(value, *others):
    return lax.optimization_barrier((value,) + others)[0]


def dot(a, b, dims, out=F32):
    return lax.dot_general(a, b, (dims, ((), ())), preferred_element_type=F32).astype(out)


NN = ((1,), (0,))
NT = ((1,), (1,))
TN = ((0,), (0,))


def swap(value, bit, size):
    return lax.ppermute(value, "rows", [(i, i ^ bit) for i in range(size)])


def swap_heads(value, bit):
    return lax.ppermute(value, "heads", [(i, i ^ bit) for i in range(4)])


HBM = pl.BlockSpec(memory_space=pltpu.HBM)


def whole_spec(rows, width):
    return pl.BlockSpec((rows, width), lambda i, *_: (0, 0))


def run_copies(copies):
    for copy in copies:
        copy.start()
    for copy in copies:
        copy.wait()


def pack(order, arrays, lists):
    rows = arrays[0].shape[0]
    widths = [sum(w for _, _, w in parts) for parts in lists]
    most = max(len(parts) for parts in lists)

    def body(order, *refs):
        ins, outs, sems = refs[: len(arrays)], refs[len(arrays) : -1], refs[-1]
        copies = []
        for j, parts in enumerate(lists):
            at = 0
            for i, (which, begin, width) in enumerate(parts):
                copies.append(
                    pltpu.make_async_copy(
                        ins[which].at[:, begin : begin + width],
                        outs[j].at[:, at : at + width],
                        sems.at[j, i],
                    )
                )
                at += width
        run_copies(copies)

    return call(
        body, (1,), order, [(a, HBM) for a in arrays],
        [((rows, w), BF16, whole_spec(rows, w)) for w in widths],
        scratch=[pltpu.SemaphoreType.DMA((len(lists), most))],
    )


class Clock:
    def __init__(self, start):
        self.token = start

    def tick(self, *places):
        held = [getattr(o, n) for o, n in places]
        held, self.token = lax.optimization_barrier((held, self.token))
        for (o, n), value in zip(places, held):
            setattr(o, n, value)


def places(here, head):
    return jnp.stack([here ^ b for b in range(8)] + [head ^ b for b in range(4)]).astype(jnp.int32)


class Gather:
    def __init__(self, pieces):
        self.pieces = list(pieces)
        self.near_x, self.near_y = [None, None], [None, None]

    def first(self, *halves):
        for half in halves or (0, 1):
            self.near_x[half] = swap(self.pieces[half], 2, 8)
            self.near_y[half] = swap(self.pieces[half], 4, 8)

    def second(self):
        self.far = [swap(self.near_x[0], 4, 8), swap(self.near_y[1], 2, 8)]

    def cross(self, *names):
        for name in names:
            setattr(self, name + "_other", [swap(p, 1, 8) for p in getattr(self, name)])

    def all(self, half):
        names = ("pieces", "near_x", "near_y", "far")
        return [getattr(self, n + core)[half] for core in ("", "_other") for n in names]


def added(*terms):
    return functools.reduce(lambda a, b: a + b, [t.astype(F32) for t in terms]).astype(BF16)


class Reduce:
    def __init__(self, order, sends, keeps, bits):
        self.order, self.sends, self.keeps, self.bits = order, list(sends), list(keeps), list(bits)

    def core(self):
        self.theirs = [swap(s, 1, 8) for s in self.sends]

    def join(self):
        half = self.keeps[0].shape[0] // 2
        self.totals = [added(k[half:], t[half:]) for k, t in zip(self.keeps, self.theirs)]

    def first(self):
        self.got = [swap(t, b, 8) for t, b in zip(self.totals, self.bits)]

    def join_first(self):
        rows = self.keeps[0].shape[0] // 4
        terms = list(zip(self.keeps, self.theirs, self.got))
        self.parts = [added(*(a[rows : 2 * rows] for a in t)) for t in terms]
        self.own = [list(t) for t in terms]

    def second(self):
        self.got_last = [swap(p, 6 - b, 8) for p, b in zip(self.parts, self.bits)]

    def settle(self, block, starts):
        return Settle(self.order, [t + [g] for t, g in zip(self.own, self.got_last)], block, starts)


class Settle:
    def __init__(self, order, parts, block, starts):
        self.order, self.block, self.count = order, block, len(starts)
        rows = self.rows = parts[0][-1].shape[0]
        widths = [p[-1].shape[1] for p in parts]
        counts = [len(p) for p in parts]

        def body(order, *refs):
            own, out, held = refs[sum(counts) :]
            at, first = 0, 0
            for width, count in zip(widths, counts):
                total = refs[first][...].astype(F32)
                for ref in refs[first + 1 : first + count]:
                    total += ref[...].astype(F32)
                held[:, at : at + width] = total
                at, first = at + width, first + count
            for z in range(4):

                @pl.when(order[8] == z)
                def _(z=z):
                    for i, start in enumerate(starts):
                        for j in range(2):
                            mine, theirs = start(z ^ (2 * j)), start(z ^ (2 * j + 1))
                            own[2 * i + j] = held[:, mine : mine + block]
                            out[2 * i + j] = held[:, theirs : theirs + block].astype(BF16)

        self.own, self.out = call(
            body, (2,), order,
            [(a, pl.BlockSpec((rows // 2, a.shape[1]), lambda i, *_: (i, 0))) for p in parts for a in p],
            [self.entry(2 * self.count, F32, 2), self.entry(2 * self.count, BF16, 2)],
            scratch=[pltpu.VMEM((rows // 2, sum(widths)), F32)],
        )

    def entry(self, count, dtype, steps=1):
        shape = (count, self.rows, self.block)
        spec = pl.BlockSpec((count, self.rows // steps, self.block), lambda i, *_: (0, i, 0))
        return shape, dtype, spec

    def given(self):
        return [(a, pl.BlockSpec(a.shape, lambda *_: (0, 0, 0))) for a in (self.own, self.got)]

    def pass_on(self, bit):
        self.got = lax.ppermute(self.out, "heads", [(i, i ^ bit) for i in range(4)])

    def join(self):
        count = self.count

        def body(order, own_ref, got_ref, mine, out):
            for i in range(count):
                mine[i] = own_ref[2 * i] + got_ref[2 * i].astype(F32)
                out[i] = (own_ref[2 * i + 1] + got_ref[2 * i + 1].astype(F32)).astype(BF16)

        self.own, self.out = call(
            body, (1,), self.order, self.given(), [self.entry(count, F32), self.entry(count, BF16)]
        )

    def result(self):
        return [self.own[i] + self.got[i].astype(F32) for i in range(self.count)]


def at_block(order_ref, index, width):
    return pl.ds(pl.multiple_of(order_ref[index] * width, width), width)


def sigmoid(v):
    return 1.0 / (1.0 + jnp.exp(-v))


def swish_slope(v):
    sig = sigmoid(v)
    return sig * (1.0 + v * (1.0 - sig))


def call(body, grid, order, ins, outs, scratch=(), flops=0):
    moved = sum(a.size * a.dtype.itemsize for a, _ in ins) + sum(
        math.prod(s) * jnp.dtype(t).itemsize for s, t, _ in outs
    )
    return pl.pallas_call(
        body,
        grid_spec=pltpu.PrefetchScalarGridSpec(
            num_scalar_prefetch=1,
            grid=grid,
            in_specs=[spec for _, spec in ins],
            out_specs=[spec for _, _, spec in outs],
            scratch_shapes=list(scratch),
        ),
        out_shape=[jax.ShapeDtypeStruct(s, t) for s, t, _ in outs],
        compiler_params=pltpu.CompilerParams(vmem_limit_bytes=VMEM_LIMIT),
        cost_estimate=pl.CostEstimate(flops=flops // 4, bytes_accessed=moved // 4, transcendentals=0),
    )(order, *[a for a, _ in ins])


def rows_spec(count, width, column=0):
    return pl.BlockSpec((count, width), lambda i, *_: (i, column))


def norm_body(order, x_ref, h_ref):
    x = x_ref[...].astype(F32)
    scale = lax.rsqrt(jnp.mean(x * x, axis=-1, keepdims=True) + EPS)
    h_ref[...] = (x * scale).astype(BF16)


def mid_body(order, x_ref, b_ref, mid_ref, h_ref):
    mid = x_ref[...].astype(F32) + b_ref[...]
    mid_ref[...] = mid
    scale = lax.rsqrt(jnp.mean(mid * mid, axis=-1, keepdims=True) + EPS)
    h_ref[...] = (mid * scale).astype(BF16)


def norm_back_body(order, v_ref, base_ref, g_ref, *outs):
    v = v_ref[...].astype(F32)
    g = g_ref[...]
    scale = lax.rsqrt(jnp.mean(v * v, axis=-1, keepdims=True) + EPS)
    inner = jnp.mean(g * v, axis=-1, keepdims=True) * (scale * scale * scale)
    total = base_ref[...].astype(F32) + scale * g - v * inner
    outs[0][...] = total
    if len(outs) > 1:
        outs[1][...] = total.astype(BF16)


def ramp(rows, start, sign, slope):
    place = lax.broadcasted_iota(jnp.int32, (rows, HEAD_DIM), 0).astype(F32)
    return jnp.exp(-slope * (start + sign * place))


def decays(ids_col, ids_row, slope):
    rows = ids_col.shape[0]
    gap = (
        lax.broadcasted_iota(jnp.int32, (rows, rows), 0)
        - lax.broadcasted_iota(jnp.int32, (rows, rows), 1)
    ).astype(F32)
    keep = (gap >= 0.0) & (ids_col == ids_row)
    return jnp.where(keep, jnp.exp(-slope * jnp.maximum(gap, 0.0)), 0.0)


def slope_of(head):
    return 2.0 ** (-8.0 * (head + 1) / HEADS)


def columns(head):
    return slice(head * HEAD_DIM, (head + 1) * HEAD_DIM)


def turned(a, cos, sin):
    return jnp.concatenate([a * cos, a * sin], axis=1)


def rounded_swish(v):
    return (v * sigmoid(v)).astype(BF16).astype(F32)


def fresh_body(order, k_ref, v_ref, cos_ref, sin_ref, tail_ref, state_ref):
    rows = k_ref.shape[1]
    cos, sin = cos_ref[...], sin_ref[...]
    tail = tail_ref[0]
    for head in range(HEADS):
        key = rounded_swish(k_ref[0, :, columns(head)])
        key = key * (ramp(rows, rows - 1.0, -1.0, slope_of(head)) * tail)
        value = v_ref[0, :, columns(head)].astype(BF16)
        state_ref[0, head] = dot(turned(key, cos, sin).astype(BF16), value, TN, BF16)


def mix_body(
    order, q_ref, k_ref, v_ref, u_ref, cos_ref, sin_ref, col_ref, row_ref, link_ref, s_ref,
    mix_ref, gated_ref,
):
    rows = q_ref.shape[1]
    cos, sin = cos_ref[...], sin_ref[...]
    ids_col, ids_row = col_ref[0], row_ref[0]
    link = link_ref[0]
    power = jnp.zeros((rows, 1), F32)
    for head in range(HEADS):
        cols = columns(head)
        slope = slope_of(head)
        rq = turned(rounded_swish(q_ref[0, :, cols]), cos, sin).astype(BF16)
        rk = turned(rounded_swish(k_ref[0, :, cols]), cos, sin).astype(BF16)
        value = v_ref[0, :, cols].astype(BF16)
        weights = (dot(rq, rk, NT) * decays(ids_col, ids_row, slope)).astype(BF16)
        mixed = dot(weights, value, NN) + dot(rq, s_ref[0, head], NN) * (
            ramp(rows, 1.0, 1.0, slope) * link
        )
        mixed = mixed.astype(BF16)
        mix_ref[0, :, cols] = mixed
        mixed = mixed.astype(F32)
        power += jnp.sum(mixed * mixed, axis=-1, keepdims=True)
    scale = lax.rsqrt(power / (HEADS * HEAD_DIM) + EPS)
    for head in range(HEADS):
        cols = columns(head)
        u = u_ref[0, :, cols]
        gated_ref[0, :, cols] = (
            mix_ref[0, :, cols].astype(F32) * scale * (u * sigmoid(u))
        ).astype(BF16)


def gate_back_body(
    order, q_ref, u_ref, mix_ref, dg_ref, cos_ref, sin_ref, link_ref, du_ref, dm_ref, state_ref
):
    rows = q_ref.shape[1]
    cos, sin = cos_ref[...], sin_ref[...]
    link = link_ref[0]
    mix = mix_ref[0].astype(F32)
    scale = lax.rsqrt(jnp.mean(mix * mix, axis=-1, keepdims=True) + EPS)
    inner = jnp.zeros((rows, 1), F32)
    for head in range(HEADS):
        cols = columns(head)
        u = u_ref[0, :, cols]
        part = mix_ref[0, :, cols].astype(F32)
        dg = dg_ref[0, :, cols]
        sig = sigmoid(u)
        inner += jnp.sum(dg * (u * sig) * part, axis=-1, keepdims=True)
        du_ref[0, :, cols] = (dg * part * scale * (sig * (1.0 + u * (1.0 - sig)))).astype(BF16)
    inner = inner * (scale * scale * scale) / (HEADS * HEAD_DIM)
    for head in range(HEADS):
        cols = columns(head)
        u = u_ref[0, :, cols]
        part = mix_ref[0, :, cols].astype(F32)
        dg = dg_ref[0, :, cols]
        d_mix = (scale * (dg * (u * sigmoid(u))) - part * inner).astype(BF16)
        dm_ref[0, :, cols] = d_mix
        query = rounded_swish(q_ref[0, :, cols]) * (
            ramp(rows, 1.0, 1.0, slope_of(head)) * link
        )
        state_ref[0, head] = dot(turned(query, cos, sin).astype(BF16), d_mix, TN, BF16)


def mix_back_body(
    order, q_ref, k_ref, v_ref, dm_ref, cos_ref, sin_ref, col_ref, row_ref, link_ref, s_ref,
    dq_ref, dk_ref, dv_ref,
):
    rows = q_ref.shape[1]
    cos, sin = cos_ref[...], sin_ref[...]
    ids_col, ids_row = col_ref[0], row_ref[0]
    link = link_ref[0]
    for head in range(HEADS):
        cols = columns(head)
        slope = slope_of(head)
        q_pre = q_ref[0, :, cols]
        rq = turned(rounded_swish(q_pre), cos, sin).astype(BF16)
        rk = turned(rounded_swish(k_ref[0, :, cols]), cos, sin).astype(BF16)
        value = v_ref[0, :, cols].astype(BF16)
        d_mix = dm_ref[0, :, cols]
        decay = decays(ids_col, ids_row, slope)
        weights = (dot(rq, rk, NT) * decay).astype(BF16)
        d_scores = (dot(d_mix, value, NT) * decay).astype(BF16)
        enter = ramp(rows, 1.0, 1.0, slope) * link
        d_rq = dot(d_scores, rk, NN) + dot(d_mix, s_ref[0, head], NT) * jnp.concatenate(
            [enter, enter], axis=1
        )
        d_query = d_rq[:, :HEAD_DIM] * cos + d_rq[:, HEAD_DIM:] * sin
        dq_ref[0, :, cols] = (
            d_query.astype(BF16).astype(F32) * swish_slope(q_pre)
        ).astype(BF16)
        d_rk = dot(d_scores, rq, TN)
        dk_ref[0, :, cols] = d_rk[:, :HEAD_DIM] * cos + d_rk[:, HEAD_DIM:] * sin
        dv_ref[0, :, cols] = dot(weights, d_mix, TN)


def state_back_body(
    order, k_ref, v_ref, dk_ref, dv_ref, cos_ref, sin_ref, tail_ref, s_ref, dko_ref, dvo_ref
):
    rows = k_ref.shape[1]
    cos, sin = cos_ref[...], sin_ref[...]
    tail = tail_ref[0]
    for head in range(HEADS):
        cols = columns(head)
        k_pre = k_ref[0, :, cols]
        leave = ramp(rows, rows - 1.0, -1.0, slope_of(head)) * tail
        key = rounded_swish(k_pre) * leave
        rk = turned(key, cos, sin).astype(BF16)
        value = v_ref[0, :, cols].astype(BF16)
        state = s_ref[0, head]
        d_rk = dot(value, state, NT) * jnp.concatenate([leave, leave], axis=1)
        d_key = dk_ref[0, :, cols] + d_rk[:, :HEAD_DIM] * cos + d_rk[:, HEAD_DIM:] * sin
        dko_ref[0, :, cols] = (d_key.astype(BF16).astype(F32) * swish_slope(k_pre)).astype(BF16)
        dvo_ref[0, :, cols] = (dv_ref[0, :, cols] + dot(rk, state, NN)).astype(BF16)


ORDERS = (BITS_Y, BITS_X)


def spread(order, h_ref, outs):
    width = h_ref.shape[1] // 8
    for out, bits in zip(outs, ORDERS):
        for k in range(8):
            out[:, k * width : (k + 1) * width] = h_ref[:, at_block(order, bits[k], width)]


def row_norm_body(order, x_ref, *refs):
    x = x_ref[...].astype(F32)
    scale = lax.rsqrt(jnp.mean(x * x, axis=-1, keepdims=True) + EPS)
    refs[-1][...] = (x * scale).astype(BF16)
    spread(order, refs[-1], refs[:-1])


def head_slope(head):
    return jnp.exp2(-8.0 * (head.astype(F32) + 1.0) / HEADS)


def block_decay(ids_col, ids_row, i, j, size, slope):
    gap = (
        (i - j) * size
        + lax.broadcasted_iota(jnp.int32, (size, size), 0)
        - lax.broadcasted_iota(jnp.int32, (size, size), 1)
    ).astype(F32)
    same = ids_col[i * size : (i + 1) * size] == ids_row[:, j * size : (j + 1) * size]
    keep = same if i > j else same & (gap >= 0.0)
    return jnp.where(keep, jnp.exp(-slope * jnp.maximum(gap, 0.0)), 0.0)


def row_mix_body(size, order, q_ref, k_ref, v_ref, cos_ref, sin_ref, col_ref, row_ref, mix_ref):
    q_ref, k_ref, v_ref = q_ref.at[0], k_ref.at[0], v_ref.at[0]
    cos, sin = cos_ref[...], sin_ref[...]
    col, row = col_ref[...], row_ref[...]
    each = q_ref.shape[1] // HEAD_DIM
    for part in range(each):
        cols = columns(part)
        slope = head_slope(pl.program_id(0) * each + part)
        rq = turned(rounded_swish(q_ref[:, cols]), cos, sin).astype(BF16)
        rk = turned(rounded_swish(k_ref[:, cols]), cos, sin).astype(BF16)
        value = v_ref[:, cols].astype(BF16)
        for i in range(rq.shape[0] // size):
            here = slice(i * size, (i + 1) * size)
            mixed = jnp.zeros((size, HEAD_DIM), F32)
            for j in range(i + 1):
                there = slice(j * size, (j + 1) * size)
                scores = dot(rq[here], rk[there], NT) * block_decay(col, row, i, j, size, slope)
                mixed += dot(scores.astype(BF16), value[there], NN)
            mix_ref[here, cols] = mixed.astype(BF16)


def row_mix_back_body(
    size, order, q_ref, k_ref, v_ref, dm_ref, cos_ref, sin_ref, col_ref, row_ref,
    d_ref,
):
    q_ref, k_ref, v_ref = q_ref.at[0], k_ref.at[0], v_ref.at[0]
    dq_ref, dk_ref, dv_ref = d_ref.at[0, 0], d_ref.at[0, 1], d_ref.at[0, 2]
    cos, sin = cos_ref[...], sin_ref[...]
    col, row = col_ref[...], row_ref[...]
    each = q_ref.shape[1] // HEAD_DIM
    count = q_ref.shape[0] // size
    cut = [slice(i * size, (i + 1) * size) for i in range(count)]

    def back(d_turned, pre, at):
        d = d_turned[:, :HEAD_DIM] * cos[at] + d_turned[:, HEAD_DIM:] * sin[at]
        return (d.astype(BF16).astype(F32) * swish_slope(pre[at])).astype(BF16)

    for part in range(each):
        cols = columns(part)
        slope = head_slope(pl.program_id(0) * each + part)
        q_pre, k_pre = q_ref[:, cols], k_ref[:, cols]
        rq = turned(rounded_swish(q_pre), cos, sin).astype(BF16)
        rk = turned(rounded_swish(k_pre), cos, sin).astype(BF16)
        value = v_ref[:, cols].astype(BF16)
        d_mix = dm_ref[:, cols]
        d_rq = [0.0] * count
        d_rk = [0.0] * count
        d_value = [0.0] * count
        for i in range(count):
            for j in range(i + 1):
                decay = block_decay(col, row, i, j, size, slope)
                scores = (dot(rq[cut[i]], rk[cut[j]], NT) * decay).astype(BF16)
                d_scores = (dot(d_mix[cut[i]], value[cut[j]], NT) * decay).astype(BF16)
                d_value[j] += dot(scores, d_mix[cut[i]], TN)
                d_rq[i] += dot(d_scores, rk[cut[j]], NN)
                d_rk[j] += dot(d_scores, rq[cut[i]], TN)
        for i in range(count):
            dq_ref[cut[i], cols] = back(d_rq[i], q_pre, cut[i])
            dk_ref[cut[i], cols] = back(d_rk[i], k_pre, cut[i])
            dv_ref[cut[i], cols] = d_value[i].astype(BF16)


def stacked(refs):
    return jnp.concatenate([r[...] for r in refs], axis=0)


def restored(order, value, out):
    width = value.shape[1] // 8
    for k, at in enumerate(BITS_Y):
        out[:, at_block(order, at, width)] = value[:, k * width : (k + 1) * width]


def project_body(order, h_ref, *refs):
    h = h_ref[...]
    refs[16][0] = dot(h, stacked(refs[:8]), NN)
    refs[16][1] = dot(h, stacked(refs[8:16]), NN)


def out_mid_body(order, mix_ref, h_in_ref, x_ref, *refs):
    u_ref, gated_ref, gated_x_ref, mid_ref = refs[16:20]
    held = refs[-1]
    mix = mix_ref[...].astype(F32)
    u = dot(h_in_ref[...], stacked(refs[:8]), NN)
    u_ref[...] = u
    scale = lax.rsqrt(jnp.mean(mix * mix, axis=-1, keepdims=True) + EPS)
    held[...] = (mix * scale * (u * sigmoid(u))).astype(BF16)
    spread(order, held, (gated_ref, gated_x_ref))
    mid = x_ref[...].astype(F32) + dot(gated_ref[...], stacked(refs[8:16]), NN)
    mid_ref[...] = mid
    scale = lax.rsqrt(jnp.mean(mid * mid, axis=-1, keepdims=True) + EPS)
    held[...] = (mid * scale).astype(BF16)
    spread(order, held, refs[20:22])


def left_right_body(order, h_ref, *refs):
    left_ref, right_ref, product_ref = refs[16:]
    h = h_ref[...]
    left = dot(h, stacked(refs[:8]), NN)
    right = dot(h, stacked(refs[8:16]), NN)
    left_ref[...] = left.astype(BF16)
    right_ref[...] = right.astype(BF16)
    product_ref[...] = (left * right).astype(BF16)


def down_grad_body(rows, order, product_ref, c_ref, *refs):
    outs, held, sems = refs[:4], refs[4], refs[5]
    step = pl.program_id(0)
    size = product_ref.shape[1]
    held[pl.ds(pl.multiple_of(step * size, size), size), :] = dot(
        product_ref[...], c_ref[...], TN, BF16
    )

    @pl.when(step == pl.num_programs(0) - 1)
    def _():
        half = held.shape[1] // 2
        copies = []
        for side, bits in enumerate((BITS_X, BITS_Y)):
            for k, bit in enumerate(bits):
                copies.append(
                    pltpu.make_async_copy(
                        held.at[at_block(order, bit, rows), side * half : (side + 1) * half],
                        outs[2 * (k // 4) + side].at[(k % 4) * rows : (k % 4 + 1) * rows, :],
                        sems.at[side, k],
                    )
                )
        run_copies(copies)


def feed_back_body(
    rows, order, left_ref, right_ref, product_ref, hx_ref, hy_ref, c_ref, mid_ref, *refs
):
    weights, downs = refs[:16], refs[16:32]
    keep_l, send_l, keep_r, send_r, d_mid_ref, d_branch_ref, act_ref = refs[32:39]
    down, grad, total, held_l, held_r, sems = refs[39:]
    step = pl.program_id(0)

    @pl.when(step == 0)
    def _():
        half = down.shape[1] // 2
        run_copies(
            [
                pltpu.make_async_copy(
                    downs[8 * side + k],
                    down.at[at_block(order, at, rows), side * half : (side + 1) * half],
                    sems.at[side, k],
                )
                for side in range(2)
                for k, at in enumerate(BITS_Y)
            ]
        )
        held_l[...] = jnp.zeros_like(held_l)
        held_r[...] = jnp.zeros_like(held_r)

    size = left_ref.shape[1]
    last = pl.num_programs(0) - 2

    def down_rows(block):
        return down[pl.ds(pl.multiple_of(block * size, size), size), :]

    d_left, d_right = held_l[...], held_r[...]
    half = hx_ref.shape[1] // 2
    g_left = dot(hx_ref[...], d_left, TN, BF16)
    keep_l[...] = g_left[:half]
    send_l[...] = g_left[half:]
    g_right = dot(hy_ref[...], d_right, TN, BF16)
    keep_r[...] = g_right[:half]
    send_r[...] = g_right[half:]
    total[...] += dot(product_ref[...], down_rows(jnp.maximum(step - 1, 0)), NN)
    grad[...] += dot(d_left, stacked(weights[:8]), NT) + dot(d_right, stacked(weights[8:]), NT)

    grad_product = dot(c_ref[...], down_rows(jnp.minimum(step, last)), NT)
    held_l[...] = (grad_product * right_ref[...].astype(F32)).astype(BF16)
    held_r[...] = (grad_product * left_ref[...].astype(F32)).astype(BF16)

    @pl.when(step == 0)
    def _():
        grad[...] = jnp.zeros_like(grad)
        total[...] = jnp.zeros_like(total)

    @pl.when(step == pl.num_programs(0) - 1)
    def _():
        mid = mid_ref[...]
        act_ref[...] = (mid + total[...]).astype(BF16)
        restored(order, grad[...], total)
        g = total[...]
        scale = lax.rsqrt(jnp.mean(mid * mid, axis=-1, keepdims=True) + EPS)
        inner = jnp.mean(g * mid, axis=-1, keepdims=True) * (scale * scale * scale)
        d_mid = c_ref[...].astype(F32) + scale * g - mid * inner
        d_mid_ref[...] = d_mid
        d_branch_ref[...] = d_mid.astype(BF16)


def gate_out_back_body(order, d_ref, mix_ref, u_ref, *refs):
    du_ref, dm_ref, held = refs[8:]
    restored(order, dot(d_ref[...], stacked(refs[:8]), NT), held)
    dg = held[...]
    mix = mix_ref[...].astype(F32)
    u = u_ref[...]
    sig = sigmoid(u)
    scale = lax.rsqrt(jnp.mean(mix * mix, axis=-1, keepdims=True) + EPS)
    du_ref[...] = (dg * mix * scale * (sig * (1.0 + u * (1.0 - sig)))).astype(BF16)
    dn = dg * (u * sig)
    inner = jnp.mean(dn * mix, axis=-1, keepdims=True) * (scale * scale * scale)
    dm_ref[...] = (scale * dn - mix * inner).astype(BF16)


def in_back_body(order, x_ref, d_mid_ref, du_ref, d_ref, *refs):
    low, high, gates, (out, grad, held) = refs[:8], refs[8:16], refs[16:24], refs[24:]
    step = pl.program_id(0)

    @pl.when(step == 0)
    def _():
        grad[...] = dot(du_ref[...], stacked(gates), NT)

    grad[...] += dot(d_ref[0, 0], stacked(low), NT) + dot(d_ref[1, 0], stacked(high), NT)

    @pl.when(step == pl.num_programs(0) - 1)
    def _():
        restored(order, grad[...], held)
        g = held[...]
        x = x_ref[...].astype(F32)
        scale = lax.rsqrt(jnp.mean(x * x, axis=-1, keepdims=True) + EPS)
        inner = jnp.mean(g * x, axis=-1, keepdims=True) * (scale * scale * scale)
        out[...] = (d_mid_ref[...] + scale * g - x * inner).astype(BF16)


def weight_grads_body(order, hx_ref, hy_ref, gx_ref, gy_ref, d_ref, du, db, *outs):
    held, sems = outs[4:8], outs[8]
    step = pl.program_id(0)
    half = hx_ref.shape[1] // 2

    def copies(side):
        return [
            pltpu.make_async_copy(held[2 * side + i], outs[2 * side + i], sems.at[2 * side + i])
            for i in range(2)
        ]

    def run(side, h, gated):
        keep, send = held[2 * side], held[2 * side + 1]
        terms = [(h, d_ref.at[0, i]) for i in range(3)] + [(h, du), (gated, db)]
        for i, (lhs, d) in enumerate(terms):
            g = dot(lhs[...], d[...], TN, BF16)
            cols = slice(i * g.shape[1], (i + 1) * g.shape[1])
            keep[:, cols] = g[:half]
            send[:, cols] = g[half:]
        for copy in copies(side):
            copy.start()

    @pl.when(step == 0)
    def _():
        run(0, hx_ref, gx_ref)

    @pl.when(step == 1)
    def _():
        run(1, hy_ref, gy_ref)
        for copy in copies(0) + copies(1):
            copy.wait()


class Chain:
    def __init__(self, fresh, factor, forward, parts):
        self.fresh, self.factor, self.forward, self.parts = fresh, factor, forward, parts
        self.seqs = fresh.shape[0]
        self.now = [fresh[s] for s in range(self.seqs)]
        self.got = [[] for _ in range(self.seqs)]
        self.turns = self.seqs + parts - 2

    def pass_on(self, s, hop):
        pair = (hop - 1, hop) if self.forward else (self.parts - hop, self.parts - hop - 1)
        self.got[s].append(lax.ppermute(self.now[s], "heads", [pair]))

    def begin(self):
        for s in range(self.seqs):
            self.pass_on(s, 1)

    def at(self, turn):
        return [(s, turn - s) for s in range(self.seqs) if 1 <= turn - s < self.parts]

    def arrivals(self, turn):
        self.new = [self.got[s][hop - 1] for s, hop in self.at(turn)]
        return self, "new"

    def go_on(self, turn):
        for (s, hop), new in zip(self.at(turn), self.new):
            self.got[s][hop - 1] = new
            if hop + 1 < self.parts:
                arrived = new.astype(F32) * self.factor[s][:, None, None]
                self.now[s] = (self.fresh[s].astype(F32) + arrived).astype(BF16)
                self.pass_on(s, hop + 1)

    def result(self):
        return jnp.stack([functools.reduce(lambda a, b: a + b, g) for g in self.got])


class Layer:
    def __init__(self, tokens, doc_lengths, cotangent):
        seqs, length, width = tokens.shape
        self.seqs, self.length, self.width, self.count = seqs, length, width, seqs * length
        self.here = lax.axis_index("rows")
        self.place = lax.axis_index("heads")
        self.order = places(self.here, self.place)
        self.x = tokens.reshape(self.count, width)
        self.dy = cotangent.reshape(self.count, width)

        ends = jnp.cumsum(doc_lengths, axis=-1, dtype=jnp.int32)[:, :-1]

        def ids_at(where):
            return jnp.sum((where[None, :, None] >= ends[:, None, :]).astype(jnp.int32), axis=-1)

        start = self.place * length
        positions = start + jnp.arange(length, dtype=jnp.int32)
        ids = ids_at(positions)
        before = jnp.where(self.place > 0, ids_at(jnp.reshape(start - 1, (1,))), -1)
        final = ids[:, -1:]
        link = (ids == before).astype(F32)[:, :, None]
        tail = (ids == final).astype(F32)[:, :, None]
        slopes = jnp.array([slope_of(h) for h in range(HEADS)], F32)
        self.factor = (final == before).astype(F32) * jnp.exp(-slopes * length)[None, :]
        theta = jnp.exp(-math.log(10000.0) * jnp.arange(HEAD_DIM, dtype=F32) / HEAD_DIM)
        angle = positions.astype(F32)[:, None] * theta[None, :]

        table = pl.BlockSpec((length, HEAD_DIM), lambda s, *_: (0, 0))
        one_col = pl.BlockSpec((1, length, 1), lambda s, *_: (s, 0, 0))
        one_row = pl.BlockSpec((1, 1, length), lambda s, *_: (s, 0, 0))
        self.turn = [(jnp.cos(angle), table), (jnp.sin(angle), table)]
        self.link = link, one_col
        self.tail = tail, one_col
        self.masks = [(ids[:, :, None], one_col), (ids[:, None, :], one_row), self.link]
        self.seq = pl.BlockSpec((1, length, width), lambda s, *_: (s, 0, 0))
        self.state = pl.BlockSpec(
            (1, HEADS, 2 * HEAD_DIM, HEAD_DIM), lambda s, *_: (s, 0, 0, 0)
        )
        self.states = (seqs, HEADS, 2 * HEAD_DIM, HEAD_DIM), BF16, self.state
        step = min(self.count, 256)
        self.grid = (self.count // step,)
        self.wide = rows_spec(step, width)

    def rows(self, body, ins, types, order=None):
        return call(
            body, self.grid, self.order, [(a, self.wide) for a in ins],
            [((self.count, self.width), t, self.wide) for t in types],
        )

    def seqwise(self, body, ins, outs):
        shape = (self.seqs, self.length, self.width)
        ins = [i if isinstance(i, tuple) else (i.reshape(shape), self.seq) for i in ins]
        outs = [o if isinstance(o, tuple) else (shape, o, self.seq) for o in outs]
        got = call(body, (self.seqs,), self.order, ins, outs)
        return [g.reshape(self.count, self.width) if g.shape == shape else g for g in got]

    def norm(self):
        return self.rows(norm_body, [self.x], [BF16])

    def fresh(self, k_pre, v_pre):
        return self.seqwise(fresh_body, [k_pre, v_pre] + self.turn + [self.tail], [self.states])[0]

    def mix(self, q_pre, k_pre, v_pre, u_pre, state_in):
        ins = [q_pre, k_pre, v_pre, u_pre] + self.turn + self.masks + [(state_in, self.state)]
        return self.seqwise(mix_body, ins, [BF16, BF16])

    def mid(self, branch):
        return self.rows(mid_body, [self.x, branch], [F32, BF16])

    def mid_back(self, x_mid, grad):
        return self.rows(norm_back_body, [x_mid, self.dy, grad], [F32, BF16])

    def in_back(self, d_mid, grad):
        return self.rows(norm_back_body, [self.x, d_mid, grad], [F32])[0]

    def gate_back(self, q_pre, u_pre, mix, d_gated):
        ins = [q_pre, u_pre, mix, d_gated] + self.turn + [self.link]
        return self.seqwise(gate_back_body, ins, [BF16, BF16, self.states])

    def mix_back(self, q_pre, k_pre, v_pre, d_mix, state_in):
        ins = [q_pre, k_pre, v_pre, d_mix] + self.turn + self.masks + [(state_in, self.state)]
        return self.seqwise(mix_back_body, ins, [BF16, F32, F32])

    def state_back(self, k_pre, v_pre, dk_near, dv_near, d_state):
        ins = [k_pre, v_pre, dk_near, dv_near] + self.turn + [self.tail, (d_state, self.state)]
        return self.seqwise(state_back_body, ins, [BF16, BF16])


def plainly(layer, heads_count, weights):
    w_query, w_key, w_value, w_gate, w_out, w_left, w_right, w_down = (
        lax.all_gather(w, "rows", axis=0, tiled=True) for w in weights
    )

    def carried(fresh, forward):
        chain = Chain(fresh, layer.factor, forward, heads_count)
        chain.begin()
        for turn in range(1, chain.turns + 1):
            chain.arrivals(turn)
            chain.go_on(turn)
        return chain.result()

    def gradient(lhs, d):
        total = lax.psum_scatter(dot(lhs, d, TN, BF16), "rows", scatter_dimension=0, tiled=True)
        return lax.psum_scatter(total, "heads", scatter_dimension=1, tiled=True).astype(F32)

    (h_in,) = layer.norm()
    q_pre, k_pre, v_pre, u_pre = (
        dot(h_in, w, NN) for w in (w_query, w_key, w_value, w_gate)
    )
    state_in = carried(layer.fresh(k_pre, v_pre), True)
    mix, gated = layer.mix(q_pre, k_pre, v_pre, u_pre, state_in)
    x_mid, h_mid = layer.mid(dot(gated, w_out, NN))
    left, right = dot(h_mid, w_left, NN), dot(h_mid, w_right, NN)
    product = (left * right).astype(BF16)
    activations = (x_mid + dot(product, w_down, NN)).astype(BF16)
    grad_product = dot(layer.dy, w_down, NT)
    d_left = (grad_product * right).astype(BF16)
    d_right = (grad_product * left).astype(BF16)
    d_mid, d_branch = layer.mid_back(
        x_mid, dot(d_left, w_left, NT) + dot(d_right, w_right, NT)
    )
    d_u, d_mix, d_fresh = layer.gate_back(q_pre, u_pre, mix, dot(d_branch, w_out, NT))
    d_state = carried(d_fresh, False)
    d_q, dk_near, dv_near = layer.mix_back(q_pre, k_pre, v_pre, d_mix, state_in)
    d_k, d_v = layer.state_back(k_pre, v_pre, dk_near, dv_near, d_state)
    grad_in = (
        dot(d_q, w_query, NT) + dot(d_u, w_gate, NT) + dot(d_k, w_key, NT) + dot(d_v, w_value, NT)
    )
    input_grad = layer.in_back(d_mid, grad_in)
    pairs = (
        (h_in, d_q), (h_in, d_k), (h_in, d_v), (h_in, d_u), (gated, d_branch),
        (h_mid, d_left), (h_mid, d_right), (product, layer.dy),
    )
    return (activations, input_grad) + tuple(gradient(lhs, d) for lhs, d in pairs)


class Row:
    def __init__(self, doc_lengths, length, width, here, head):
        self.length, self.width = length, width
        self.order = places(here, head)
        lengths = lax.dynamic_index_in_dim(doc_lengths, head, 0, keepdims=False)
        ends = jnp.cumsum(lengths, dtype=jnp.int32)[:-1]
        positions = jnp.arange(length, dtype=jnp.int32)
        ids = jnp.sum((positions[:, None] >= ends[None, :]).astype(jnp.int32), axis=-1)
        theta = jnp.exp(-math.log(10000.0) * jnp.arange(HEAD_DIM, dtype=F32) / HEAD_DIM)
        angle = positions.astype(F32)[:, None] * theta[None, :]

        def whole(rows, cols):
            return pl.BlockSpec((rows, cols), lambda *_: (0, 0))

        table = whole(length, HEAD_DIM)
        self.extra = [
            (jnp.cos(angle), table), (jnp.sin(angle), table),
            (ids[:, None], whole(length, 1)), (ids[None, :], whole(1, length)),
        ]
        self.heads = pl.BlockSpec((length, 2 * HEAD_DIM), lambda h, *_: (0, h))
        self.wide = rows_spec(min(length, 256), width)
        self.all = whole(length, width)
        self.block = math.gcd(length, 256)
        self.flops = 2 * length * width * width

    def norm(self, x):
        return self.by_rows(row_norm_body, [(x, self.wide)], [], [BF16, BF16], [BF16])

    def pieces(self, group, half, width=None):
        rows, whole = group.pieces[half].shape
        spec = pl.BlockSpec((rows, width or whole), lambda i, *_: (0, i if width else 0))
        return [(a, spec) for a in group.all(half)]

    def thirds(self, which=None, dtype=F32):
        half = self.width // 2
        if which is None:
            return pl.BlockSpec((2, self.length, half), lambda i, *_: (0, 0, i))
        pair = 2 * HEAD_DIM
        each = half // pair
        return pl.BlockSpec(
            (1, self.length, pair), lambda i, *_: (i // each, 0, which * each + i % each)
        )

    def project(self, h, qkv):
        half = self.width // 2
        return call(
            project_body, (3,), self.order,
            [(h, self.all)] + self.pieces(qkv, 0, half) + self.pieces(qkv, 1, half),
            [((2, self.length, 3 * half), F32, self.thirds())], flops=3 * self.flops,
        )[0]

    def column(self, block, offset=0):
        return pl.BlockSpec((self.length, block), lambda i, *_: (0, offset + i))

    def mix(self, pre):
        return call(
            functools.partial(row_mix_body, self.block), (HEADS // 2,), self.order,
            [(pre, self.thirds(i)) for i in range(3)] + self.extra,
            [((self.length, self.width), BF16, self.heads)], flops=self.flops * 3 // 8,
        )[0]

    def mix_back(self, pre, d_mix):
        pair, half = 2 * HEAD_DIM, self.width // 2
        each = half // pair
        spec = pl.BlockSpec((1, 3, self.length, pair), lambda i, *_: (i // each, 0, 0, i % each))
        return call(
            functools.partial(row_mix_back_body, self.block), (HEADS // 2,), self.order,
            [(pre, self.thirds(i)) for i in range(3)] + [(d_mix, self.heads)] + self.extra,
            [((2, 3, self.length, half), BF16, spec)], flops=self.flops,
        )[0]

    def by_rows(self, body, ins, weights, types, scratch):
        step = self.wide.block_shape[0]
        return call(
            body, (self.length // step,), self.order, ins + weights,
            [((self.length, self.width), t, self.wide) for t in types],
            scratch=[pltpu.VMEM((step, self.width), t) for t in scratch], flops=self.flops,
        )

    def out_mid(self, mix, h, x, uo):
        return self.by_rows(
            out_mid_body, [(mix, self.wide), (h, self.wide), (x, self.wide)],
            self.pieces(uo, 0) + self.pieces(uo, 1),
            [F32, BF16, BF16, F32, BF16, BF16], [BF16],
        )

    def gate_out_back(self, d_branch, mix, u_pre, uo):
        return self.by_rows(
            gate_out_back_body, [(d_branch, self.wide), (mix, self.wide), (u_pre, self.wide)],
            self.pieces(uo, 1), [BF16, BF16], [F32],
        )

    def left_right(self, h, ff):
        inner = ff.pieces[0].shape[1]
        block = math.gcd(inner, 1408)
        return call(
            left_right_body, (inner // block,), self.order,
            [(h, self.all)] + self.pieces(ff, 0, block) + self.pieces(ff, 1, block),
            [((self.length, inner), BF16, self.column(block))] * 3,
            flops=2 * self.flops * inner // self.width,
        )

    def down_grad(self, product, c):
        inner, half = product.shape[1], self.width // 2
        block = math.gcd(inner, 1408)
        rows = inner // 8
        got = call(
            functools.partial(down_grad_body, rows), (inner // block,), self.order,
            [(product, self.column(block)), (c, self.all)], [((4 * rows, half), BF16, HBM)] * 4,
            scratch=[pltpu.VMEM((inner, self.width), BF16), pltpu.SemaphoreType.DMA((2, 8))],
            flops=self.flops * inner // self.width,
        )
        return Reduce(self.order, got[2:], got[:2], [2, 4])

    def feed_back(self, left, right, product, h_x, h_y, c, x_mid, ff, down):
        inner, rows = ff.pieces[0].shape[1], down.pieces[0].shape[0]
        block = math.gcd(inner, 256)
        steps = inner // block

        def now(rows):
            return pl.BlockSpec((rows, block), lambda i, *_: (0, jnp.minimum(i, steps - 1)))

        def before(rows):
            return pl.BlockSpec((rows, block), lambda i, *_: (0, jnp.maximum(i - 1, 0)))

        full = (self.length, self.width)
        weights = [
            (a, before(ff.pieces[0].shape[0])) for a in ff.all(0) + ff.all(1)
        ]
        return call(
            functools.partial(feed_back_body, rows), (steps + 1,), self.order,
            [(left, now(self.length)), (right, now(self.length)), (product, before(self.length))]
            + [(a, self.all) for a in (h_x, h_y, c, x_mid)]
            + weights + [(a, HBM) for a in down.all(0) + down.all(1)],
            [((self.width // 2, inner), BF16, before(self.width // 2))] * 4
            + [(full, F32, self.all), (full, BF16, self.all), (full, BF16, self.all)],
            scratch=[pltpu.VMEM((inner, self.width), BF16)] + [pltpu.VMEM(full, F32)] * 2
            + [pltpu.VMEM((self.length, block), BF16)] * 2 + [pltpu.SemaphoreType.DMA((2, 8))],
            flops=6 * self.flops * inner // self.width,
        )

    def in_back(self, x, d_mid, d, d_u, qkv, uo):
        half = self.width // 2
        full = (self.length, self.width)
        third = pl.BlockSpec((2, 1, self.length, half), lambda i, *_: (0, i, 0, 0))
        return call(
            in_back_body, (3,), self.order,
            [(x, self.all), (d_mid, self.all), (d_u, self.all), (d, third)]
            + self.pieces(qkv, 0, half) + self.pieces(qkv, 1, half) + self.pieces(uo, 0),
            [(full, BF16, self.all)], scratch=[pltpu.VMEM(full, F32)] * 2, flops=4 * self.flops,
        )[0]

    def weight_grads(self, h_x, h_y, gated_x, gated_y, d, d_u, d_branch):
        half = self.width // 2
        shape = (half, 5 * half)
        thirds = pl.BlockSpec((1, 3, self.length, half), lambda i, *_: (i, 0, 0, 0))
        got = call(
            weight_grads_body, (2,), self.order,
            [(a, self.all) for a in (h_x, h_y, gated_x, gated_y)]
            + [(d, thirds), (d_u, self.column(half)), (d_branch, self.column(half))],
            [(shape, BF16, HBM)] * 4,
            scratch=[pltpu.VMEM(shape, BF16)] * 4 + [pltpu.SemaphoreType.DMA((4,))],
            flops=5 * self.flops,
        )
        return Reduce(self.order, got[1::2], got[::2], [2, 4])


def stepwise(tokens, doc_lengths, cotangent, weights):
    w_query, w_key, w_value, w_gate, w_out, w_left, w_right, w_down = weights
    size, width = tokens.shape[1:]
    length, half = 4 * size, width // 2
    here, head = lax.axis_index("rows"), lax.axis_index("heads")
    row = Row(doc_lengths, length, width, here, head)
    order = row.order
    v = types.SimpleNamespace()
    clock = Clock(order)
    tick = clock.tick

    def exchanged(a):
        return lax.all_to_all(a.reshape(4, size, width), "heads", 0, 0, tiled=True)

    def whole_row(a):
        return exchanged(a).reshape(length, width)

    inner = w_left.shape[1]
    uo = Gather([w_gate, w_out])
    uo.first()
    qkv = Gather(
        pack(order, [w_query, w_key, w_value], [[(i, at, half) for i in range(3)] for at in (0, half)])
    )
    qkv.first()
    v.x = whole_row(after(tokens, uo.near_x[0]))
    v.extra = [a for a, _ in row.extra]
    ff = Gather([w_left, w_right])
    v.c = cotangent
    tick((qkv, "near_x"), (qkv, "near_y"), (uo, "near_x"), (uo, "near_y"), (uo, "pieces"), (v, "c"), (v, "extra"))
    row.extra = [(a, spec) for a, (_, spec) in zip(v.extra, row.extra)]
    qkv.second()
    uo.second()
    qkv.cross("pieces", "near_x", "near_y")
    uo.cross("pieces", "near_x", "near_y")
    v.h = row.norm(v.x)
    tick((qkv, "far"), (uo, "far"), (v, "h"), (ff, "pieces"))
    ff.first()
    ff.cross("pieces")
    qkv.cross("far")
    uo.cross("far")
    v.pre = row.project(v.h[0], qkv)
    v.mix = row.mix(v.pre)
    v.u_pre, v.gated, v.gated_x, v.x_mid, *v.h_mid = row.out_mid(v.mix, v.h[0], v.x, uo)
    v.down = w_down
    tick((v, "x_mid"), (v, "h_mid"), (ff, "near_x"), (ff, "near_y"), (v, "down"), (v, "c"))
    ff.second()
    v.c = whole_row(v.c)
    ff.cross("near_x", "near_y")
    v.down = pack(order, [v.down], [[(0, 0, half)], [(0, half, half)]])
    tick((ff, "far"), (v, "down"))
    down = Gather(v.down)
    ff.cross("far")
    down.first()
    down.cross("pieces")
    h_y, h_x = v.h_mid

    v.left, v.right, v.product = row.left_right(h_y, ff)
    tick((v, "left"), (v, "right"), (v, "product"), (down, "near_x"), (down, "near_y"), (v, "c"))
    down.second()
    down.cross("near_x", "near_y")
    v.g_down = dot(v.product, v.c, TN, BF16)
    tick((v, "g_down"), (down, "far"), (v, "left"))
    v.sum_down = lax.psum_scatter(v.g_down, "rows", scatter_dimension=0, tiled=True)
    down.cross("far")
    tick((down, "far_other"), (v, "left"))
    keep_l, send_l, keep_r, send_r, v.d_mid, v.d_branch, v.act = row.feed_back(
        v.left, v.right, v.product, h_x, h_y, v.c, v.x_mid, ff, down
    )
    r_ff = Reduce(order, [send_l, send_r], [keep_l, keep_r], [2, 4])
    tick((r_ff, "sends"), (v, "d_mid"), (v, "d_branch"), (v, "act"))
    r_ff.core()
    v.d_u, v.d_mix = row.gate_out_back(v.d_branch, v.mix, v.u_pre, uo)
    tick((r_ff, "theirs"), (v, "d_u"), (v, "d_mix"))
    r_ff.join()
    tick((r_ff, "totals"), (v, "act"), (v, "d_mix"))
    r_ff.first()
    v.act = exchanged(v.act)
    v.d = row.mix_back(v.pre, v.d_mix)
    tick((v, "d"))
    v.back = row.in_back(v.x, v.d_mid, v.d, v.d_u, qkv, uo)
    tick((v, "back"), (v, "d"), (v, "act"))
    v.back = exchanged(v.back)
    r_att = row.weight_grads(v.h[1], v.h[0], v.gated_x, v.gated, v.d, v.d_u, v.d_branch)
    tick((r_att, "sends"), (r_ff, "got"), (v, "sum_down"))
    r_att.core()
    r_ff.join_first()
    tick((r_att, "theirs"), (r_ff, "parts"), (v, "sum_down"))
    r_ff.second()
    r_att.join()
    sum_down = after(v.sum_down, *r_att.totals)
    s_down = Settle(order, [[sum_down]], half // 2, [lambda z: z * (half // 2)])
    tick((r_att, "totals"), (r_ff, "got_last"), (s_down, "out"))
    r_att.first()
    s_down.pass_on(1)
    quarter = inner // 4
    s_ff = r_ff.settle(quarter, [lambda z: z * quarter, lambda z: inner + z * quarter])
    tick((s_ff, "out"), (s_down, "got"))
    s_ff.pass_on(1)
    s_down.join()
    tick((s_down, "out"), (v, "back"))
    v.back = v.back.astype(F32)
    tick((s_down, "out"), (s_ff, "got"), (v, "back"))
    s_down.pass_on(2)
    s_ff.join()
    tick((s_ff, "out"), (r_att, "got"), (s_down, "got"))
    s_ff.pass_on(2)
    r_att.join_first()
    tick((r_att, "parts"), (s_down, "got"))
    r_att.second()
    (v.g_down,) = s_down.result()
    tick((r_att, "got_last"), (v, "g_down"))
    s_att = r_att.settle(
        half // 2,
        [
            lambda z, i=i: (z // 2) * 5 * half + i * half + (z % 2) * (half // 2)
            for i in range(5)
        ],
    )
    tick((s_att, "out"), (s_ff, "got"))
    s_att.pass_on(1)
    v.g_ff = s_ff.result()
    tick((s_att, "got"), (v, "g_ff"))
    s_att.join()
    tick((s_att, "out"))
    s_att.pass_on(2)
    g_query, g_key, g_value, g_gate, g_out = s_att.result()
    g_left, g_right = v.g_ff
    return (
        v.act, v.back, g_query, g_key, g_value, g_gate, g_out, g_left, g_right, v.g_down
    )


def on_device(rows_count, heads_count, tokens, doc_lengths, cotangent, *weights):
    if rows_count == 8 and heads_count == 4 and tokens.shape[0] == 4:
        return stepwise(tokens, doc_lengths, cotangent, weights)
    layer = Layer(tokens, doc_lengths, cotangent)
    activations, input_grad, *grads = plainly(layer, heads_count, weights)
    return (activations.reshape(tokens.shape), input_grad.reshape(tokens.shape), *grads)


def solution(mesh):
    sizes = dict(mesh.shape)
    tokens = P("rows", "heads", None)
    weights = P("rows", None)
    grads = P("rows", "heads")
    return jax.shard_map(
        functools.partial(on_device, sizes["rows"], sizes["heads"]),
        mesh=mesh,
        in_specs=(tokens, weights, tokens) + (weights,) * 8,
        out_specs=(tokens, tokens) + (grads,) * 8,
        check_vma=False,
    )
```

```python
import functools
import math
import types

import jax
import jax.numpy as jnp
from jax import lax
from jax.experimental import pallas as pl
from jax.experimental.pallas import tpu as pltpu
from jax.sharding import PartitionSpec as P

HEADS = 8
HEAD_DIM = 128
EPS = 1e-06
F32 = jnp.float32
BF16 = jnp.bfloat16
VMEM_LIMIT = 60 << 20

BITS = (0, 2, 4, 6, 1, 3, 5, 7)
BITS_X = (0, 4, 2, 6, 1, 5, 3, 7)
BITS_Y = (0, 2, 4, 6, 1, 3, 5, 7)


def after(value, *others):
    return lax.optimization_barrier((value,) + others)[0]


def dot(a, b, dims, out=F32):
    return lax.dot_general(a, b, (dims, ((), ())), preferred_element_type=F32).astype(out)


NN = ((1,), (0,))
NT = ((1,), (1,))
TN = ((0,), (0,))


def swap(value, bit, size):
    return lax.ppermute(value, "rows", [(i, i ^ bit) for i in range(size)])


def swap_heads(value, bit):
    return lax.ppermute(value, "heads", [(i, i ^ bit) for i in range(4)])


HBM = pl.BlockSpec(memory_space=pltpu.HBM)


def whole_spec(rows, width):
    return pl.BlockSpec((rows, width), lambda i, *_: (0, 0))


def run_copies(copies):
    for copy in copies:
        copy.start()
    for copy in copies:
        copy.wait()


def pack(order, arrays, lists):
    rows = arrays[0].shape[0]
    widths = [sum(w for _, _, w in parts) for parts in lists]
    most = max(len(parts) for parts in lists)

    def body(order, *refs):
        ins, outs, sems = refs[: len(arrays)], refs[len(arrays) : -1], refs[-1]
        copies = []
        for j, parts in enumerate(lists):
            at = 0
            for i, (which, begin, width) in enumerate(parts):
                copies.append(
                    pltpu.make_async_copy(
                        ins[which].at[:, begin : begin + width],
                        outs[j].at[:, at : at + width],
                        sems.at[j, i],
                    )
                )
                at += width
        run_copies(copies)

    return call(
        body, (1,), order, [(a, HBM) for a in arrays],
        [((rows, w), BF16, whole_spec(rows, w)) for w in widths],
        scratch=[pltpu.SemaphoreType.DMA((len(lists), most))],
    )


class Clock:
    def __init__(self, start):
        self.token = start

    def tick(self, *places):
        held = [getattr(o, n) for o, n in places]
        held, self.token = lax.optimization_barrier((held, self.token))
        for (o, n), value in zip(places, held):
            setattr(o, n, value)


def places(here, head):
    return jnp.stack([here ^ b for b in range(8)] + [head ^ b for b in range(4)]).astype(jnp.int32)


class Gather:
    def __init__(self, pieces):
        self.pieces = list(pieces)
        self.near_x, self.near_y = [None, None], [None, None]

    def first(self, *halves):
        for half in halves or (0, 1):
            self.near_x[half] = swap(self.pieces[half], 2, 8)
            self.near_y[half] = swap(self.pieces[half], 4, 8)

    def second(self):
        self.far = [swap(self.near_x[0], 4, 8), swap(self.near_y[1], 2, 8)]

    def cross(self, *names):
        for name in names:
            setattr(self, name + "_other", [swap(p, 1, 8) for p in getattr(self, name)])

    def all(self, half):
        names = ("pieces", "near_x", "near_y", "far")
        return [getattr(self, n + core)[half] for core in ("", "_other") for n in names]


def added(*terms):
    return functools.reduce(lambda a, b: a + b, [t.astype(F32) for t in terms]).astype(BF16)


class Reduce:
    def __init__(self, order, sends, keeps, bits):
        self.order, self.sends, self.keeps, self.bits = order, list(sends), list(keeps), list(bits)

    def core(self):
        self.theirs = [swap(s, 1, 8) for s in self.sends]

    def join(self):
        half = self.keeps[0].shape[0] // 2
        self.totals = [added(k[half:], t[half:]) for k, t in zip(self.keeps, self.theirs)]

    def first(self):
        self.got = [swap(t, b, 8) for t, b in zip(self.totals, self.bits)]

    def join_first(self):
        rows = self.keeps[0].shape[0] // 4
        terms = list(zip(self.keeps, self.theirs, self.got))
        self.parts = [added(*(a[rows : 2 * rows] for a in t)) for t in terms]
        self.own = [list(t) for t in terms]

    def second(self):
        self.got_last = [swap(p, 6 - b, 8) for p, b in zip(self.parts, self.bits)]

    def settle(self, block, starts):
        return Settle(self.order, [t + [g] for t, g in zip(self.own, self.got_last)], block, starts)


class Settle:
    def __init__(self, order, parts, block, starts):
        self.order, self.block, self.count = order, block, len(starts)
        rows = self.rows = parts[0][-1].shape[0]
        widths = [p[-1].shape[1] for p in parts]
        counts = [len(p) for p in parts]

        def body(order, *refs):
            *results, held = refs[sum(counts) :]
            owns, outs = results[:2], results[2:]
            at, first = 0, 0
            for width, count in zip(widths, counts):
                total = refs[first][...].astype(F32)
                for ref in refs[first + 1 : first + count]:
                    total += ref[...].astype(F32)
                held[:, at : at + width] = total
                at, first = at + width, first + count
            for z in range(4):

                @pl.when(order[8] == z)
                def _(z=z):
                    for i, start in enumerate(starts):
                        for j, (mine, theirs) in enumerate(((0, 1), (2, 3))):
                            mine, theirs = start(z ^ mine), start(z ^ theirs)
                            owns[j][i] = held[:, mine : mine + block]
                            outs[j][i] = held[:, theirs : theirs + block].astype(BF16)

        shape = (self.count, rows, block)
        spec = pl.BlockSpec((self.count, rows // 2, block), lambda i, *_: (0, i, 0))
        self.own, self.far, self.last, self.out = call(
            body, (2,), order,
            [(a, pl.BlockSpec((rows // 2, a.shape[1]), lambda i, *_: (i, 0))) for p in parts for a in p],
            [(shape, F32, spec)] * 2 + [(shape, BF16, spec)] * 2,
            scratch=[pltpu.VMEM((rows // 2, sum(widths)), F32)],
        )

    def first(self):
        self.got = swap_heads(self.out, 1)

    def join(self):
        self.out = (self.far + self.got.astype(F32)).astype(BF16)

    def second(self):
        self.got_far = swap_heads(self.out, 2)
        self.got_near = swap_heads(self.last, 1)

    def result(self):
        return [
            self.own[i] + self.got_near[i].astype(F32) + self.got_far[i].astype(F32)
            for i in range(self.count)
        ]


def at_block(order_ref, index, width):
    return pl.ds(pl.multiple_of(order_ref[index] * width, width), width)


def sigmoid(v):
    return 1.0 / (1.0 + jnp.exp(-v))


def swish_slope(v):
    sig = sigmoid(v)
    return sig * (1.0 + v * (1.0 - sig))


def call(body, grid, order, ins, outs, scratch=(), flops=0):
    moved = sum(a.size * a.dtype.itemsize for a, _ in ins) + sum(
        math.prod(s) * jnp.dtype(t).itemsize for s, t, _ in outs
    )
    return pl.pallas_call(
        body,
        grid_spec=pltpu.PrefetchScalarGridSpec(
            num_scalar_prefetch=1,
            grid=grid,
            in_specs=[spec for _, spec in ins],
            out_specs=[spec for _, _, spec in outs],
            scratch_shapes=list(scratch),
        ),
        out_shape=[jax.ShapeDtypeStruct(s, t) for s, t, _ in outs],
        compiler_params=pltpu.CompilerParams(vmem_limit_bytes=VMEM_LIMIT),
        cost_estimate=pl.CostEstimate(flops=flops // 4, bytes_accessed=moved // 4, transcendentals=0),
    )(order, *[a for a, _ in ins])


def rows_spec(count, width, column=0):
    return pl.BlockSpec((count, width), lambda i, *_: (i, column))


def norm_body(order, x_ref, h_ref):
    x = x_ref[...].astype(F32)
    scale = lax.rsqrt(jnp.mean(x * x, axis=-1, keepdims=True) + EPS)
    h_ref[...] = (x * scale).astype(BF16)


def mid_body(order, x_ref, b_ref, mid_ref, h_ref):
    mid = x_ref[...].astype(F32) + b_ref[...]
    mid_ref[...] = mid
    scale = lax.rsqrt(jnp.mean(mid * mid, axis=-1, keepdims=True) + EPS)
    h_ref[...] = (mid * scale).astype(BF16)


def norm_back_body(order, v_ref, base_ref, g_ref, *outs):
    v = v_ref[...].astype(F32)
    g = g_ref[...]
    scale = lax.rsqrt(jnp.mean(v * v, axis=-1, keepdims=True) + EPS)
    inner = jnp.mean(g * v, axis=-1, keepdims=True) * (scale * scale * scale)
    total = base_ref[...].astype(F32) + scale * g - v * inner
    outs[0][...] = total
    if len(outs) > 1:
        outs[1][...] = total.astype(BF16)


def ramp(rows, start, sign, slope):
    place = lax.broadcasted_iota(jnp.int32, (rows, HEAD_DIM), 0).astype(F32)
    return jnp.exp(-slope * (start + sign * place))


def decays(ids_col, ids_row, slope):
    rows = ids_col.shape[0]
    gap = (
        lax.broadcasted_iota(jnp.int32, (rows, rows), 0)
        - lax.broadcasted_iota(jnp.int32, (rows, rows), 1)
    ).astype(F32)
    keep = (gap >= 0.0) & (ids_col == ids_row)
    return jnp.where(keep, jnp.exp(-slope * jnp.maximum(gap, 0.0)), 0.0)


def slope_of(head):
    return 2.0 ** (-8.0 * (head + 1) / HEADS)


def columns(head):
    return slice(head * HEAD_DIM, (head + 1) * HEAD_DIM)


def turned(a, cos, sin):
    return jnp.concatenate([a * cos, a * sin], axis=1)


def rounded_swish(v):
    return (v * sigmoid(v)).astype(BF16).astype(F32)


def fresh_body(order, k_ref, v_ref, cos_ref, sin_ref, tail_ref, state_ref):
    rows = k_ref.shape[1]
    cos, sin = cos_ref[...], sin_ref[...]
    tail = tail_ref[0]
    for head in range(HEADS):
        key = rounded_swish(k_ref[0, :, columns(head)])
        key = key * (ramp(rows, rows - 1.0, -1.0, slope_of(head)) * tail)
        value = v_ref[0, :, columns(head)].astype(BF16)
        state_ref[0, head] = dot(turned(key, cos, sin).astype(BF16), value, TN, BF16)


def mix_body(
    order, q_ref, k_ref, v_ref, u_ref, cos_ref, sin_ref, col_ref, row_ref, link_ref, s_ref,
    mix_ref, gated_ref,
):
    rows = q_ref.shape[1]
    cos, sin = cos_ref[...], sin_ref[...]
    ids_col, ids_row = col_ref[0], row_ref[0]
    link = link_ref[0]
    power = jnp.zeros((rows, 1), F32)
    for head in range(HEADS):
        cols = columns(head)
        slope = slope_of(head)
        rq = turned(rounded_swish(q_ref[0, :, cols]), cos, sin).astype(BF16)
        rk = turned(rounded_swish(k_ref[0, :, cols]), cos, sin).astype(BF16)
        value = v_ref[0, :, cols].astype(BF16)
        weights = (dot(rq, rk, NT) * decays(ids_col, ids_row, slope)).astype(BF16)
        mixed = dot(weights, value, NN) + dot(rq, s_ref[0, head], NN) * (
            ramp(rows, 1.0, 1.0, slope) * link
        )
        mixed = mixed.astype(BF16)
        mix_ref[0, :, cols] = mixed
        mixed = mixed.astype(F32)
        power += jnp.sum(mixed * mixed, axis=-1, keepdims=True)
    scale = lax.rsqrt(power / (HEADS * HEAD_DIM) + EPS)
    for head in range(HEADS):
        cols = columns(head)
        u = u_ref[0, :, cols]
        gated_ref[0, :, cols] = (
            mix_ref[0, :, cols].astype(F32) * scale * (u * sigmoid(u))
        ).astype(BF16)


def gate_back_body(
    order, q_ref, u_ref, mix_ref, dg_ref, cos_ref, sin_ref, link_ref, du_ref, dm_ref, state_ref
):
    rows = q_ref.shape[1]
    cos, sin = cos_ref[...], sin_ref[...]
    link = link_ref[0]
    mix = mix_ref[0].astype(F32)
    scale = lax.rsqrt(jnp.mean(mix * mix, axis=-1, keepdims=True) + EPS)
    inner = jnp.zeros((rows, 1), F32)
    for head in range(HEADS):
        cols = columns(head)
        u = u_ref[0, :, cols]
        part = mix_ref[0, :, cols].astype(F32)
        dg = dg_ref[0, :, cols]
        sig = sigmoid(u)
        inner += jnp.sum(dg * (u * sig) * part, axis=-1, keepdims=True)
        du_ref[0, :, cols] = (dg * part * scale * (sig * (1.0 + u * (1.0 - sig)))).astype(BF16)
    inner = inner * (scale * scale * scale) / (HEADS * HEAD_DIM)
    for head in range(HEADS):
        cols = columns(head)
        u = u_ref[0, :, cols]
        part = mix_ref[0, :, cols].astype(F32)
        dg = dg_ref[0, :, cols]
        d_mix = (scale * (dg * (u * sigmoid(u))) - part * inner).astype(BF16)
        dm_ref[0, :, cols] = d_mix
        query = rounded_swish(q_ref[0, :, cols]) * (
            ramp(rows, 1.0, 1.0, slope_of(head)) * link
        )
        state_ref[0, head] = dot(turned(query, cos, sin).astype(BF16), d_mix, TN, BF16)


def mix_back_body(
    order, q_ref, k_ref, v_ref, dm_ref, cos_ref, sin_ref, col_ref, row_ref, link_ref, s_ref,
    dq_ref, dk_ref, dv_ref,
):
    rows = q_ref.shape[1]
    cos, sin = cos_ref[...], sin_ref[...]
    ids_col, ids_row = col_ref[0], row_ref[0]
    link = link_ref[0]
    for head in range(HEADS):
        cols = columns(head)
        slope = slope_of(head)
        q_pre = q_ref[0, :, cols]
        rq = turned(rounded_swish(q_pre), cos, sin).astype(BF16)
        rk = turned(rounded_swish(k_ref[0, :, cols]), cos, sin).astype(BF16)
        value = v_ref[0, :, cols].astype(BF16)
        d_mix = dm_ref[0, :, cols]
        decay = decays(ids_col, ids_row, slope)
        weights = (dot(rq, rk, NT) * decay).astype(BF16)
        d_scores = (dot(d_mix, value, NT) * decay).astype(BF16)
        enter = ramp(rows, 1.0, 1.0, slope) * link
        d_rq = dot(d_scores, rk, NN) + dot(d_mix, s_ref[0, head], NT) * jnp.concatenate(
            [enter, enter], axis=1
        )
        d_query = d_rq[:, :HEAD_DIM] * cos + d_rq[:, HEAD_DIM:] * sin
        dq_ref[0, :, cols] = (
            d_query.astype(BF16).astype(F32) * swish_slope(q_pre)
        ).astype(BF16)
        d_rk = dot(d_scores, rq, TN)
        dk_ref[0, :, cols] = d_rk[:, :HEAD_DIM] * cos + d_rk[:, HEAD_DIM:] * sin
        dv_ref[0, :, cols] = dot(weights, d_mix, TN)


def state_back_body(
    order, k_ref, v_ref, dk_ref, dv_ref, cos_ref, sin_ref, tail_ref, s_ref, dko_ref, dvo_ref
):
    rows = k_ref.shape[1]
    cos, sin = cos_ref[...], sin_ref[...]
    tail = tail_ref[0]
    for head in range(HEADS):
        cols = columns(head)
        k_pre = k_ref[0, :, cols]
        leave = ramp(rows, rows - 1.0, -1.0, slope_of(head)) * tail
        key = rounded_swish(k_pre) * leave
        rk = turned(key, cos, sin).astype(BF16)
        value = v_ref[0, :, cols].astype(BF16)
        state = s_ref[0, head]
        d_rk = dot(value, state, NT) * jnp.concatenate([leave, leave], axis=1)
        d_key = dk_ref[0, :, cols] + d_rk[:, :HEAD_DIM] * cos + d_rk[:, HEAD_DIM:] * sin
        dko_ref[0, :, cols] = (d_key.astype(BF16).astype(F32) * swish_slope(k_pre)).astype(BF16)
        dvo_ref[0, :, cols] = (dv_ref[0, :, cols] + dot(rk, state, NN)).astype(BF16)


def spread(order, h_ref, out):
    width = h_ref.shape[1] // 8
    for k in range(8):
        out[:, k * width : (k + 1) * width] = h_ref[:, at_block(order, BITS_Y[k], width)]


def row_norm_body(order, x_ref, out, held):
    x = x_ref[...].astype(F32)
    scale = lax.rsqrt(jnp.mean(x * x, axis=-1, keepdims=True) + EPS)
    held[...] = (x * scale).astype(BF16)
    spread(order, held, out)


def head_slope(head):
    return jnp.exp2(-8.0 * (head.astype(F32) + 1.0) / HEADS)


def block_decay(ids_col, ids_row, i, j, size, slope):
    gap = (
        (i - j) * size
        + lax.broadcasted_iota(jnp.int32, (size, size), 0)
        - lax.broadcasted_iota(jnp.int32, (size, size), 1)
    ).astype(F32)
    same = ids_col[i * size : (i + 1) * size] == ids_row[:, j * size : (j + 1) * size]
    keep = same if i > j else same & (gap >= 0.0)
    return jnp.where(keep, jnp.exp(-slope * jnp.maximum(gap, 0.0)), 0.0)


def row_mix_body(size, order, q_ref, k_ref, v_ref, cos_ref, sin_ref, col_ref, row_ref, mix_ref):
    q_ref, k_ref, v_ref = q_ref.at[0], k_ref.at[0], v_ref.at[0]
    cos, sin = cos_ref[...], sin_ref[...]
    col, row = col_ref[...], row_ref[...]
    each = q_ref.shape[1] // HEAD_DIM
    for part in range(each):
        cols = columns(part)
        slope = head_slope(pl.program_id(0) * each + part)
        rq = turned(rounded_swish(q_ref[:, cols]), cos, sin).astype(BF16)
        rk = turned(rounded_swish(k_ref[:, cols]), cos, sin).astype(BF16)
        value = v_ref[:, cols].astype(BF16)
        for i in range(rq.shape[0] // size):
            here = slice(i * size, (i + 1) * size)
            mixed = jnp.zeros((size, HEAD_DIM), F32)
            for j in range(i + 1):
                there = slice(j * size, (j + 1) * size)
                scores = dot(rq[here], rk[there], NT) * block_decay(col, row, i, j, size, slope)
                mixed += dot(scores.astype(BF16), value[there], NN)
            mix_ref[here, cols] = mixed.astype(BF16)


def row_mix_back_body(
    size, order, q_ref, k_ref, v_ref, dm_ref, cos_ref, sin_ref, col_ref, row_ref,
    d_ref,
):
    q_ref, k_ref, v_ref = q_ref.at[0], k_ref.at[0], v_ref.at[0]
    dq_ref, dk_ref, dv_ref = d_ref.at[0, 0], d_ref.at[0, 1], d_ref.at[0, 2]
    cos, sin = cos_ref[...], sin_ref[...]
    col, row = col_ref[...], row_ref[...]
    each = q_ref.shape[1] // HEAD_DIM
    count = q_ref.shape[0] // size
    cut = [slice(i * size, (i + 1) * size) for i in range(count)]

    def back(d_turned, pre, at):
        d = d_turned[:, :HEAD_DIM] * cos[at] + d_turned[:, HEAD_DIM:] * sin[at]
        return (d.astype(BF16).astype(F32) * swish_slope(pre[at])).astype(BF16)

    for part in range(each):
        cols = columns(part)
        slope = head_slope(pl.program_id(0) * each + part)
        q_pre, k_pre = q_ref[:, cols], k_ref[:, cols]
        rq = turned(rounded_swish(q_pre), cos, sin).astype(BF16)
        rk = turned(rounded_swish(k_pre), cos, sin).astype(BF16)
        value = v_ref[:, cols].astype(BF16)
        d_mix = dm_ref[:, cols]
        d_rq = [0.0] * count
        d_rk = [0.0] * count
        d_value = [0.0] * count
        for i in range(count):
            for j in range(i + 1):
                decay = block_decay(col, row, i, j, size, slope)
                scores = (dot(rq[cut[i]], rk[cut[j]], NT) * decay).astype(BF16)
                d_scores = (dot(d_mix[cut[i]], value[cut[j]], NT) * decay).astype(BF16)
                d_value[j] += dot(scores, d_mix[cut[i]], TN)
                d_rq[i] += dot(d_scores, rk[cut[j]], NN)
                d_rk[j] += dot(d_scores, rq[cut[i]], TN)
        for i in range(count):
            dq_ref[cut[i], cols] = back(d_rq[i], q_pre, cut[i])
            dk_ref[cut[i], cols] = back(d_rk[i], k_pre, cut[i])
            dv_ref[cut[i], cols] = d_value[i].astype(BF16)


def stacked(refs):
    return jnp.concatenate([r[...] for r in refs], axis=0)


def restored(order, value, out):
    width = value.shape[1] // 8
    for k, at in enumerate(BITS_Y):
        out[:, at_block(order, at, width)] = value[:, k * width : (k + 1) * width]


def project_body(order, h_ref, *refs):
    h = h_ref[...]
    refs[16][0] = dot(h, stacked(refs[:8]), NN)
    refs[16][1] = dot(h, stacked(refs[8:16]), NN)


def out_mid_body(order, mix_ref, h_in_ref, x_ref, *refs):
    u_ref, gated_ref, mid_ref, h_ref = refs[16:20]
    held = refs[-1]
    mix = mix_ref[...].astype(F32)
    u = dot(h_in_ref[...], stacked(refs[:8]), NN)
    u_ref[...] = u
    scale = lax.rsqrt(jnp.mean(mix * mix, axis=-1, keepdims=True) + EPS)
    held[...] = (mix * scale * (u * sigmoid(u))).astype(BF16)
    spread(order, held, gated_ref)
    mid = x_ref[...].astype(F32) + dot(gated_ref[...], stacked(refs[8:16]), NN)
    mid_ref[...] = mid
    scale = lax.rsqrt(jnp.mean(mid * mid, axis=-1, keepdims=True) + EPS)
    held[...] = (mid * scale).astype(BF16)
    spread(order, held, h_ref)


def left_right_body(order, h_ref, *refs):
    left_ref, right_ref, product_ref = refs[16:]
    h = h_ref[...]
    left = dot(h, stacked(refs[:8]), NN)
    right = dot(h, stacked(refs[8:16]), NN)
    left_ref[...] = left.astype(BF16)
    right_ref[...] = right.astype(BF16)
    product_ref[...] = (left * right).astype(BF16)


def down_grad_body(rows, order, product_ref, c_ref, *refs):
    outs, held, sems = refs[:4], refs[4], refs[5]
    step = pl.program_id(0)
    size = product_ref.shape[1]
    held[pl.ds(pl.multiple_of(step * size, size), size), :] = dot(
        product_ref[...], c_ref[...], TN, BF16
    )

    @pl.when(step == pl.num_programs(0) - 1)
    def _():
        half = held.shape[1] // 2
        copies = []
        for side, bits in enumerate((BITS_X, BITS_Y)):
            for k, bit in enumerate(bits):
                copies.append(
                    pltpu.make_async_copy(
                        held.at[at_block(order, bit, rows), side * half : (side + 1) * half],
                        outs[2 * (k // 4) + side].at[(k % 4) * rows : (k % 4 + 1) * rows, :],
                        sems.at[side, k],
                    )
                )
        run_copies(copies)


def store_apart(g, keep, send, cols, over_x):
    rows = g.shape[0] // 8
    for i, block in enumerate((0, 2, 1, 3) if over_x else (0, 1, 2, 3)):
        place = slice(i * rows, (i + 1) * rows)
        keep[place, cols] = g[block * rows : (block + 1) * rows]
        send[place, cols] = g[(4 + block) * rows : (5 + block) * rows]


def feed_back_body(rows, order, left_ref, right_ref, product_ref, h_ref, c_ref, mid_ref, *refs):
    weights, downs = refs[:16], refs[16:32]
    keep_l, send_l, keep_r, send_r, d_mid_ref, d_branch_ref, act_ref = refs[32:39]
    down, grad, total, held, sems = refs[39:]
    step = pl.program_id(0)

    @pl.when(step == 0)
    def _():
        half = down.shape[1] // 2
        run_copies(
            [
                pltpu.make_async_copy(
                    downs[8 * side + k],
                    down.at[at_block(order, at, rows), side * half : (side + 1) * half],
                    sems.at[side, k],
                )
                for side in range(2)
                for k, at in enumerate(BITS_Y)
            ]
        )
        held[...] = jnp.zeros_like(held)

    size = left_ref.shape[1]
    last = pl.num_programs(0) - 2
    whole = slice(0, size)
    both = held[...]
    g = dot(h_ref[...], both, TN, BF16)
    store_apart(g[:, :size], keep_l, send_l, whole, True)
    store_apart(g[:, size:], keep_r, send_r, whole, False)
    wide = jnp.concatenate([stacked(weights[:8]), stacked(weights[8:])], axis=1)
    grad[...] += dot(both, wide, NT)

    block = jnp.minimum(step, last)
    w_down = down[pl.ds(pl.multiple_of(block * size, size), size), :]
    grad_product = dot(c_ref[...], w_down, NT)
    held[:, :size] = (grad_product * right_ref[...].astype(F32)).astype(BF16)
    held[:, size:] = (grad_product * left_ref[...].astype(F32)).astype(BF16)

    @pl.when(step == 0)
    def _():
        grad[...] = jnp.zeros_like(grad)

    @pl.when(step == pl.num_programs(0) - 1)
    def _():
        mid = mid_ref[...]
        act_ref[...] = (mid + dot(product_ref[...], down[...], NN)).astype(BF16)
        restored(order, grad[...], total)
        g = total[...]
        scale = lax.rsqrt(jnp.mean(mid * mid, axis=-1, keepdims=True) + EPS)
        inner = jnp.mean(g * mid, axis=-1, keepdims=True) * (scale * scale * scale)
        d_mid = c_ref[...].astype(F32) + scale * g - mid * inner
        d_mid_ref[...] = d_mid
        d_branch_ref[...] = d_mid.astype(BF16)


def gate_out_back_body(order, d_ref, mix_ref, u_ref, *refs):
    du_ref, dm_ref, held = refs[8:]
    restored(order, dot(d_ref[...], stacked(refs[:8]), NT), held)
    dg = held[...]
    mix = mix_ref[...].astype(F32)
    u = u_ref[...]
    sig = sigmoid(u)
    scale = lax.rsqrt(jnp.mean(mix * mix, axis=-1, keepdims=True) + EPS)
    du_ref[...] = (dg * mix * scale * (sig * (1.0 + u * (1.0 - sig)))).astype(BF16)
    dn = dg * (u * sig)
    inner = jnp.mean(dn * mix, axis=-1, keepdims=True) * (scale * scale * scale)
    dm_ref[...] = (scale * dn - mix * inner).astype(BF16)


def in_back_body(order, x_ref, d_mid_ref, du_ref, d_ref, *refs):
    low, high, gates, (out, grad, held) = refs[:8], refs[8:16], refs[16:24], refs[24:]
    step = pl.program_id(0)

    @pl.when(step == 0)
    def _():
        grad[...] = dot(du_ref[...], stacked(gates), NT)

    grad[...] += dot(d_ref[0, 0], stacked(low), NT) + dot(d_ref[1, 0], stacked(high), NT)

    @pl.when(step == pl.num_programs(0) - 1)
    def _():
        restored(order, grad[...], held)
        g = held[...]
        x = x_ref[...].astype(F32)
        scale = lax.rsqrt(jnp.mean(x * x, axis=-1, keepdims=True) + EPS)
        inner = jnp.mean(g * x, axis=-1, keepdims=True) * (scale * scale * scale)
        out[...] = (d_mid_ref[...] + scale * g - x * inner).astype(BF16)


def weight_grads_body(order, h_ref, gated_ref, d_ref, du, db, *outs):
    held, sems = outs[4:8], outs[8]
    step = pl.program_id(0)

    def copies(side):
        return [
            pltpu.make_async_copy(held[2 * side + i], outs[2 * side + i], sems.at[2 * side + i])
            for i in range(2)
        ]

    def run(side):
        terms = [(h_ref, d_ref.at[0, i]) for i in range(3)] + [(h_ref, du), (gated_ref, db)]
        for i, (lhs, d) in enumerate(terms):
            g = dot(lhs[...], d[...], TN, BF16)
            cols = slice(i * g.shape[1], (i + 1) * g.shape[1])
            store_apart(g, held[2 * side], held[2 * side + 1], cols, side == 0)
        for copy in copies(side):
            copy.start()

    @pl.when(step == 0)
    def _():
        run(0)

    @pl.when(step == 1)
    def _():
        run(1)
        for copy in copies(0) + copies(1):
            copy.wait()


class Chain:
    def __init__(self, fresh, factor, forward, parts):
        self.fresh, self.factor, self.forward, self.parts = fresh, factor, forward, parts
        self.seqs = fresh.shape[0]
        self.now = [fresh[s] for s in range(self.seqs)]
        self.got = [[] for _ in range(self.seqs)]
        self.turns = self.seqs + parts - 2

    def pass_on(self, s, hop):
        pair = (hop - 1, hop) if self.forward else (self.parts - hop, self.parts - hop - 1)
        self.got[s].append(lax.ppermute(self.now[s], "heads", [pair]))

    def begin(self):
        for s in range(self.seqs):
            self.pass_on(s, 1)

    def at(self, turn):
        return [(s, turn - s) for s in range(self.seqs) if 1 <= turn - s < self.parts]

    def arrivals(self, turn):
        self.new = [self.got[s][hop - 1] for s, hop in self.at(turn)]
        return self, "new"

    def go_on(self, turn):
        for (s, hop), new in zip(self.at(turn), self.new):
            self.got[s][hop - 1] = new
            if hop + 1 < self.parts:
                arrived = new.astype(F32) * self.factor[s][:, None, None]
                self.now[s] = (self.fresh[s].astype(F32) + arrived).astype(BF16)
                self.pass_on(s, hop + 1)

    def result(self):
        return jnp.stack([functools.reduce(lambda a, b: a + b, g) for g in self.got])


class Layer:
    def __init__(self, tokens, doc_lengths, cotangent):
        seqs, length, width = tokens.shape
        self.seqs, self.length, self.width, self.count = seqs, length, width, seqs * length
        self.here = lax.axis_index("rows")
        self.place = lax.axis_index("heads")
        self.order = places(self.here, self.place)
        self.x = tokens.reshape(self.count, width)
        self.dy = cotangent.reshape(self.count, width)

        ends = jnp.cumsum(doc_lengths, axis=-1, dtype=jnp.int32)[:, :-1]

        def ids_at(where):
            return jnp.sum((where[None, :, None] >= ends[:, None, :]).astype(jnp.int32), axis=-1)

        start = self.place * length
        positions = start + jnp.arange(length, dtype=jnp.int32)
        ids = ids_at(positions)
        before = jnp.where(self.place > 0, ids_at(jnp.reshape(start - 1, (1,))), -1)
        final = ids[:, -1:]
        link = (ids == before).astype(F32)[:, :, None]
        tail = (ids == final).astype(F32)[:, :, None]
        slopes = jnp.array([slope_of(h) for h in range(HEADS)], F32)
        self.factor = (final == before).astype(F32) * jnp.exp(-slopes * length)[None, :]
        theta = jnp.exp(-math.log(10000.0) * jnp.arange(HEAD_DIM, dtype=F32) / HEAD_DIM)
        angle = positions.astype(F32)[:, None] * theta[None, :]

        table = pl.BlockSpec((length, HEAD_DIM), lambda s, *_: (0, 0))
        one_col = pl.BlockSpec((1, length, 1), lambda s, *_: (s, 0, 0))
        one_row = pl.BlockSpec((1, 1, length), lambda s, *_: (s, 0, 0))
        self.turn = [(jnp.cos(angle), table), (jnp.sin(angle), table)]
        self.link = link, one_col
        self.tail = tail, one_col
        self.masks = [(ids[:, :, None], one_col), (ids[:, None, :], one_row), self.link]
        self.seq = pl.BlockSpec((1, length, width), lambda s, *_: (s, 0, 0))
        self.state = pl.BlockSpec(
            (1, HEADS, 2 * HEAD_DIM, HEAD_DIM), lambda s, *_: (s, 0, 0, 0)
        )
        self.states = (seqs, HEADS, 2 * HEAD_DIM, HEAD_DIM), BF16, self.state
        step = min(self.count, 256)
        self.grid = (self.count // step,)
        self.wide = rows_spec(step, width)

    def rows(self, body, ins, types, order=None):
        return call(
            body, self.grid, self.order, [(a, self.wide) for a in ins],
            [((self.count, self.width), t, self.wide) for t in types],
        )

    def seqwise(self, body, ins, outs):
        shape = (self.seqs, self.length, self.width)
        ins = [i if isinstance(i, tuple) else (i.reshape(shape), self.seq) for i in ins]
        outs = [o if isinstance(o, tuple) else (shape, o, self.seq) for o in outs]
        got = call(body, (self.seqs,), self.order, ins, outs)
        return [g.reshape(self.count, self.width) if g.shape == shape else g for g in got]

    def norm(self):
        return self.rows(norm_body, [self.x], [BF16])

    def fresh(self, k_pre, v_pre):
        return self.seqwise(fresh_body, [k_pre, v_pre] + self.turn + [self.tail], [self.states])[0]

    def mix(self, q_pre, k_pre, v_pre, u_pre, state_in):
        ins = [q_pre, k_pre, v_pre, u_pre] + self.turn + self.masks + [(state_in, self.state)]
        return self.seqwise(mix_body, ins, [BF16, BF16])

    def mid(self, branch):
        return self.rows(mid_body, [self.x, branch], [F32, BF16])

    def mid_back(self, x_mid, grad):
        return self.rows(norm_back_body, [x_mid, self.dy, grad], [F32, BF16])

    def in_back(self, d_mid, grad):
        return self.rows(norm_back_body, [self.x, d_mid, grad], [F32])[0]

    def gate_back(self, q_pre, u_pre, mix, d_gated):
        ins = [q_pre, u_pre, mix, d_gated] + self.turn + [self.link]
        return self.seqwise(gate_back_body, ins, [BF16, BF16, self.states])

    def mix_back(self, q_pre, k_pre, v_pre, d_mix, state_in):
        ins = [q_pre, k_pre, v_pre, d_mix] + self.turn + self.masks + [(state_in, self.state)]
        return self.seqwise(mix_back_body, ins, [BF16, F32, F32])

    def state_back(self, k_pre, v_pre, dk_near, dv_near, d_state):
        ins = [k_pre, v_pre, dk_near, dv_near] + self.turn + [self.tail, (d_state, self.state)]
        return self.seqwise(state_back_body, ins, [BF16, BF16])


def plainly(layer, heads_count, weights):
    w_query, w_key, w_value, w_gate, w_out, w_left, w_right, w_down = (
        lax.all_gather(w, "rows", axis=0, tiled=True) for w in weights
    )

    def carried(fresh, forward):
        chain = Chain(fresh, layer.factor, forward, heads_count)
        chain.begin()
        for turn in range(1, chain.turns + 1):
            chain.arrivals(turn)
            chain.go_on(turn)
        return chain.result()

    def gradient(lhs, d):
        total = lax.psum_scatter(dot(lhs, d, TN, BF16), "rows", scatter_dimension=0, tiled=True)
        return lax.psum_scatter(total, "heads", scatter_dimension=1, tiled=True).astype(F32)

    (h_in,) = layer.norm()
    q_pre, k_pre, v_pre, u_pre = (
        dot(h_in, w, NN) for w in (w_query, w_key, w_value, w_gate)
    )
    state_in = carried(layer.fresh(k_pre, v_pre), True)
    mix, gated = layer.mix(q_pre, k_pre, v_pre, u_pre, state_in)
    x_mid, h_mid = layer.mid(dot(gated, w_out, NN))
    left, right = dot(h_mid, w_left, NN), dot(h_mid, w_right, NN)
    product = (left * right).astype(BF16)
    activations = (x_mid + dot(product, w_down, NN)).astype(BF16)
    grad_product = dot(layer.dy, w_down, NT)
    d_left = (grad_product * right).astype(BF16)
    d_right = (grad_product * left).astype(BF16)
    d_mid, d_branch = layer.mid_back(
        x_mid, dot(d_left, w_left, NT) + dot(d_right, w_right, NT)
    )
    d_u, d_mix, d_fresh = layer.gate_back(q_pre, u_pre, mix, dot(d_branch, w_out, NT))
    d_state = carried(d_fresh, False)
    d_q, dk_near, dv_near = layer.mix_back(q_pre, k_pre, v_pre, d_mix, state_in)
    d_k, d_v = layer.state_back(k_pre, v_pre, dk_near, dv_near, d_state)
    grad_in = (
        dot(d_q, w_query, NT) + dot(d_u, w_gate, NT) + dot(d_k, w_key, NT) + dot(d_v, w_value, NT)
    )
    input_grad = layer.in_back(d_mid, grad_in)
    pairs = (
        (h_in, d_q), (h_in, d_k), (h_in, d_v), (h_in, d_u), (gated, d_branch),
        (h_mid, d_left), (h_mid, d_right), (product, layer.dy),
    )
    return (activations, input_grad) + tuple(gradient(lhs, d) for lhs, d in pairs)


class Row:
    def __init__(self, doc_lengths, length, width, here, head):
        self.length, self.width = length, width
        self.order = places(here, head)
        lengths = lax.dynamic_index_in_dim(doc_lengths, head, 0, keepdims=False)
        ends = jnp.cumsum(lengths, dtype=jnp.int32)[:-1]
        positions = jnp.arange(length, dtype=jnp.int32)
        ids = jnp.sum((positions[:, None] >= ends[None, :]).astype(jnp.int32), axis=-1)
        theta = jnp.exp(-math.log(10000.0) * jnp.arange(HEAD_DIM, dtype=F32) / HEAD_DIM)
        angle = positions.astype(F32)[:, None] * theta[None, :]

        def whole(rows, cols):
            return pl.BlockSpec((rows, cols), lambda *_: (0, 0))

        table = whole(length, HEAD_DIM)
        self.extra = [
            (jnp.cos(angle), table), (jnp.sin(angle), table),
            (ids[:, None], whole(length, 1)), (ids[None, :], whole(1, length)),
        ]
        self.heads = pl.BlockSpec((length, 2 * HEAD_DIM), lambda h, *_: (0, h))
        self.wide = rows_spec(min(length, 256), width)
        self.all = whole(length, width)
        self.block = math.gcd(length, 256)
        self.flops = 2 * length * width * width

    def norm(self, x):
        return self.by_rows(row_norm_body, [(x, self.wide)], [], [BF16], [BF16])

    def pieces(self, group, half, width=None):
        rows, whole = group.pieces[half].shape
        spec = pl.BlockSpec((rows, width or whole), lambda i, *_: (0, i if width else 0))
        return [(a, spec) for a in group.all(half)]

    def thirds(self, which=None, dtype=F32):
        half = self.width // 2
        if which is None:
            return pl.BlockSpec((2, self.length, half), lambda i, *_: (0, 0, i))
        pair = 2 * HEAD_DIM
        each = half // pair
        return pl.BlockSpec(
            (1, self.length, pair), lambda i, *_: (i // each, 0, which * each + i % each)
        )

    def project(self, h, qkv):
        half = self.width // 2
        return call(
            project_body, (3,), self.order,
            [(h, self.all)] + self.pieces(qkv, 0, half) + self.pieces(qkv, 1, half),
            [((2, self.length, 3 * half), F32, self.thirds())], flops=3 * self.flops,
        )[0]

    def column(self, block, offset=0):
        return pl.BlockSpec((self.length, block), lambda i, *_: (0, offset + i))

    def mix(self, pre):
        return call(
            functools.partial(row_mix_body, self.block), (HEADS // 2,), self.order,
            [(pre, self.thirds(i)) for i in range(3)] + self.extra,
            [((self.length, self.width), BF16, self.heads)], flops=self.flops * 3 // 8,
        )[0]

    def mix_back(self, pre, d_mix):
        pair, half = 2 * HEAD_DIM, self.width // 2
        each = half // pair
        spec = pl.BlockSpec((1, 3, self.length, pair), lambda i, *_: (i // each, 0, 0, i % each))
        return call(
            functools.partial(row_mix_back_body, self.block), (HEADS // 2,), self.order,
            [(pre, self.thirds(i)) for i in range(3)] + [(d_mix, self.heads)] + self.extra,
            [((2, 3, self.length, half), BF16, spec)], flops=self.flops,
        )[0]

    def by_rows(self, body, ins, weights, types, scratch):
        step = self.wide.block_shape[0]
        return call(
            body, (self.length // step,), self.order, ins + weights,
            [((self.length, self.width), t, self.wide) for t in types],
            scratch=[pltpu.VMEM((step, self.width), t) for t in scratch], flops=self.flops,
        )

    def out_mid(self, mix, h, x, uo):
        return self.by_rows(
            out_mid_body, [(mix, self.wide), (h, self.wide), (x, self.wide)],
            self.pieces(uo, 0) + self.pieces(uo, 1),
            [F32, BF16, F32, BF16], [BF16],
        )

    def gate_out_back(self, d_branch, mix, u_pre, uo):
        return self.by_rows(
            gate_out_back_body, [(d_branch, self.wide), (mix, self.wide), (u_pre, self.wide)],
            self.pieces(uo, 1), [BF16, BF16], [F32],
        )

    def left_right(self, h, ff):
        inner = ff.pieces[0].shape[1]
        block = math.gcd(inner, 1408)
        return call(
            left_right_body, (inner // block,), self.order,
            [(h, self.all)] + self.pieces(ff, 0, block) + self.pieces(ff, 1, block),
            [((self.length, inner), BF16, self.column(block))] * 3,
            flops=2 * self.flops * inner // self.width,
        )

    def down_grad(self, product, c):
        inner, half = product.shape[1], self.width // 2
        block = math.gcd(inner, 1408)
        rows = inner // 8
        got = call(
            functools.partial(down_grad_body, rows), (inner // block,), self.order,
            [(product, self.column(block)), (c, self.all)], [((4 * rows, half), BF16, HBM)] * 4,
            scratch=[pltpu.VMEM((inner, self.width), BF16), pltpu.SemaphoreType.DMA((2, 8))],
            flops=self.flops * inner // self.width,
        )
        return Reduce(self.order, got[2:], got[:2], [2, 4])

    def feed_back(self, left, right, product, h, c, x_mid, ff, down):
        inner, rows = ff.pieces[0].shape[1], down.pieces[0].shape[0]
        block = math.gcd(inner, 256)
        steps = inner // block

        def now(rows):
            return pl.BlockSpec((rows, block), lambda i, *_: (0, jnp.minimum(i, steps - 1)))

        def before(rows):
            return pl.BlockSpec((rows, block), lambda i, *_: (0, jnp.maximum(i - 1, 0)))

        full = (self.length, self.width)
        weights = [(a, before(ff.pieces[0].shape[0])) for a in ff.all(0) + ff.all(1)]
        return call(
            functools.partial(feed_back_body, rows), (steps + 1,), self.order,
            [(left, now(self.length)), (right, now(self.length))]
            + [(product, whole_spec(self.length, inner))]
            + [(a, self.all) for a in (h, c, x_mid)]
            + weights + [(a, HBM) for a in down.all(0) + down.all(1)],
            [((self.width // 2, inner), BF16, before(self.width // 2))] * 4
            + [(full, F32, self.all), (full, BF16, self.all), (full, BF16, self.all)],
            scratch=[pltpu.VMEM((inner, self.width), BF16)] + [pltpu.VMEM(full, F32)] * 2
            + [pltpu.VMEM((self.length, 2 * block), BF16), pltpu.SemaphoreType.DMA((2, 8))],
            flops=6 * self.flops * inner // self.width,
        )

    def in_back(self, x, d_mid, d, d_u, qkv, uo):
        half = self.width // 2
        full = (self.length, self.width)
        third = pl.BlockSpec((2, 1, self.length, half), lambda i, *_: (0, i, 0, 0))
        return call(
            in_back_body, (3,), self.order,
            [(x, self.all), (d_mid, self.all), (d_u, self.all), (d, third)]
            + self.pieces(qkv, 0, half) + self.pieces(qkv, 1, half) + self.pieces(uo, 0),
            [(full, BF16, self.all)], scratch=[pltpu.VMEM(full, F32)] * 2, flops=4 * self.flops,
        )[0]

    def weight_grads(self, h, gated, d, d_u, d_branch):
        half = self.width // 2
        shape = (half, 5 * half)
        thirds = pl.BlockSpec((1, 3, self.length, half), lambda i, *_: (i, 0, 0, 0))
        got = call(
            weight_grads_body, (2,), self.order,
            [(h, self.all), (gated, self.all)]
            + [(d, thirds), (d_u, self.column(half)), (d_branch, self.column(half))],
            [(shape, BF16, HBM)] * 4,
            scratch=[pltpu.VMEM(shape, BF16)] * 4 + [pltpu.SemaphoreType.DMA((4,))],
            flops=5 * self.flops,
        )
        return Reduce(self.order, got[1::2], got[::2], [2, 4])


def stepwise(tokens, doc_lengths, cotangent, weights):
    w_query, w_key, w_value, w_gate, w_out, w_left, w_right, w_down = weights
    size, width = tokens.shape[1:]
    length, half = 4 * size, width // 2
    here, head = lax.axis_index("rows"), lax.axis_index("heads")
    row = Row(doc_lengths, length, width, here, head)
    order = row.order
    v = types.SimpleNamespace()
    clock = Clock(order)
    tick = clock.tick

    def exchanged(a):
        return lax.all_to_all(a.reshape(4, size, width), "heads", 0, 0, tiled=True)

    def whole_row(a):
        return exchanged(a).reshape(length, width)

    inner = w_left.shape[1]
    uo = Gather([w_gate, w_out])
    uo.first()
    qkv = Gather(
        pack(order, [w_query, w_key, w_value], [[(i, at, half) for i in range(3)] for at in (0, half)])
    )
    qkv.first()
    v.x = whole_row(after(tokens, uo.near_x[0]))
    v.extra = [a for a, _ in row.extra]
    ff = Gather([w_left, w_right])
    v.c = cotangent
    tick((qkv, "near_x"), (qkv, "near_y"), (uo, "near_x"), (uo, "near_y"), (uo, "pieces"), (v, "c"), (v, "extra"))
    row.extra = [(a, spec) for a, (_, spec) in zip(v.extra, row.extra)]
    qkv.second()
    uo.second()
    qkv.cross("pieces", "near_x", "near_y")
    uo.cross("pieces", "near_x", "near_y")
    (v.h,) = row.norm(v.x)
    tick((qkv, "far"), (uo, "far"), (v, "h"), (ff, "pieces"))
    ff.first()
    ff.cross("pieces")
    qkv.cross("far")
    uo.cross("far")
    v.pre = row.project(v.h, qkv)
    v.mix = row.mix(v.pre)
    v.u_pre, v.gated, v.x_mid, v.h_mid = row.out_mid(v.mix, v.h, v.x, uo)
    v.down = w_down
    tick((v, "x_mid"), (v, "h_mid"), (ff, "near_x"), (ff, "near_y"), (v, "down"), (v, "c"))
    ff.second()
    v.c = whole_row(v.c)
    ff.cross("near_x", "near_y")
    v.down = pack(order, [v.down], [[(0, 0, half)], [(0, half, half)]])
    tick((ff, "far"), (v, "down"))
    down = Gather(v.down)
    ff.cross("far")
    down.first()
    down.cross("pieces")

    v.left, v.right, v.product = row.left_right(v.h_mid, ff)
    tick((v, "left"), (v, "right"), (v, "product"), (down, "near_x"), (down, "near_y"), (v, "c"))
    down.second()
    down.cross("near_x", "near_y")
    v.g_down = dot(v.product, v.c, TN, BF16)
    tick((v, "g_down"), (down, "far"), (v, "left"))
    v.sum_down = lax.psum_scatter(v.g_down, "rows", scatter_dimension=0, tiled=True)
    down.cross("far")
    tick((down, "far_other"), (v, "left"))
    keep_l, send_l, keep_r, send_r, v.d_mid, v.d_branch, v.act = row.feed_back(
        v.left, v.right, v.product, v.h_mid, v.c, v.x_mid, ff, down
    )
    r_ff = Reduce(order, [send_l, send_r], [keep_l, keep_r], [2, 4])
    tick((r_ff, "sends"), (v, "d_mid"), (v, "d_branch"), (v, "act"))
    r_ff.core()
    v.d_u, v.d_mix = row.gate_out_back(v.d_branch, v.mix, v.u_pre, uo)
    tick((r_ff, "theirs"), (v, "d_u"), (v, "d_mix"))
    r_ff.join()
    tick((r_ff, "totals"), (v, "act"), (v, "d_mix"))
    r_ff.first()
    v.act = exchanged(v.act)
    v.d = row.mix_back(v.pre, v.d_mix)
    tick((v, "d"))
    v.back = row.in_back(v.x, v.d_mid, v.d, v.d_u, qkv, uo)
    tick((v, "back"), (v, "d"), (v, "act"))
    r_att = row.weight_grads(v.h, v.gated, v.d, v.d_u, v.d_branch)
    tick((r_att, "sends"), (r_ff, "got"), (v, "sum_down"))
    r_att.core()
    r_ff.join_first()
    tick((r_att, "theirs"), (r_ff, "parts"), (v, "sum_down"), (v, "back"))
    r_ff.second()
    r_att.join()
    sum_down = after(v.sum_down, *r_att.totals)
    s_down = Settle(order, [[sum_down]], half // 2, [lambda z: z * (half // 2)])
    v.back = exchanged(after(v.back, *r_att.totals))
    tick((r_att, "totals"), (r_ff, "got_last"), (s_down, "out"))
    r_att.first()
    s_down.first()
    quarter = inner // 4
    s_ff = r_ff.settle(quarter, [lambda z: z * quarter, lambda z: inner + z * quarter])
    tick((s_ff, "out"), (s_down, "got"))
    s_ff.first()
    s_down.join()
    tick((s_down, "out"), (v, "back"))
    v.back = v.back.astype(F32)
    tick((s_down, "out"), (s_down, "last"), (s_ff, "got"), (v, "back"))
    s_down.second()
    s_ff.join()
    tick((s_ff, "out"), (s_ff, "last"), (r_att, "got"))
    s_ff.second()
    r_att.join_first()
    tick((r_att, "parts"), (s_down, "got_near"), (s_down, "got_far"))
    r_att.second()
    (v.g_down,) = s_down.result()
    tick((r_att, "got_last"), (v, "g_down"))
    s_att = r_att.settle(
        half // 2,
        [
            lambda z, i=i: (z // 2) * 5 * half + i * half + (z % 2) * (half // 2)
            for i in range(5)
        ],
    )
    tick((s_att, "out"), (s_ff, "got_near"), (s_ff, "got_far"))
    s_att.first()
    v.g_ff = s_ff.result()
    tick((s_att, "got"), (v, "g_ff"))
    s_att.join()
    tick((s_att, "out"), (s_att, "last"))
    s_att.second()
    g_query, g_key, g_value, g_gate, g_out = s_att.result()
    g_left, g_right = v.g_ff
    return (
        v.act, v.back, g_query, g_key, g_value, g_gate, g_out, g_left, g_right, v.g_down
    )


def on_device(rows_count, heads_count, tokens, doc_lengths, cotangent, *weights):
    if rows_count == 8 and heads_count == 4 and tokens.shape[0] == 4:
        return stepwise(tokens, doc_lengths, cotangent, weights)
    layer = Layer(tokens, doc_lengths, cotangent)
    activations, input_grad, *grads = plainly(layer, heads_count, weights)
    return (activations.reshape(tokens.shape), input_grad.reshape(tokens.shape), *grads)


def solution(mesh):
    sizes = dict(mesh.shape)
    tokens = P("rows", "heads", None)
    weights = P("rows", None)
    grads = P("rows", "heads")
    return jax.shard_map(
        functools.partial(on_device, sizes["rows"], sizes["heads"]),
        mesh=mesh,
        in_specs=(tokens, weights, tokens) + (weights,) * 8,
        out_specs=(tokens, tokens) + (grads,) * 8,
        check_vma=False,
    )
```

```python
import functools
import math
import types

import jax
import jax.numpy as jnp
from jax import lax
from jax.experimental import pallas as pl
from jax.experimental.pallas import tpu as pltpu
from jax.sharding import PartitionSpec as P

HEADS = 8
HEAD_DIM = 128
EPS = 1e-06
F32 = jnp.float32
BF16 = jnp.bfloat16
VMEM_LIMIT = 54 << 20

BITS = (0, 2, 4, 6, 1, 3, 5, 7)
BITS_X = (0, 4, 2, 6, 1, 5, 3, 7)
BITS_Y = (0, 2, 4, 6, 1, 3, 5, 7)


def after(value, *others):
    return lax.optimization_barrier((value,) + others)[0]


def dot(a, b, dims, out=F32):
    return lax.dot_general(a, b, (dims, ((), ())), preferred_element_type=F32).astype(out)


NN = ((1,), (0,))
NT = ((1,), (1,))
TN = ((0,), (0,))


def swap(value, bit, size):
    return lax.ppermute(value, "rows", [(i, i ^ bit) for i in range(size)])


def swap_heads(value, bit):
    return lax.ppermute(value, "heads", [(i, i ^ bit) for i in range(4)])


HBM = pl.BlockSpec(memory_space=pltpu.HBM)


def whole_spec(rows, width):
    return pl.BlockSpec((rows, width), lambda i, *_: (0, 0))


def run_copies(copies):
    for copy in copies:
        copy.start()
    for copy in copies:
        copy.wait()


def pack(order, arrays, lists):
    rows = arrays[0].shape[0]
    widths = [sum(w for _, _, w in parts) for parts in lists]
    most = max(len(parts) for parts in lists)

    def body(order, *refs):
        ins, outs, sems = refs[: len(arrays)], refs[len(arrays) : -1], refs[-1]
        copies = []
        for j, parts in enumerate(lists):
            at = 0
            for i, (which, begin, width) in enumerate(parts):
                copies.append(
                    pltpu.make_async_copy(
                        ins[which].at[:, begin : begin + width],
                        outs[j].at[:, at : at + width],
                        sems.at[j, i],
                    )
                )
                at += width
        run_copies(copies)

    return call(
        body, (1,), order, [(a, HBM) for a in arrays],
        [((rows, w), BF16, whole_spec(rows, w)) for w in widths],
        scratch=[pltpu.SemaphoreType.DMA((len(lists), most))],
    )


class Clock:
    def __init__(self, start):
        self.token = start

    def tick(self, *places):
        held = [getattr(o, n) for o, n in places]
        held, self.token = lax.optimization_barrier((held, self.token))
        for (o, n), value in zip(places, held):
            setattr(o, n, value)


def places(here, head):
    return jnp.stack([here ^ b for b in range(8)] + [head ^ b for b in range(4)]).astype(jnp.int32)


class Gather:
    def __init__(self, pieces):
        self.pieces = list(pieces)
        self.near_x, self.near_y = [None, None], [None, None]

    def first(self, *halves):
        for half in halves or (0, 1):
            self.near_x[half] = swap(self.pieces[half], 2, 8)
            self.near_y[half] = swap(self.pieces[half], 4, 8)

    def second(self):
        self.far = [swap(self.near_x[0], 4, 8), swap(self.near_y[1], 2, 8)]

    def cross(self, *names):
        for name in names:
            setattr(self, name + "_other", [swap(p, 1, 8) for p in getattr(self, name)])

    def all(self, half):
        names = ("pieces", "near_x", "near_y", "far")
        return [getattr(self, n + core)[half] for core in ("", "_other") for n in names]


def added(*terms):
    return functools.reduce(lambda a, b: a + b, [t.astype(F32) for t in terms]).astype(BF16)


class Reduce:
    def __init__(self, order, sends, keeps, bits):
        self.order, self.sends, self.keeps, self.bits = order, list(sends), list(keeps), list(bits)

    def core(self):
        self.theirs = [swap(s, 1, 8) for s in self.sends]

    def joined(self, quarter, *more):
        rows = self.keeps[0].shape[0] // 4
        place = slice(quarter * rows, (quarter + 1) * rows)
        return [
            added(k[place], t[place], *m) for k, t, *m in zip(self.keeps, self.theirs, *more)
        ]

    def join_far(self):
        self.far = self.joined(3)

    def join_near(self):
        self.near = self.joined(2)

    def first_far(self):
        self.got_far = [swap(t, b, 8) for t, b in zip(self.far, self.bits)]

    def first_near(self):
        self.got_near = [swap(t, b, 8) for t, b in zip(self.near, self.bits)]

    def join_first(self):
        self.parts = self.joined(1, self.got_far)

    def join(self):
        half = self.keeps[0].shape[0] // 2
        self.both = [added(k[half:], t[half:]) for k, t in zip(self.keeps, self.theirs)]

    def first(self):
        self.got_near = [swap(t, b, 8) for t, b in zip(self.both, self.bits)]

    def join_first_both(self):
        rows = self.keeps[0].shape[0] // 4
        self.parts = self.joined(1, [g[rows:] for g in self.got_near])

    def second(self):
        self.got_last = [swap(p, 6 - b, 8) for p, b in zip(self.parts, self.bits)]

    def settle(self, block, starts):
        parts = zip(self.keeps, self.theirs, self.got_near, self.got_last)
        return Settle(self.order, [list(p) for p in parts], block, starts)


class Settle:
    def __init__(self, order, parts, block, starts):
        self.order, self.block, self.count = order, block, len(starts)
        rows = self.rows = parts[0][-1].shape[0]
        widths = [p[-1].shape[1] for p in parts]
        counts = [len(p) for p in parts]

        def body(order, *refs):
            *results, held = refs[sum(counts) :]
            owns, outs = results[:2], results[2:]
            at, first = 0, 0
            for width, count in zip(widths, counts):
                total = refs[first][...].astype(F32)
                for ref in refs[first + 1 : first + count]:
                    total += ref[...].astype(F32)
                held[:, at : at + width] = total
                at, first = at + width, first + count
            for z in range(4):

                @pl.when(order[8] == z)
                def _(z=z):
                    for i, start in enumerate(starts):
                        for j, (mine, theirs) in enumerate(((0, 1), (2, 3))):
                            mine, theirs = start(z ^ mine), start(z ^ theirs)
                            owns[j][i] = held[:, mine : mine + block]
                            outs[j][i] = held[:, theirs : theirs + block].astype(BF16)

        shape = (self.count, rows, block)
        spec = pl.BlockSpec((self.count, rows // 2, block), lambda i, *_: (0, i, 0))
        self.own, self.far, self.last, self.out = call(
            body, (2,), order,
            [(a, pl.BlockSpec((rows // 2, a.shape[1]), lambda i, *_: (i, 0))) for p in parts for a in p],
            [(shape, F32, spec)] * 2 + [(shape, BF16, spec)] * 2,
            scratch=[pltpu.VMEM((rows // 2, sum(widths)), F32)],
        )

    def first(self):
        self.got = swap_heads(self.out, 1)

    def join(self):
        self.out = (self.far + self.got.astype(F32)).astype(BF16)

    def second(self):
        self.got_far = swap_heads(self.out, 2)
        self.got_near = swap_heads(self.last, 1)

    def result(self):
        return [
            self.own[i] + self.got_near[i].astype(F32) + self.got_far[i].astype(F32)
            for i in range(self.count)
        ]


def at_block(order_ref, index, width):
    return pl.ds(pl.multiple_of(order_ref[index] * width, width), width)


def sigmoid(v):
    return 1.0 / (1.0 + jnp.exp(-v))


def swish_slope(v):
    sig = sigmoid(v)
    return sig * (1.0 + v * (1.0 - sig))


def call(body, grid, order, ins, outs, scratch=(), flops=0):
    moved = sum(a.size * a.dtype.itemsize for a, _ in ins) + sum(
        math.prod(s) * jnp.dtype(t).itemsize for s, t, _ in outs
    )
    return pl.pallas_call(
        body,
        grid_spec=pltpu.PrefetchScalarGridSpec(
            num_scalar_prefetch=1,
            grid=grid,
            in_specs=[spec for _, spec in ins],
            out_specs=[spec for _, _, spec in outs],
            scratch_shapes=list(scratch),
        ),
        out_shape=[jax.ShapeDtypeStruct(s, t) for s, t, _ in outs],
        compiler_params=pltpu.CompilerParams(vmem_limit_bytes=VMEM_LIMIT),
        cost_estimate=pl.CostEstimate(flops=flops // 4, bytes_accessed=moved // 4, transcendentals=0),
    )(order, *[a for a, _ in ins])


def rows_spec(count, width, column=0):
    return pl.BlockSpec((count, width), lambda i, *_: (i, column))


def norm_body(order, x_ref, h_ref):
    x = x_ref[...].astype(F32)
    scale = lax.rsqrt(jnp.mean(x * x, axis=-1, keepdims=True) + EPS)
    h_ref[...] = (x * scale).astype(BF16)


def mid_body(order, x_ref, b_ref, mid_ref, h_ref):
    mid = x_ref[...].astype(F32) + b_ref[...]
    mid_ref[...] = mid
    scale = lax.rsqrt(jnp.mean(mid * mid, axis=-1, keepdims=True) + EPS)
    h_ref[...] = (mid * scale).astype(BF16)


def norm_back_body(order, v_ref, base_ref, g_ref, *outs):
    v = v_ref[...].astype(F32)
    g = g_ref[...]
    scale = lax.rsqrt(jnp.mean(v * v, axis=-1, keepdims=True) + EPS)
    inner = jnp.mean(g * v, axis=-1, keepdims=True) * (scale * scale * scale)
    total = base_ref[...].astype(F32) + scale * g - v * inner
    outs[0][...] = total
    if len(outs) > 1:
        outs[1][...] = total.astype(BF16)


def ramp(rows, start, sign, slope):
    place = lax.broadcasted_iota(jnp.int32, (rows, HEAD_DIM), 0).astype(F32)
    return jnp.exp(-slope * (start + sign * place))


def decays(ids_col, ids_row, slope):
    rows = ids_col.shape[0]
    gap = (
        lax.broadcasted_iota(jnp.int32, (rows, rows), 0)
        - lax.broadcasted_iota(jnp.int32, (rows, rows), 1)
    ).astype(F32)
    keep = (gap >= 0.0) & (ids_col == ids_row)
    return jnp.where(keep, jnp.exp(-slope * jnp.maximum(gap, 0.0)), 0.0)


def slope_of(head):
    return 2.0 ** (-8.0 * (head + 1) / HEADS)


def columns(head):
    return slice(head * HEAD_DIM, (head + 1) * HEAD_DIM)


def turned(a, cos, sin):
    return jnp.concatenate([a * cos, a * sin], axis=1)


def rounded_swish(v):
    return (v * sigmoid(v)).astype(BF16).astype(F32)


def fresh_body(order, k_ref, v_ref, cos_ref, sin_ref, tail_ref, state_ref):
    rows = k_ref.shape[1]
    cos, sin = cos_ref[...], sin_ref[...]
    tail = tail_ref[0]
    for head in range(HEADS):
        key = rounded_swish(k_ref[0, :, columns(head)])
        key = key * (ramp(rows, rows - 1.0, -1.0, slope_of(head)) * tail)
        value = v_ref[0, :, columns(head)].astype(BF16)
        state_ref[0, head] = dot(turned(key, cos, sin).astype(BF16), value, TN, BF16)


def mix_body(
    order, q_ref, k_ref, v_ref, u_ref, cos_ref, sin_ref, col_ref, row_ref, link_ref, s_ref,
    mix_ref, gated_ref,
):
    rows = q_ref.shape[1]
    cos, sin = cos_ref[...], sin_ref[...]
    ids_col, ids_row = col_ref[0], row_ref[0]
    link = link_ref[0]
    power = jnp.zeros((rows, 1), F32)
    for head in range(HEADS):
        cols = columns(head)
        slope = slope_of(head)
        rq = turned(rounded_swish(q_ref[0, :, cols]), cos, sin).astype(BF16)
        rk = turned(rounded_swish(k_ref[0, :, cols]), cos, sin).astype(BF16)
        value = v_ref[0, :, cols].astype(BF16)
        weights = (dot(rq, rk, NT) * decays(ids_col, ids_row, slope)).astype(BF16)
        mixed = dot(weights, value, NN) + dot(rq, s_ref[0, head], NN) * (
            ramp(rows, 1.0, 1.0, slope) * link
        )
        mixed = mixed.astype(BF16)
        mix_ref[0, :, cols] = mixed
        mixed = mixed.astype(F32)
        power += jnp.sum(mixed * mixed, axis=-1, keepdims=True)
    scale = lax.rsqrt(power / (HEADS * HEAD_DIM) + EPS)
    for head in range(HEADS):
        cols = columns(head)
        u = u_ref[0, :, cols]
        gated_ref[0, :, cols] = (
            mix_ref[0, :, cols].astype(F32) * scale * (u * sigmoid(u))
        ).astype(BF16)


def gate_back_body(
    order, q_ref, u_ref, mix_ref, dg_ref, cos_ref, sin_ref, link_ref, du_ref, dm_ref, state_ref
):
    rows = q_ref.shape[1]
    cos, sin = cos_ref[...], sin_ref[...]
    link = link_ref[0]
    mix = mix_ref[0].astype(F32)
    scale = lax.rsqrt(jnp.mean(mix * mix, axis=-1, keepdims=True) + EPS)
    inner = jnp.zeros((rows, 1), F32)
    for head in range(HEADS):
        cols = columns(head)
        u = u_ref[0, :, cols]
        part = mix_ref[0, :, cols].astype(F32)
        dg = dg_ref[0, :, cols]
        sig = sigmoid(u)
        inner += jnp.sum(dg * (u * sig) * part, axis=-1, keepdims=True)
        du_ref[0, :, cols] = (dg * part * scale * (sig * (1.0 + u * (1.0 - sig)))).astype(BF16)
    inner = inner * (scale * scale * scale) / (HEADS * HEAD_DIM)
    for head in range(HEADS):
        cols = columns(head)
        u = u_ref[0, :, cols]
        part = mix_ref[0, :, cols].astype(F32)
        dg = dg_ref[0, :, cols]
        d_mix = (scale * (dg * (u * sigmoid(u))) - part * inner).astype(BF16)
        dm_ref[0, :, cols] = d_mix
        query = rounded_swish(q_ref[0, :, cols]) * (
            ramp(rows, 1.0, 1.0, slope_of(head)) * link
        )
        state_ref[0, head] = dot(turned(query, cos, sin).astype(BF16), d_mix, TN, BF16)


def mix_back_body(
    order, q_ref, k_ref, v_ref, dm_ref, cos_ref, sin_ref, col_ref, row_ref, link_ref, s_ref,
    dq_ref, dk_ref, dv_ref,
):
    rows = q_ref.shape[1]
    cos, sin = cos_ref[...], sin_ref[...]
    ids_col, ids_row = col_ref[0], row_ref[0]
    link = link_ref[0]
    for head in range(HEADS):
        cols = columns(head)
        slope = slope_of(head)
        q_pre = q_ref[0, :, cols]
        rq = turned(rounded_swish(q_pre), cos, sin).astype(BF16)
        rk = turned(rounded_swish(k_ref[0, :, cols]), cos, sin).astype(BF16)
        value = v_ref[0, :, cols].astype(BF16)
        d_mix = dm_ref[0, :, cols]
        decay = decays(ids_col, ids_row, slope)
        weights = (dot(rq, rk, NT) * decay).astype(BF16)
        d_scores = (dot(d_mix, value, NT) * decay).astype(BF16)
        enter = ramp(rows, 1.0, 1.0, slope) * link
        d_rq = dot(d_scores, rk, NN) + dot(d_mix, s_ref[0, head], NT) * jnp.concatenate(
            [enter, enter], axis=1
        )
        d_query = d_rq[:, :HEAD_DIM] * cos + d_rq[:, HEAD_DIM:] * sin
        dq_ref[0, :, cols] = (
            d_query.astype(BF16).astype(F32) * swish_slope(q_pre)
        ).astype(BF16)
        d_rk = dot(d_scores, rq, TN)
        dk_ref[0, :, cols] = d_rk[:, :HEAD_DIM] * cos + d_rk[:, HEAD_DIM:] * sin
        dv_ref[0, :, cols] = dot(weights, d_mix, TN)


def state_back_body(
    order, k_ref, v_ref, dk_ref, dv_ref, cos_ref, sin_ref, tail_ref, s_ref, dko_ref, dvo_ref
):
    rows = k_ref.shape[1]
    cos, sin = cos_ref[...], sin_ref[...]
    tail = tail_ref[0]
    for head in range(HEADS):
        cols = columns(head)
        k_pre = k_ref[0, :, cols]
        leave = ramp(rows, rows - 1.0, -1.0, slope_of(head)) * tail
        key = rounded_swish(k_pre) * leave
        rk = turned(key, cos, sin).astype(BF16)
        value = v_ref[0, :, cols].astype(BF16)
        state = s_ref[0, head]
        d_rk = dot(value, state, NT) * jnp.concatenate([leave, leave], axis=1)
        d_key = dk_ref[0, :, cols] + d_rk[:, :HEAD_DIM] * cos + d_rk[:, HEAD_DIM:] * sin
        dko_ref[0, :, cols] = (d_key.astype(BF16).astype(F32) * swish_slope(k_pre)).astype(BF16)
        dvo_ref[0, :, cols] = (dv_ref[0, :, cols] + dot(rk, state, NN)).astype(BF16)


def spread(order, h_ref, out):
    width = h_ref.shape[1] // 8
    for k in range(8):
        out[:, k * width : (k + 1) * width] = h_ref[:, at_block(order, BITS_Y[k], width)]


def row_norm_body(order, x_ref, out, held):
    x = x_ref[...].astype(F32)
    scale = lax.rsqrt(jnp.mean(x * x, axis=-1, keepdims=True) + EPS)
    held[...] = (x * scale).astype(BF16)
    spread(order, held, out)


def head_slope(head):
    return jnp.exp2(-8.0 * (head.astype(F32) + 1.0) / HEADS)


def block_decay(ids_col, ids_row, i, j, size, slope):
    gap = (
        (i - j) * size
        + lax.broadcasted_iota(jnp.int32, (size, size), 0)
        - lax.broadcasted_iota(jnp.int32, (size, size), 1)
    ).astype(F32)
    same = ids_col[i * size : (i + 1) * size] == ids_row[:, j * size : (j + 1) * size]
    keep = same if i > j else same & (gap >= 0.0)
    return jnp.where(keep, jnp.exp(-slope * jnp.maximum(gap, 0.0)), 0.0)


def row_mix_body(size, order, q_ref, k_ref, v_ref, cos_ref, sin_ref, col_ref, row_ref, mix_ref):
    q_ref, k_ref, v_ref = q_ref.at[0], k_ref.at[0], v_ref.at[0]
    cos, sin = cos_ref[...], sin_ref[...]
    col, row = col_ref[...], row_ref[...]
    each = q_ref.shape[1] // HEAD_DIM
    for part in range(each):
        cols = columns(part)
        slope = head_slope(pl.program_id(0) * each + part)
        rq = turned(rounded_swish(q_ref[:, cols]), cos, sin).astype(BF16)
        rk = turned(rounded_swish(k_ref[:, cols]), cos, sin).astype(BF16)
        value = v_ref[:, cols].astype(BF16)
        for i in range(rq.shape[0] // size):
            here = slice(i * size, (i + 1) * size)
            mixed = jnp.zeros((size, HEAD_DIM), F32)
            for j in range(i + 1):
                there = slice(j * size, (j + 1) * size)
                scores = dot(rq[here], rk[there], NT) * block_decay(col, row, i, j, size, slope)
                mixed += dot(scores.astype(BF16), value[there], NN)
            mix_ref[here, cols] = mixed.astype(BF16)


def row_mix_back_body(
    size, order, q_ref, k_ref, v_ref, dm_ref, cos_ref, sin_ref, col_ref, row_ref,
    d_ref,
):
    q_ref, k_ref, v_ref = q_ref.at[0], k_ref.at[0], v_ref.at[0]
    dq_ref, dk_ref, dv_ref = d_ref.at[0, 0], d_ref.at[0, 1], d_ref.at[0, 2]
    cos, sin = cos_ref[...], sin_ref[...]
    col, row = col_ref[...], row_ref[...]
    each = q_ref.shape[1] // HEAD_DIM
    count = q_ref.shape[0] // size
    cut = [slice(i * size, (i + 1) * size) for i in range(count)]

    def back(d_turned, pre, at):
        d = d_turned[:, :HEAD_DIM] * cos[at] + d_turned[:, HEAD_DIM:] * sin[at]
        return (d.astype(BF16).astype(F32) * swish_slope(pre[at])).astype(BF16)

    for part in range(each):
        cols = columns(part)
        slope = head_slope(pl.program_id(0) * each + part)
        q_pre, k_pre = q_ref[:, cols], k_ref[:, cols]
        rq = turned(rounded_swish(q_pre), cos, sin).astype(BF16)
        rk = turned(rounded_swish(k_pre), cos, sin).astype(BF16)
        value = v_ref[:, cols].astype(BF16)
        d_mix = dm_ref[:, cols]
        d_rq = [0.0] * count
        d_rk = [0.0] * count
        d_value = [0.0] * count
        for i in range(count):
            for j in range(i + 1):
                decay = block_decay(col, row, i, j, size, slope)
                scores = (dot(rq[cut[i]], rk[cut[j]], NT) * decay).astype(BF16)
                d_scores = (dot(d_mix[cut[i]], value[cut[j]], NT) * decay).astype(BF16)
                d_value[j] += dot(scores, d_mix[cut[i]], TN)
                d_rq[i] += dot(d_scores, rk[cut[j]], NN)
                d_rk[j] += dot(d_scores, rq[cut[i]], TN)
        for i in range(count):
            dq_ref[cut[i], cols] = back(d_rq[i], q_pre, cut[i])
            dk_ref[cut[i], cols] = back(d_rk[i], k_pre, cut[i])
            dv_ref[cut[i], cols] = d_value[i].astype(BF16)


def stacked(refs):
    return jnp.concatenate([r[...] for r in refs], axis=0)


def restored(order, value, out):
    width = value.shape[1] // 8
    for k, at in enumerate(BITS_Y):
        out[:, at_block(order, at, width)] = value[:, k * width : (k + 1) * width]


def project_body(order, h_ref, *refs):
    h = h_ref[...]
    refs[16][0] = dot(h, stacked(refs[:8]), NN)
    refs[16][1] = dot(h, stacked(refs[8:16]), NN)


def out_mid_body(order, mix_ref, h_in_ref, x_ref, *refs):
    u_ref, gated_ref, mid_ref, h_ref = refs[16:20]
    held = refs[-1]
    mix = mix_ref[...].astype(F32)
    u = dot(h_in_ref[...], stacked(refs[:8]), NN)
    u_ref[...] = u
    scale = lax.rsqrt(jnp.mean(mix * mix, axis=-1, keepdims=True) + EPS)
    held[...] = (mix * scale * (u * sigmoid(u))).astype(BF16)
    spread(order, held, gated_ref)
    mid = x_ref[...].astype(F32) + dot(gated_ref[...], stacked(refs[8:16]), NN)
    mid_ref[...] = mid
    scale = lax.rsqrt(jnp.mean(mid * mid, axis=-1, keepdims=True) + EPS)
    held[...] = (mid * scale).astype(BF16)
    spread(order, held, h_ref)


def left_right_body(order, h_ref, *refs):
    left_ref, right_ref, product_ref = refs[16:]
    h = h_ref[...]
    left = dot(h, stacked(refs[:8]), NN)
    right = dot(h, stacked(refs[8:16]), NN)
    left_ref[...] = left.astype(BF16)
    right_ref[...] = right.astype(BF16)
    product_ref[...] = (left * right).astype(BF16)


def down_grad_body(rows, order, product_ref, c_ref, *refs):
    outs, held, sems = refs[:4], refs[4], refs[5]
    step = pl.program_id(0)
    size = product_ref.shape[1]
    held[pl.ds(pl.multiple_of(step * size, size), size), :] = dot(
        product_ref[...], c_ref[...], TN, BF16
    )

    @pl.when(step == pl.num_programs(0) - 1)
    def _():
        half = held.shape[1] // 2
        copies = []
        for side, bits in enumerate((BITS_X, BITS_Y)):
            for k, bit in enumerate(bits):
                copies.append(
                    pltpu.make_async_copy(
                        held.at[at_block(order, bit, rows), side * half : (side + 1) * half],
                        outs[2 * (k // 4) + side].at[(k % 4) * rows : (k % 4 + 1) * rows, :],
                        sems.at[side, k],
                    )
                )
        run_copies(copies)


def store_apart(g, keep, send, cols, over_x):
    rows = g.shape[0] // 8
    for i, block in enumerate((0, 2, 1, 3) if over_x else (0, 1, 2, 3)):
        place = slice(i * rows, (i + 1) * rows)
        keep[place, cols] = g[block * rows : (block + 1) * rows]
        send[place, cols] = g[(4 + block) * rows : (5 + block) * rows]


def feed_back_body(rows, order, left_ref, right_ref, product_ref, h_ref, c_ref, mid_ref, *refs):
    weights, downs = refs[:16], refs[16:32]
    keep_l, send_l, keep_r, send_r, d_mid_ref, d_branch_ref, act_ref = refs[32:39]
    down, grad, total, held, sems = refs[39:]
    step = pl.program_id(0)

    @pl.when(step == 0)
    def _():
        half = down.shape[1] // 2
        run_copies(
            [
                pltpu.make_async_copy(
                    downs[8 * side + k],
                    down.at[at_block(order, at, rows), side * half : (side + 1) * half],
                    sems.at[side, k],
                )
                for side in range(2)
                for k, at in enumerate(BITS_Y)
            ]
        )
        held[...] = jnp.zeros_like(held)

    size = left_ref.shape[1]
    last = pl.num_programs(0) - 2
    whole = slice(0, size)
    both = held[...]
    g = dot(h_ref[...], both, TN, BF16)
    store_apart(g[:, :size], keep_l, send_l, whole, True)
    store_apart(g[:, size:], keep_r, send_r, whole, False)
    wide = jnp.concatenate([stacked(weights[:8]), stacked(weights[8:])], axis=1)
    grad[...] += dot(both, wide, NT)

    block = jnp.minimum(step, last)
    w_down = down[pl.ds(pl.multiple_of(block * size, size), size), :]
    grad_product = dot(c_ref[...], w_down, NT)
    held[:, :size] = (grad_product * right_ref[...].astype(F32)).astype(BF16)
    held[:, size:] = (grad_product * left_ref[...].astype(F32)).astype(BF16)

    @pl.when(step == 0)
    def _():
        grad[...] = jnp.zeros_like(grad)

    @pl.when(step == pl.num_programs(0) - 1)
    def _():
        mid = mid_ref[...]
        act_ref[...] = (mid + dot(product_ref[...], down[...], NN)).astype(BF16)
        restored(order, grad[...], total)
        g = total[...]
        scale = lax.rsqrt(jnp.mean(mid * mid, axis=-1, keepdims=True) + EPS)
        inner = jnp.mean(g * mid, axis=-1, keepdims=True) * (scale * scale * scale)
        d_mid = c_ref[...].astype(F32) + scale * g - mid * inner
        d_mid_ref[...] = d_mid
        d_branch_ref[...] = d_mid.astype(BF16)


def gate_out_back_body(order, d_ref, mix_ref, u_ref, *refs):
    du_ref, dm_ref, held = refs[8:]
    restored(order, dot(d_ref[...], stacked(refs[:8]), NT), held)
    dg = held[...]
    mix = mix_ref[...].astype(F32)
    u = u_ref[...]
    sig = sigmoid(u)
    scale = lax.rsqrt(jnp.mean(mix * mix, axis=-1, keepdims=True) + EPS)
    du_ref[...] = (dg * mix * scale * (sig * (1.0 + u * (1.0 - sig)))).astype(BF16)
    dn = dg * (u * sig)
    inner = jnp.mean(dn * mix, axis=-1, keepdims=True) * (scale * scale * scale)
    dm_ref[...] = (scale * dn - mix * inner).astype(BF16)


def in_back_body(order, x_ref, d_mid_ref, du_ref, d_ref, *refs):
    low, high, gates, (out, grad, held) = refs[:8], refs[8:16], refs[16:24], refs[24:]
    step = pl.program_id(0)

    @pl.when(step == 0)
    def _():
        grad[...] = dot(du_ref[...], stacked(gates), NT)

    grad[...] += dot(d_ref[0, 0], stacked(low), NT) + dot(d_ref[1, 0], stacked(high), NT)

    @pl.when(step == pl.num_programs(0) - 1)
    def _():
        restored(order, grad[...], held)
        g = held[...]
        x = x_ref[...].astype(F32)
        scale = lax.rsqrt(jnp.mean(x * x, axis=-1, keepdims=True) + EPS)
        inner = jnp.mean(g * x, axis=-1, keepdims=True) * (scale * scale * scale)
        out[...] = (d_mid_ref[...] + scale * g - x * inner).astype(BF16)


def weight_grads_body(order, h_ref, gated_ref, d_ref, du, db, *outs):
    held, sems = outs[4:8], outs[8]
    step = pl.program_id(0)

    def copies(side):
        return [
            pltpu.make_async_copy(held[2 * side + i], outs[2 * side + i], sems.at[2 * side + i])
            for i in range(2)
        ]

    def run(side):
        terms = [(h_ref, d_ref.at[0, i]) for i in range(3)] + [(h_ref, du), (gated_ref, db)]
        for i, (lhs, d) in enumerate(terms):
            g = dot(lhs[...], d[...], TN, BF16)
            cols = slice(i * g.shape[1], (i + 1) * g.shape[1])
            store_apart(g, held[2 * side], held[2 * side + 1], cols, side == 0)
        for copy in copies(side):
            copy.start()

    @pl.when(step == 0)
    def _():
        run(0)

    @pl.when(step == 1)
    def _():
        run(1)
        for copy in copies(0) + copies(1):
            copy.wait()


class Chain:
    def __init__(self, fresh, factor, forward, parts):
        self.fresh, self.factor, self.forward, self.parts = fresh, factor, forward, parts
        self.seqs = fresh.shape[0]
        self.now = [fresh[s] for s in range(self.seqs)]
        self.got = [[] for _ in range(self.seqs)]
        self.turns = self.seqs + parts - 2

    def pass_on(self, s, hop):
        pair = (hop - 1, hop) if self.forward else (self.parts - hop, self.parts - hop - 1)
        self.got[s].append(lax.ppermute(self.now[s], "heads", [pair]))

    def begin(self):
        for s in range(self.seqs):
            self.pass_on(s, 1)

    def at(self, turn):
        return [(s, turn - s) for s in range(self.seqs) if 1 <= turn - s < self.parts]

    def arrivals(self, turn):
        self.new = [self.got[s][hop - 1] for s, hop in self.at(turn)]
        return self, "new"

    def go_on(self, turn):
        for (s, hop), new in zip(self.at(turn), self.new):
            self.got[s][hop - 1] = new
            if hop + 1 < self.parts:
                arrived = new.astype(F32) * self.factor[s][:, None, None]
                self.now[s] = (self.fresh[s].astype(F32) + arrived).astype(BF16)
                self.pass_on(s, hop + 1)

    def result(self):
        return jnp.stack([functools.reduce(lambda a, b: a + b, g) for g in self.got])


class Layer:
    def __init__(self, tokens, doc_lengths, cotangent):
        seqs, length, width = tokens.shape
        self.seqs, self.length, self.width, self.count = seqs, length, width, seqs * length
        self.here = lax.axis_index("rows")
        self.place = lax.axis_index("heads")
        self.order = places(self.here, self.place)
        self.x = tokens.reshape(self.count, width)
        self.dy = cotangent.reshape(self.count, width)

        ends = jnp.cumsum(doc_lengths, axis=-1, dtype=jnp.int32)[:, :-1]

        def ids_at(where):
            return jnp.sum((where[None, :, None] >= ends[:, None, :]).astype(jnp.int32), axis=-1)

        start = self.place * length
        positions = start + jnp.arange(length, dtype=jnp.int32)
        ids = ids_at(positions)
        before = jnp.where(self.place > 0, ids_at(jnp.reshape(start - 1, (1,))), -1)
        final = ids[:, -1:]
        link = (ids == before).astype(F32)[:, :, None]
        tail = (ids == final).astype(F32)[:, :, None]
        slopes = jnp.array([slope_of(h) for h in range(HEADS)], F32)
        self.factor = (final == before).astype(F32) * jnp.exp(-slopes * length)[None, :]
        theta = jnp.exp(-math.log(10000.0) * jnp.arange(HEAD_DIM, dtype=F32) / HEAD_DIM)
        angle = positions.astype(F32)[:, None] * theta[None, :]

        table = pl.BlockSpec((length, HEAD_DIM), lambda s, *_: (0, 0))
        one_col = pl.BlockSpec((1, length, 1), lambda s, *_: (s, 0, 0))
        one_row = pl.BlockSpec((1, 1, length), lambda s, *_: (s, 0, 0))
        self.turn = [(jnp.cos(angle), table), (jnp.sin(angle), table)]
        self.link = link, one_col
        self.tail = tail, one_col
        self.masks = [(ids[:, :, None], one_col), (ids[:, None, :], one_row), self.link]
        self.seq = pl.BlockSpec((1, length, width), lambda s, *_: (s, 0, 0))
        self.state = pl.BlockSpec(
            (1, HEADS, 2 * HEAD_DIM, HEAD_DIM), lambda s, *_: (s, 0, 0, 0)
        )
        self.states = (seqs, HEADS, 2 * HEAD_DIM, HEAD_DIM), BF16, self.state
        step = min(self.count, 256)
        self.grid = (self.count // step,)
        self.wide = rows_spec(step, width)

    def rows(self, body, ins, types, order=None):
        return call(
            body, self.grid, self.order, [(a, self.wide) for a in ins],
            [((self.count, self.width), t, self.wide) for t in types],
        )

    def seqwise(self, body, ins, outs):
        shape = (self.seqs, self.length, self.width)
        ins = [i if isinstance(i, tuple) else (i.reshape(shape), self.seq) for i in ins]
        outs = [o if isinstance(o, tuple) else (shape, o, self.seq) for o in outs]
        got = call(body, (self.seqs,), self.order, ins, outs)
        return [g.reshape(self.count, self.width) if g.shape == shape else g for g in got]

    def norm(self):
        return self.rows(norm_body, [self.x], [BF16])

    def fresh(self, k_pre, v_pre):
        return self.seqwise(fresh_body, [k_pre, v_pre] + self.turn + [self.tail], [self.states])[0]

    def mix(self, q_pre, k_pre, v_pre, u_pre, state_in):
        ins = [q_pre, k_pre, v_pre, u_pre] + self.turn + self.masks + [(state_in, self.state)]
        return self.seqwise(mix_body, ins, [BF16, BF16])

    def mid(self, branch):
        return self.rows(mid_body, [self.x, branch], [F32, BF16])

    def mid_back(self, x_mid, grad):
        return self.rows(norm_back_body, [x_mid, self.dy, grad], [F32, BF16])

    def in_back(self, d_mid, grad):
        return self.rows(norm_back_body, [self.x, d_mid, grad], [F32])[0]

    def gate_back(self, q_pre, u_pre, mix, d_gated):
        ins = [q_pre, u_pre, mix, d_gated] + self.turn + [self.link]
        return self.seqwise(gate_back_body, ins, [BF16, BF16, self.states])

    def mix_back(self, q_pre, k_pre, v_pre, d_mix, state_in):
        ins = [q_pre, k_pre, v_pre, d_mix] + self.turn + self.masks + [(state_in, self.state)]
        return self.seqwise(mix_back_body, ins, [BF16, F32, F32])

    def state_back(self, k_pre, v_pre, dk_near, dv_near, d_state):
        ins = [k_pre, v_pre, dk_near, dv_near] + self.turn + [self.tail, (d_state, self.state)]
        return self.seqwise(state_back_body, ins, [BF16, BF16])


def plainly(layer, heads_count, weights):
    w_query, w_key, w_value, w_gate, w_out, w_left, w_right, w_down = (
        lax.all_gather(w, "rows", axis=0, tiled=True) for w in weights
    )

    def carried(fresh, forward):
        chain = Chain(fresh, layer.factor, forward, heads_count)
        chain.begin()
        for turn in range(1, chain.turns + 1):
            chain.arrivals(turn)
            chain.go_on(turn)
        return chain.result()

    def gradient(lhs, d):
        total = lax.psum_scatter(dot(lhs, d, TN, BF16), "rows", scatter_dimension=0, tiled=True)
        return lax.psum_scatter(total, "heads", scatter_dimension=1, tiled=True).astype(F32)

    (h_in,) = layer.norm()
    q_pre, k_pre, v_pre, u_pre = (
        dot(h_in, w, NN) for w in (w_query, w_key, w_value, w_gate)
    )
    state_in = carried(layer.fresh(k_pre, v_pre), True)
    mix, gated = layer.mix(q_pre, k_pre, v_pre, u_pre, state_in)
    x_mid, h_mid = layer.mid(dot(gated, w_out, NN))
    left, right = dot(h_mid, w_left, NN), dot(h_mid, w_right, NN)
    product = (left * right).astype(BF16)
    activations = (x_mid + dot(product, w_down, NN)).astype(BF16)
    grad_product = dot(layer.dy, w_down, NT)
    d_left = (grad_product * right).astype(BF16)
    d_right = (grad_product * left).astype(BF16)
    d_mid, d_branch = layer.mid_back(
        x_mid, dot(d_left, w_left, NT) + dot(d_right, w_right, NT)
    )
    d_u, d_mix, d_fresh = layer.gate_back(q_pre, u_pre, mix, dot(d_branch, w_out, NT))
    d_state = carried(d_fresh, False)
    d_q, dk_near, dv_near = layer.mix_back(q_pre, k_pre, v_pre, d_mix, state_in)
    d_k, d_v = layer.state_back(k_pre, v_pre, dk_near, dv_near, d_state)
    grad_in = (
        dot(d_q, w_query, NT) + dot(d_u, w_gate, NT) + dot(d_k, w_key, NT) + dot(d_v, w_value, NT)
    )
    input_grad = layer.in_back(d_mid, grad_in)
    pairs = (
        (h_in, d_q), (h_in, d_k), (h_in, d_v), (h_in, d_u), (gated, d_branch),
        (h_mid, d_left), (h_mid, d_right), (product, layer.dy),
    )
    return (activations, input_grad) + tuple(gradient(lhs, d) for lhs, d in pairs)


class Row:
    def __init__(self, doc_lengths, length, width, here, head):
        self.length, self.width = length, width
        self.order = places(here, head)
        lengths = lax.dynamic_index_in_dim(doc_lengths, head, 0, keepdims=False)
        ends = jnp.cumsum(lengths, dtype=jnp.int32)[:-1]
        positions = jnp.arange(length, dtype=jnp.int32)
        ids = jnp.sum((positions[:, None] >= ends[None, :]).astype(jnp.int32), axis=-1)
        theta = jnp.exp(-math.log(10000.0) * jnp.arange(HEAD_DIM, dtype=F32) / HEAD_DIM)
        angle = positions.astype(F32)[:, None] * theta[None, :]

        def whole(rows, cols):
            return pl.BlockSpec((rows, cols), lambda *_: (0, 0))

        table = whole(length, HEAD_DIM)
        self.extra = [
            (jnp.cos(angle), table), (jnp.sin(angle), table),
            (ids[:, None], whole(length, 1)), (ids[None, :], whole(1, length)),
        ]
        self.heads = pl.BlockSpec((length, 2 * HEAD_DIM), lambda h, *_: (0, h))
        self.wide = rows_spec(min(length, 256), width)
        self.all = whole(length, width)
        self.block = math.gcd(length, 256)
        self.flops = 2 * length * width * width

    def norm(self, x):
        return self.by_rows(row_norm_body, [(x, self.wide)], [], [BF16], [BF16])

    def pieces(self, group, half, width=None):
        rows, whole = group.pieces[half].shape
        spec = pl.BlockSpec((rows, width or whole), lambda i, *_: (0, i if width else 0))
        return [(a, spec) for a in group.all(half)]

    def thirds(self, which=None, dtype=F32):
        half = self.width // 2
        if which is None:
            return pl.BlockSpec((2, self.length, half), lambda i, *_: (0, 0, i))
        pair = 2 * HEAD_DIM
        each = half // pair
        return pl.BlockSpec(
            (1, self.length, pair), lambda i, *_: (i // each, 0, which * each + i % each)
        )

    def project(self, h, qkv):
        half = self.width // 2
        return call(
            project_body, (3,), self.order,
            [(h, self.all)] + self.pieces(qkv, 0, half) + self.pieces(qkv, 1, half),
            [((2, self.length, 3 * half), F32, self.thirds())], flops=3 * self.flops,
        )[0]

    def column(self, block, offset=0):
        return pl.BlockSpec((self.length, block), lambda i, *_: (0, offset + i))

    def mix(self, pre):
        return call(
            functools.partial(row_mix_body, self.block), (HEADS // 2,), self.order,
            [(pre, self.thirds(i)) for i in range(3)] + self.extra,
            [((self.length, self.width), BF16, self.heads)], flops=self.flops * 3 // 8,
        )[0]

    def mix_back(self, pre, d_mix):
        pair, half = 2 * HEAD_DIM, self.width // 2
        each = half // pair
        spec = pl.BlockSpec((1, 3, self.length, pair), lambda i, *_: (i // each, 0, 0, i % each))
        return call(
            functools.partial(row_mix_back_body, self.block), (HEADS // 2,), self.order,
            [(pre, self.thirds(i)) for i in range(3)] + [(d_mix, self.heads)] + self.extra,
            [((2, 3, self.length, half), BF16, spec)], flops=self.flops,
        )[0]

    def by_rows(self, body, ins, weights, types, scratch):
        step = self.wide.block_shape[0]
        return call(
            body, (self.length // step,), self.order, ins + weights,
            [((self.length, self.width), t, self.wide) for t in types],
            scratch=[pltpu.VMEM((step, self.width), t) for t in scratch], flops=self.flops,
        )

    def out_mid(self, mix, h, x, uo):
        return self.by_rows(
            out_mid_body, [(mix, self.wide), (h, self.wide), (x, self.wide)],
            self.pieces(uo, 0) + self.pieces(uo, 1),
            [F32, BF16, F32, BF16], [BF16],
        )

    def gate_out_back(self, d_branch, mix, u_pre, uo):
        return self.by_rows(
            gate_out_back_body, [(d_branch, self.wide), (mix, self.wide), (u_pre, self.wide)],
            self.pieces(uo, 1), [BF16, BF16], [F32],
        )

    def left_right(self, h, ff):
        inner = ff.pieces[0].shape[1]
        block = math.gcd(inner, 1408)
        return call(
            left_right_body, (inner // block,), self.order,
            [(h, self.all)] + self.pieces(ff, 0, block) + self.pieces(ff, 1, block),
            [((self.length, inner), BF16, self.column(block))] * 3,
            flops=2 * self.flops * inner // self.width,
        )

    def down_grad(self, product, c):
        inner, half = product.shape[1], self.width // 2
        block = math.gcd(inner, 1408)
        rows = inner // 8
        got = call(
            functools.partial(down_grad_body, rows), (inner // block,), self.order,
            [(product, self.column(block)), (c, self.all)], [((4 * rows, half), BF16, HBM)] * 4,
            scratch=[pltpu.VMEM((inner, self.width), BF16), pltpu.SemaphoreType.DMA((2, 8))],
            flops=self.flops * inner // self.width,
        )
        return Reduce(self.order, got[2:], got[:2], [2, 4])

    def feed_back(self, left, right, product, h, c, x_mid, ff, down):
        inner, rows = ff.pieces[0].shape[1], down.pieces[0].shape[0]
        block = math.gcd(inner, 256)
        steps = inner // block

        def now(rows):
            return pl.BlockSpec((rows, block), lambda i, *_: (0, jnp.minimum(i, steps - 1)))

        def before(rows):
            return pl.BlockSpec((rows, block), lambda i, *_: (0, jnp.maximum(i - 1, 0)))

        full = (self.length, self.width)
        weights = [(a, before(ff.pieces[0].shape[0])) for a in ff.all(0) + ff.all(1)]
        return call(
            functools.partial(feed_back_body, rows), (steps + 1,), self.order,
            [(left, now(self.length)), (right, now(self.length))]
            + [(product, whole_spec(self.length, inner))]
            + [(a, self.all) for a in (h, c, x_mid)]
            + weights + [(a, HBM) for a in down.all(0) + down.all(1)],
            [((self.width // 2, inner), BF16, before(self.width // 2))] * 4
            + [(full, F32, self.all), (full, BF16, self.all), (full, BF16, self.all)],
            scratch=[pltpu.VMEM((inner, self.width), BF16)] + [pltpu.VMEM(full, F32)] * 2
            + [pltpu.VMEM((self.length, 2 * block), BF16), pltpu.SemaphoreType.DMA((2, 8))],
            flops=6 * self.flops * inner // self.width,
        )

    def in_back(self, x, d_mid, d, d_u, qkv, uo):
        half = self.width // 2
        full = (self.length, self.width)
        third = pl.BlockSpec((2, 1, self.length, half), lambda i, *_: (0, i, 0, 0))
        return call(
            in_back_body, (3,), self.order,
            [(x, self.all), (d_mid, self.all), (d_u, self.all), (d, third)]
            + self.pieces(qkv, 0, half) + self.pieces(qkv, 1, half) + self.pieces(uo, 0),
            [(full, BF16, self.all)], scratch=[pltpu.VMEM(full, F32)] * 2, flops=4 * self.flops,
        )[0]

    def weight_grads(self, h, gated, d, d_u, d_branch):
        half = self.width // 2
        shape = (half, 5 * half)
        thirds = pl.BlockSpec((1, 3, self.length, half), lambda i, *_: (i, 0, 0, 0))
        got = call(
            weight_grads_body, (2,), self.order,
            [(h, self.all), (gated, self.all)]
            + [(d, thirds), (d_u, self.column(half)), (d_branch, self.column(half))],
            [(shape, BF16, HBM)] * 4,
            scratch=[pltpu.VMEM(shape, BF16)] * 4 + [pltpu.SemaphoreType.DMA((4,))],
            flops=5 * self.flops,
        )
        return Reduce(self.order, got[1::2], got[::2], [2, 4])


def stepwise(tokens, doc_lengths, cotangent, weights):
    w_query, w_key, w_value, w_gate, w_out, w_left, w_right, w_down = weights
    size, width = tokens.shape[1:]
    length, half = 4 * size, width // 2
    here, head = lax.axis_index("rows"), lax.axis_index("heads")
    row = Row(doc_lengths, length, width, here, head)
    order = row.order
    v = types.SimpleNamespace()
    clock = Clock(order)
    tick = clock.tick

    def exchanged(a):
        return lax.all_to_all(a.reshape(4, size, width), "heads", 0, 0, tiled=True)

    def whole_row(a):
        return exchanged(a).reshape(length, width)

    inner = w_left.shape[1]
    uo = Gather([w_gate, w_out])
    uo.first()
    qkv = Gather(
        pack(order, [w_query, w_key, w_value], [[(i, at, half) for i in range(3)] for at in (0, half)])
    )
    qkv.first()
    v.x = whole_row(after(tokens, uo.near_x[0]))
    v.extra = [a for a, _ in row.extra]
    ff = Gather([w_left, w_right])
    v.c = cotangent
    tick((qkv, "near_x"), (qkv, "near_y"), (uo, "near_x"), (uo, "near_y"), (uo, "pieces"), (v, "c"), (v, "extra"))
    row.extra = [(a, spec) for a, (_, spec) in zip(v.extra, row.extra)]
    qkv.second()
    uo.second()
    qkv.cross("pieces", "near_x", "near_y")
    uo.cross("pieces", "near_x", "near_y")
    (v.h,) = row.norm(v.x)
    tick((qkv, "far"), (uo, "far"), (v, "h"), (ff, "pieces"))
    ff.first()
    ff.cross("pieces")
    qkv.cross("far")
    uo.cross("far")
    v.pre = row.project(v.h, qkv)
    v.mix = row.mix(v.pre)
    v.u_pre, v.gated, v.x_mid, v.h_mid = row.out_mid(v.mix, v.h, v.x, uo)
    v.down = w_down
    tick((v, "x_mid"), (v, "h_mid"), (ff, "near_x"), (ff, "near_y"), (v, "down"), (v, "c"))
    ff.second()
    v.c = whole_row(v.c)
    ff.cross("near_x", "near_y")
    v.down = pack(order, [v.down], [[(0, 0, half)], [(0, half, half)]])
    tick((ff, "far"), (v, "down"))
    down = Gather(v.down)
    ff.cross("far")
    down.first()
    down.cross("pieces")

    v.left, v.right, v.product = row.left_right(v.h_mid, ff)
    tick((v, "left"), (v, "right"), (v, "product"), (down, "near_x"), (down, "near_y"), (v, "c"))
    down.second()
    down.cross("near_x", "near_y")
    v.g_down = dot(v.product, v.c, TN, BF16)
    tick((v, "g_down"), (down, "far"), (v, "left"))
    v.sum_down = lax.psum_scatter(v.g_down, "rows", scatter_dimension=0, tiled=True)
    down.cross("far")
    tick((down, "far_other"), (v, "left"))
    keep_l, send_l, keep_r, send_r, v.d_mid, v.d_branch, v.act = row.feed_back(
        v.left, v.right, v.product, v.h_mid, v.c, v.x_mid, ff, down
    )
    r_ff = Reduce(order, [send_l, send_r], [keep_l, keep_r], [2, 4])
    tick((r_ff, "sends"), (v, "d_mid"), (v, "d_branch"), (v, "act"))
    r_ff.core()
    v.d_u, v.d_mix = row.gate_out_back(v.d_branch, v.mix, v.u_pre, uo)
    tick((r_ff, "theirs"), (v, "d_u"), (v, "d_mix"))
    r_ff.join_far()
    tick((r_ff, "far"), (r_ff, "theirs"))
    r_ff.first_far()
    r_ff.join_near()
    tick((r_ff, "near"), (v, "act"), (v, "d_mix"))
    r_ff.first_near()
    v.act = exchanged(v.act)
    v.d = row.mix_back(v.pre, v.d_mix)
    tick((v, "d"), (r_ff, "got_far"))
    r_ff.join_first()
    tick((r_ff, "parts"), (v, "d"), (v, "sum_down"))
    r_ff.second()
    r_att = row.weight_grads(v.h, v.gated, v.d, v.d_u, v.d_branch)
    tick((r_att, "sends"), (r_ff, "got_near"), (v, "sum_down"))
    r_att.core()
    s_down = Settle(order, [[v.sum_down]], half // 2, [lambda z: z * (half // 2)])
    tick((r_att, "theirs"), (s_down, "out"), (v, "d"))
    s_down.first()
    r_att.join()
    v.back = row.in_back(v.x, v.d_mid, after(v.d, *r_att.both), v.d_u, qkv, uo)
    tick((r_att, "both"), (r_ff, "got_last"), (v, "back"), (s_down, "got"), (v, "act"))
    r_att.first()
    v.back = exchanged(v.back)
    quarter = inner // 4
    s_ff = r_ff.settle(quarter, [lambda z: z * quarter, lambda z: inner + z * quarter])
    s_down.join()
    tick((s_ff, "out"), (s_down, "out"), (s_down, "last"))
    s_ff.first()
    s_down.second()
    tick((s_ff, "got"))
    s_ff.join()
    tick((s_ff, "out"), (s_ff, "last"), (r_att, "got_near"))
    s_ff.second()
    r_att.join_first_both()
    tick((r_att, "parts"))
    r_att.second()
    tick((s_down, "got_near"), (s_down, "got_far"))
    (v.g_down,) = s_down.result()
    tick((r_att, "got_last"), (v, "g_down"))
    s_att = r_att.settle(
        half // 2,
        [
            lambda z, i=i: (z // 2) * 5 * half + i * half + (z % 2) * (half // 2)
            for i in range(5)
        ],
    )
    tick((s_att, "out"), (v, "back"))
    s_att.first()
    v.back = v.back.astype(F32)
    tick((s_ff, "got_near"), (s_ff, "got_far"), (v, "back"))
    v.g_ff = s_ff.result()
    tick((s_att, "got"), (v, "g_ff"))
    s_att.join()
    tick((s_att, "out"), (s_att, "last"))
    s_att.second()
    g_query, g_key, g_value, g_gate, g_out = s_att.result()
    g_left, g_right = v.g_ff
    return (
        v.act, v.back, g_query, g_key, g_value, g_gate, g_out, g_left, g_right, v.g_down
    )


def on_device(rows_count, heads_count, tokens, doc_lengths, cotangent, *weights):
    if rows_count == 8 and heads_count == 4 and tokens.shape[0] == 4:
        return stepwise(tokens, doc_lengths, cotangent, weights)
    layer = Layer(tokens, doc_lengths, cotangent)
    activations, input_grad, *grads = plainly(layer, heads_count, weights)
    return (activations.reshape(tokens.shape), input_grad.reshape(tokens.shape), *grads)


def solution(mesh):
    sizes = dict(mesh.shape)
    tokens = P("rows", "heads", None)
    weights = P("rows", None)
    grads = P("rows", "heads")
    return jax.shard_map(
        functools.partial(on_device, sizes["rows"], sizes["heads"]),
        mesh=mesh,
        in_specs=(tokens, weights, tokens) + (weights,) * 8,
        out_specs=(tokens, tokens) + (grads,) * 8,
        check_vma=False,
    )
```

```python
import functools
import math
import types

import jax
import jax.numpy as jnp
from jax import lax
from jax.experimental import pallas as pl
from jax.experimental.pallas import tpu as pltpu
from jax.sharding import PartitionSpec as P

HEADS = 8
HEAD_DIM = 128
EPS = 1e-06
F32 = jnp.float32
BF16 = jnp.bfloat16
VMEM_LIMIT = 54 << 20

BITS = (0, 2, 4, 6, 1, 3, 5, 7)
BITS_X = (0, 4, 2, 6, 1, 5, 3, 7)
BITS_Y = (0, 2, 4, 6, 1, 3, 5, 7)


def after(value, *others):
    return lax.optimization_barrier((value,) + others)[0]


def dot(a, b, dims, out=F32):
    return lax.dot_general(a, b, (dims, ((), ())), preferred_element_type=F32).astype(out)


NN = ((1,), (0,))
NT = ((1,), (1,))
TN = ((0,), (0,))


def swap(value, bit, size):
    return lax.ppermute(value, "rows", [(i, i ^ bit) for i in range(size)])


def swap_heads(value, bit):
    return lax.ppermute(value, "heads", [(i, i ^ bit) for i in range(4)])


HBM = pl.BlockSpec(memory_space=pltpu.HBM)


def whole_spec(rows, width):
    return pl.BlockSpec((rows, width), lambda i, *_: (0, 0))


def run_copies(copies):
    for copy in copies:
        copy.start()
    for copy in copies:
        copy.wait()


def pack(order, arrays, lists):
    rows = arrays[0].shape[0]
    widths = [sum(w for _, _, w in parts) for parts in lists]
    most = max(len(parts) for parts in lists)

    def body(order, *refs):
        ins, outs, sems = refs[: len(arrays)], refs[len(arrays) : -1], refs[-1]
        copies = []
        for j, parts in enumerate(lists):
            at = 0
            for i, (which, begin, width) in enumerate(parts):
                copies.append(
                    pltpu.make_async_copy(
                        ins[which].at[:, begin : begin + width],
                        outs[j].at[:, at : at + width],
                        sems.at[j, i],
                    )
                )
                at += width
        run_copies(copies)

    return call(
        body, (1,), order, [(a, HBM) for a in arrays],
        [((rows, w), BF16, whole_spec(rows, w)) for w in widths],
        scratch=[pltpu.SemaphoreType.DMA((len(lists), most))],
    )


class Clock:
    def __init__(self, start):
        self.token = start

    def tick(self, *places):
        held = [getattr(o, n) for o, n in places]
        held, self.token = lax.optimization_barrier((held, self.token))
        for (o, n), value in zip(places, held):
            setattr(o, n, value)


def places(here, head):
    return jnp.stack([here ^ b for b in range(8)] + [head ^ b for b in range(4)]).astype(jnp.int32)


class Gather:
    def __init__(self, pieces):
        self.pieces = list(pieces)
        self.near_x, self.near_y = [None, None], [None, None]

    def first(self, *halves):
        for half in halves or (0, 1):
            self.near_x[half] = swap(self.pieces[half], 2, 8)
            self.near_y[half] = swap(self.pieces[half], 4, 8)

    def second(self):
        self.far = [swap(self.near_x[0], 4, 8), swap(self.near_y[1], 2, 8)]

    def cross(self, *names):
        for name in names:
            setattr(self, name + "_other", [swap(p, 1, 8) for p in getattr(self, name)])

    def all(self, half):
        names = ("pieces", "near_x", "near_y", "far")
        return [getattr(self, n + core)[half] for core in ("", "_other") for n in names]


def added(*terms):
    return functools.reduce(lambda a, b: a + b, [t.astype(F32) for t in terms]).astype(BF16)


class Reduce:
    def __init__(self, order, sends, keeps, bits):
        self.order, self.sends, self.keeps, self.bits = order, list(sends), list(keeps), list(bits)

    def core(self):
        self.theirs = [swap(s, 1, 8) for s in self.sends]

    def joined(self, quarter, *more):
        rows = self.keeps[0].shape[0] // 4
        place = slice(quarter * rows, (quarter + 1) * rows)
        return [
            added(k[place], t[place], *m) for k, t, *m in zip(self.keeps, self.theirs, *more)
        ]

    def join_far(self):
        self.far = self.joined(3)

    def join_near(self):
        self.near = self.joined(2)

    def first_far(self):
        self.got_far = [swap(t, b, 8) for t, b in zip(self.far, self.bits)]

    def first_near(self):
        self.got_near = [swap(t, b, 8) for t, b in zip(self.near, self.bits)]

    def join_first(self):
        self.parts = self.joined(1, self.got_far)

    def join(self):
        half = self.keeps[0].shape[0] // 2
        self.both = [added(k[half:], t[half:]) for k, t in zip(self.keeps, self.theirs)]

    def first(self):
        self.got_near = [swap(t, b, 8) for t, b in zip(self.both, self.bits)]

    def join_first_both(self):
        rows = self.keeps[0].shape[0] // 4
        self.parts = self.joined(1, [g[rows:] for g in self.got_near])

    def second(self):
        self.got_last = [swap(p, 6 - b, 8) for p, b in zip(self.parts, self.bits)]

    def settle(self, block, starts):
        parts = zip(self.keeps, self.theirs, self.got_near, self.got_last)
        return Settle(self.order, [list(p) for p in parts], block, starts)


class Settle:
    def __init__(self, order, parts, block, starts):
        self.order, self.block, self.count = order, block, len(starts)
        rows = self.rows = parts[0][-1].shape[0]
        widths = [p[-1].shape[1] for p in parts]
        counts = [len(p) for p in parts]

        def body(order, *refs):
            *results, held = refs[sum(counts) :]
            owns, outs = results[:2], results[2:]
            at, first = 0, 0
            for width, count in zip(widths, counts):
                total = refs[first][...].astype(F32)
                for ref in refs[first + 1 : first + count]:
                    total += ref[...].astype(F32)
                held[:, at : at + width] = total
                at, first = at + width, first + count
            for z in range(4):

                @pl.when(order[8] == z)
                def _(z=z):
                    for i, start in enumerate(starts):
                        for j, (mine, theirs) in enumerate(((0, 1), (2, 3))):
                            mine, theirs = start(z ^ mine), start(z ^ theirs)
                            owns[j][i] = held[:, mine : mine + block]
                            outs[j][i] = held[:, theirs : theirs + block].astype(BF16)

        shape = (self.count, rows, block)
        spec = pl.BlockSpec((self.count, rows // 2, block), lambda i, *_: (0, i, 0))
        self.own, self.far, self.last, self.out = call(
            body, (2,), order,
            [(a, pl.BlockSpec((rows // 2, a.shape[1]), lambda i, *_: (i, 0))) for p in parts for a in p],
            [(shape, F32, spec)] * 2 + [(shape, BF16, spec)] * 2,
            scratch=[pltpu.VMEM((rows // 2, sum(widths)), F32)],
        )

    def first(self):
        self.got = swap_heads(self.out, 1)

    def join(self):
        self.out = (self.far + self.got.astype(F32)).astype(BF16)

    def second(self):
        self.got_far = swap_heads(self.out, 2)
        self.got_near = swap_heads(self.last, 1)

    def result(self):
        return [
            self.own[i] + self.got_near[i].astype(F32) + self.got_far[i].astype(F32)
            for i in range(self.count)
        ]


def at_block(order_ref, index, width):
    return pl.ds(pl.multiple_of(order_ref[index] * width, width), width)


def sigmoid(v):
    return 1.0 / (1.0 + jnp.exp(-v))


def swish_slope(v):
    sig = sigmoid(v)
    return sig * (1.0 + v * (1.0 - sig))


def call(body, grid, order, ins, outs, scratch=(), flops=0):
    moved = sum(a.size * a.dtype.itemsize for a, _ in ins) + sum(
        math.prod(s) * jnp.dtype(t).itemsize for s, t, _ in outs
    )
    return pl.pallas_call(
        body,
        grid_spec=pltpu.PrefetchScalarGridSpec(
            num_scalar_prefetch=1,
            grid=grid,
            in_specs=[spec for _, spec in ins],
            out_specs=[spec for _, _, spec in outs],
            scratch_shapes=list(scratch),
        ),
        out_shape=[jax.ShapeDtypeStruct(s, t) for s, t, _ in outs],
        compiler_params=pltpu.CompilerParams(vmem_limit_bytes=VMEM_LIMIT),
        cost_estimate=pl.CostEstimate(flops=flops // 4, bytes_accessed=moved // 4, transcendentals=0),
    )(order, *[a for a, _ in ins])


def rows_spec(count, width, column=0):
    return pl.BlockSpec((count, width), lambda i, *_: (i, column))


def norm_body(order, x_ref, h_ref):
    x = x_ref[...].astype(F32)
    scale = lax.rsqrt(jnp.mean(x * x, axis=-1, keepdims=True) + EPS)
    h_ref[...] = (x * scale).astype(BF16)


def mid_body(order, x_ref, b_ref, mid_ref, h_ref):
    mid = x_ref[...].astype(F32) + b_ref[...]
    mid_ref[...] = mid
    scale = lax.rsqrt(jnp.mean(mid * mid, axis=-1, keepdims=True) + EPS)
    h_ref[...] = (mid * scale).astype(BF16)


def norm_back_body(order, v_ref, base_ref, g_ref, *outs):
    v = v_ref[...].astype(F32)
    g = g_ref[...]
    scale = lax.rsqrt(jnp.mean(v * v, axis=-1, keepdims=True) + EPS)
    inner = jnp.mean(g * v, axis=-1, keepdims=True) * (scale * scale * scale)
    total = base_ref[...].astype(F32) + scale * g - v * inner
    outs[0][...] = total
    if len(outs) > 1:
        outs[1][...] = total.astype(BF16)


def ramp(rows, start, sign, slope):
    place = lax.broadcasted_iota(jnp.int32, (rows, HEAD_DIM), 0).astype(F32)
    return jnp.exp(-slope * (start + sign * place))


def decays(ids_col, ids_row, slope):
    rows = ids_col.shape[0]
    gap = (
        lax.broadcasted_iota(jnp.int32, (rows, rows), 0)
        - lax.broadcasted_iota(jnp.int32, (rows, rows), 1)
    ).astype(F32)
    keep = (gap >= 0.0) & (ids_col == ids_row)
    return jnp.where(keep, jnp.exp(-slope * jnp.maximum(gap, 0.0)), 0.0)


def slope_of(head):
    return 2.0 ** (-8.0 * (head + 1) / HEADS)


def columns(head):
    return slice(head * HEAD_DIM, (head + 1) * HEAD_DIM)


def turned(a, cos, sin):
    return jnp.concatenate([a * cos, a * sin], axis=1)


def rounded_swish(v):
    return (v * sigmoid(v)).astype(BF16).astype(F32)


def fresh_body(order, k_ref, v_ref, cos_ref, sin_ref, tail_ref, state_ref):
    rows = k_ref.shape[1]
    cos, sin = cos_ref[...], sin_ref[...]
    tail = tail_ref[0]
    for head in range(HEADS):
        key = rounded_swish(k_ref[0, :, columns(head)])
        key = key * (ramp(rows, rows - 1.0, -1.0, slope_of(head)) * tail)
        value = v_ref[0, :, columns(head)].astype(BF16)
        state_ref[0, head] = dot(turned(key, cos, sin).astype(BF16), value, TN, BF16)


def mix_body(
    order, q_ref, k_ref, v_ref, u_ref, cos_ref, sin_ref, col_ref, row_ref, link_ref, s_ref,
    mix_ref, gated_ref,
):
    rows = q_ref.shape[1]
    cos, sin = cos_ref[...], sin_ref[...]
    ids_col, ids_row = col_ref[0], row_ref[0]
    link = link_ref[0]
    power = jnp.zeros((rows, 1), F32)
    for head in range(HEADS):
        cols = columns(head)
        slope = slope_of(head)
        rq = turned(rounded_swish(q_ref[0, :, cols]), cos, sin).astype(BF16)
        rk = turned(rounded_swish(k_ref[0, :, cols]), cos, sin).astype(BF16)
        value = v_ref[0, :, cols].astype(BF16)
        weights = (dot(rq, rk, NT) * decays(ids_col, ids_row, slope)).astype(BF16)
        mixed = dot(weights, value, NN) + dot(rq, s_ref[0, head], NN) * (
            ramp(rows, 1.0, 1.0, slope) * link
        )
        mixed = mixed.astype(BF16)
        mix_ref[0, :, cols] = mixed
        mixed = mixed.astype(F32)
        power += jnp.sum(mixed * mixed, axis=-1, keepdims=True)
    scale = lax.rsqrt(power / (HEADS * HEAD_DIM) + EPS)
    for head in range(HEADS):
        cols = columns(head)
        u = u_ref[0, :, cols]
        gated_ref[0, :, cols] = (
            mix_ref[0, :, cols].astype(F32) * scale * (u * sigmoid(u))
        ).astype(BF16)


def gate_back_body(
    order, q_ref, u_ref, mix_ref, dg_ref, cos_ref, sin_ref, link_ref, du_ref, dm_ref, state_ref
):
    rows = q_ref.shape[1]
    cos, sin = cos_ref[...], sin_ref[...]
    link = link_ref[0]
    mix = mix_ref[0].astype(F32)
    scale = lax.rsqrt(jnp.mean(mix * mix, axis=-1, keepdims=True) + EPS)
    inner = jnp.zeros((rows, 1), F32)
    for head in range(HEADS):
        cols = columns(head)
        u = u_ref[0, :, cols]
        part = mix_ref[0, :, cols].astype(F32)
        dg = dg_ref[0, :, cols]
        sig = sigmoid(u)
        inner += jnp.sum(dg * (u * sig) * part, axis=-1, keepdims=True)
        du_ref[0, :, cols] = (dg * part * scale * (sig * (1.0 + u * (1.0 - sig)))).astype(BF16)
    inner = inner * (scale * scale * scale) / (HEADS * HEAD_DIM)
    for head in range(HEADS):
        cols = columns(head)
        u = u_ref[0, :, cols]
        part = mix_ref[0, :, cols].astype(F32)
        dg = dg_ref[0, :, cols]
        d_mix = (scale * (dg * (u * sigmoid(u))) - part * inner).astype(BF16)
        dm_ref[0, :, cols] = d_mix
        query = rounded_swish(q_ref[0, :, cols]) * (
            ramp(rows, 1.0, 1.0, slope_of(head)) * link
        )
        state_ref[0, head] = dot(turned(query, cos, sin).astype(BF16), d_mix, TN, BF16)


def mix_back_body(
    order, q_ref, k_ref, v_ref, dm_ref, cos_ref, sin_ref, col_ref, row_ref, link_ref, s_ref,
    dq_ref, dk_ref, dv_ref,
):
    rows = q_ref.shape[1]
    cos, sin = cos_ref[...], sin_ref[...]
    ids_col, ids_row = col_ref[0], row_ref[0]
    link = link_ref[0]
    for head in range(HEADS):
        cols = columns(head)
        slope = slope_of(head)
        q_pre = q_ref[0, :, cols]
        rq = turned(rounded_swish(q_pre), cos, sin).astype(BF16)
        rk = turned(rounded_swish(k_ref[0, :, cols]), cos, sin).astype(BF16)
        value = v_ref[0, :, cols].astype(BF16)
        d_mix = dm_ref[0, :, cols]
        decay = decays(ids_col, ids_row, slope)
        weights = (dot(rq, rk, NT) * decay).astype(BF16)
        d_scores = (dot(d_mix, value, NT) * decay).astype(BF16)
        enter = ramp(rows, 1.0, 1.0, slope) * link
        d_rq = dot(d_scores, rk, NN) + dot(d_mix, s_ref[0, head], NT) * jnp.concatenate(
            [enter, enter], axis=1
        )
        d_query = d_rq[:, :HEAD_DIM] * cos + d_rq[:, HEAD_DIM:] * sin
        dq_ref[0, :, cols] = (
            d_query.astype(BF16).astype(F32) * swish_slope(q_pre)
        ).astype(BF16)
        d_rk = dot(d_scores, rq, TN)
        dk_ref[0, :, cols] = d_rk[:, :HEAD_DIM] * cos + d_rk[:, HEAD_DIM:] * sin
        dv_ref[0, :, cols] = dot(weights, d_mix, TN)


def state_back_body(
    order, k_ref, v_ref, dk_ref, dv_ref, cos_ref, sin_ref, tail_ref, s_ref, dko_ref, dvo_ref
):
    rows = k_ref.shape[1]
    cos, sin = cos_ref[...], sin_ref[...]
    tail = tail_ref[0]
    for head in range(HEADS):
        cols = columns(head)
        k_pre = k_ref[0, :, cols]
        leave = ramp(rows, rows - 1.0, -1.0, slope_of(head)) * tail
        key = rounded_swish(k_pre) * leave
        rk = turned(key, cos, sin).astype(BF16)
        value = v_ref[0, :, cols].astype(BF16)
        state = s_ref[0, head]
        d_rk = dot(value, state, NT) * jnp.concatenate([leave, leave], axis=1)
        d_key = dk_ref[0, :, cols] + d_rk[:, :HEAD_DIM] * cos + d_rk[:, HEAD_DIM:] * sin
        dko_ref[0, :, cols] = (d_key.astype(BF16).astype(F32) * swish_slope(k_pre)).astype(BF16)
        dvo_ref[0, :, cols] = (dv_ref[0, :, cols] + dot(rk, state, NN)).astype(BF16)


def spread(order, h_ref, out):
    width = h_ref.shape[1] // 8
    for k in range(8):
        out[:, k * width : (k + 1) * width] = h_ref[:, at_block(order, BITS_Y[k], width)]


def row_norm_body(order, x_ref, out, held):
    x = x_ref[...].astype(F32)
    scale = lax.rsqrt(jnp.mean(x * x, axis=-1, keepdims=True) + EPS)
    held[...] = (x * scale).astype(BF16)
    spread(order, held, out)


def head_slope(head):
    return jnp.exp2(-8.0 * (head.astype(F32) + 1.0) / HEADS)


def block_decay(ids_col, ids_row, i, j, size, slope):
    gap = (
        (i - j) * size
        + lax.broadcasted_iota(jnp.int32, (size, size), 0)
        - lax.broadcasted_iota(jnp.int32, (size, size), 1)
    ).astype(F32)
    same = ids_col[i * size : (i + 1) * size] == ids_row[:, j * size : (j + 1) * size]
    keep = same if i > j else same & (gap >= 0.0)
    return jnp.where(keep, jnp.exp(-slope * jnp.maximum(gap, 0.0)), 0.0)


def row_mix_body(size, order, q_ref, k_ref, v_ref, cos_ref, sin_ref, col_ref, row_ref, mix_ref):
    q_ref, k_ref, v_ref = q_ref.at[0], k_ref.at[0], v_ref.at[0]
    cos, sin = cos_ref[...], sin_ref[...]
    col, row = col_ref[...], row_ref[...]
    each = q_ref.shape[1] // HEAD_DIM
    for part in range(each):
        cols = columns(part)
        slope = head_slope(pl.program_id(0) * each + part)
        rq = turned(rounded_swish(q_ref[:, cols]), cos, sin).astype(BF16)
        rk = turned(rounded_swish(k_ref[:, cols]), cos, sin).astype(BF16)
        value = v_ref[:, cols].astype(BF16)
        for i in range(rq.shape[0] // size):
            here = slice(i * size, (i + 1) * size)
            mixed = jnp.zeros((size, HEAD_DIM), F32)
            for j in range(i + 1):
                there = slice(j * size, (j + 1) * size)
                scores = dot(rq[here], rk[there], NT) * block_decay(col, row, i, j, size, slope)
                mixed += dot(scores.astype(BF16), value[there], NN)
            mix_ref[here, cols] = mixed.astype(BF16)


def row_mix_back_body(
    size, order, q_ref, k_ref, v_ref, dm_ref, cos_ref, sin_ref, col_ref, row_ref,
    d_ref,
):
    q_ref, k_ref, v_ref = q_ref.at[0], k_ref.at[0], v_ref.at[0]
    dq_ref, dk_ref, dv_ref = d_ref.at[0, 0], d_ref.at[0, 1], d_ref.at[0, 2]
    cos, sin = cos_ref[...], sin_ref[...]
    col, row = col_ref[...], row_ref[...]
    each = q_ref.shape[1] // HEAD_DIM
    count = q_ref.shape[0] // size
    cut = [slice(i * size, (i + 1) * size) for i in range(count)]

    def back(d_turned, pre, at):
        d = d_turned[:, :HEAD_DIM] * cos[at] + d_turned[:, HEAD_DIM:] * sin[at]
        return (d.astype(BF16).astype(F32) * swish_slope(pre[at])).astype(BF16)

    for part in range(each):
        cols = columns(part)
        slope = head_slope(pl.program_id(0) * each + part)
        q_pre, k_pre = q_ref[:, cols], k_ref[:, cols]
        rq = turned(rounded_swish(q_pre), cos, sin).astype(BF16)
        rk = turned(rounded_swish(k_pre), cos, sin).astype(BF16)
        value = v_ref[:, cols].astype(BF16)
        d_mix = dm_ref[:, cols]
        d_rq = [0.0] * count
        d_rk = [0.0] * count
        d_value = [0.0] * count
        for i in range(count):
            for j in range(i + 1):
                decay = block_decay(col, row, i, j, size, slope)
                scores = (dot(rq[cut[i]], rk[cut[j]], NT) * decay).astype(BF16)
                d_scores = (dot(d_mix[cut[i]], value[cut[j]], NT) * decay).astype(BF16)
                d_value[j] += dot(scores, d_mix[cut[i]], TN)
                d_rq[i] += dot(d_scores, rk[cut[j]], NN)
                d_rk[j] += dot(d_scores, rq[cut[i]], TN)
        for i in range(count):
            dq_ref[cut[i], cols] = back(d_rq[i], q_pre, cut[i])
            dk_ref[cut[i], cols] = back(d_rk[i], k_pre, cut[i])
            dv_ref[cut[i], cols] = d_value[i].astype(BF16)


def stacked(refs):
    return jnp.concatenate([r[...] for r in refs], axis=0)


def restored(order, value, out):
    width = value.shape[1] // 8
    for k, at in enumerate(BITS_Y):
        out[:, at_block(order, at, width)] = value[:, k * width : (k + 1) * width]


def project_body(order, h_ref, *refs):
    h = h_ref[...]
    refs[16][0] = dot(h, stacked(refs[:8]), NN)
    refs[16][1] = dot(h, stacked(refs[8:16]), NN)


def out_mid_body(order, mix_ref, h_in_ref, x_ref, *refs):
    u_ref, gated_ref, mid_ref, h_ref = refs[16:20]
    held = refs[-1]
    mix = mix_ref[...].astype(F32)
    u = dot(h_in_ref[...], stacked(refs[:8]), NN)
    u_ref[...] = u
    scale = lax.rsqrt(jnp.mean(mix * mix, axis=-1, keepdims=True) + EPS)
    held[...] = (mix * scale * (u * sigmoid(u))).astype(BF16)
    spread(order, held, gated_ref)
    mid = x_ref[...].astype(F32) + dot(gated_ref[...], stacked(refs[8:16]), NN)
    mid_ref[...] = mid
    scale = lax.rsqrt(jnp.mean(mid * mid, axis=-1, keepdims=True) + EPS)
    held[...] = (mid * scale).astype(BF16)
    spread(order, held, h_ref)


def left_right_body(order, h_ref, *refs):
    left_ref, right_ref, product_ref = refs[16:]
    h = h_ref[...]
    left = dot(h, stacked(refs[:8]), NN)
    right = dot(h, stacked(refs[8:16]), NN)
    left_ref[...] = left.astype(BF16)
    right_ref[...] = right.astype(BF16)
    product_ref[...] = (left * right).astype(BF16)


def down_grad_body(rows, order, product_ref, c_ref, *refs):
    outs, held, sems = refs[:4], refs[4], refs[5]
    step = pl.program_id(0)
    size = product_ref.shape[1]
    held[pl.ds(pl.multiple_of(step * size, size), size), :] = dot(
        product_ref[...], c_ref[...], TN, BF16
    )

    @pl.when(step == pl.num_programs(0) - 1)
    def _():
        half = held.shape[1] // 2
        copies = []
        for side, bits in enumerate((BITS_X, BITS_Y)):
            for k, bit in enumerate(bits):
                copies.append(
                    pltpu.make_async_copy(
                        held.at[at_block(order, bit, rows), side * half : (side + 1) * half],
                        outs[2 * (k // 4) + side].at[(k % 4) * rows : (k % 4 + 1) * rows, :],
                        sems.at[side, k],
                    )
                )
        run_copies(copies)


def store_apart(g, keep, send, cols, over_x):
    rows = g.shape[0] // 8
    for i, block in enumerate((0, 2, 1, 3) if over_x else (0, 1, 2, 3)):
        place = slice(i * rows, (i + 1) * rows)
        keep[place, cols] = g[block * rows : (block + 1) * rows]
        send[place, cols] = g[(4 + block) * rows : (5 + block) * rows]


def feed_back_body(rows, order, left_ref, right_ref, product_ref, h_ref, c_ref, mid_ref, *refs):
    weights, downs = refs[:16], refs[16:32]
    keep_l, send_l, keep_r, send_r, d_mid_ref, d_branch_ref, act_ref = refs[32:39]
    down, grad, total, held, sems = refs[39:]
    step = pl.program_id(0)

    @pl.when(step == 0)
    def _():
        half = down.shape[1] // 2
        run_copies(
            [
                pltpu.make_async_copy(
                    downs[8 * side + k],
                    down.at[at_block(order, at, rows), side * half : (side + 1) * half],
                    sems.at[side, k],
                )
                for side in range(2)
                for k, at in enumerate(BITS_Y)
            ]
        )
        held[...] = jnp.zeros_like(held)

    size = left_ref.shape[1]
    last = pl.num_programs(0) - 2
    whole = slice(0, size)
    both = held[...]
    g = dot(h_ref[...], both, TN, BF16)
    store_apart(g[:, :size], keep_l, send_l, whole, True)
    store_apart(g[:, size:], keep_r, send_r, whole, False)
    wide = jnp.concatenate([stacked(weights[:8]), stacked(weights[8:])], axis=1)
    grad[...] += dot(both, wide, NT)

    block = jnp.minimum(step, last)
    w_down = down[pl.ds(pl.multiple_of(block * size, size), size), :]
    grad_product = dot(c_ref[...], w_down, NT)
    held[:, :size] = (grad_product * right_ref[...].astype(F32)).astype(BF16)
    held[:, size:] = (grad_product * left_ref[...].astype(F32)).astype(BF16)

    @pl.when(step == 0)
    def _():
        grad[...] = jnp.zeros_like(grad)

    @pl.when(step == pl.num_programs(0) - 1)
    def _():
        mid = mid_ref[...]
        act_ref[...] = (mid + dot(product_ref[...], down[...], NN)).astype(BF16)
        restored(order, grad[...], total)
        g = total[...]
        scale = lax.rsqrt(jnp.mean(mid * mid, axis=-1, keepdims=True) + EPS)
        inner = jnp.mean(g * mid, axis=-1, keepdims=True) * (scale * scale * scale)
        d_mid = c_ref[...].astype(F32) + scale * g - mid * inner
        d_mid_ref[...] = d_mid
        d_branch_ref[...] = d_mid.astype(BF16)


def gate_out_back_body(order, d_ref, mix_ref, u_ref, *refs):
    du_ref, dm_ref, held = refs[8:]
    restored(order, dot(d_ref[...], stacked(refs[:8]), NT), held)
    dg = held[...]
    mix = mix_ref[...].astype(F32)
    u = u_ref[...]
    sig = sigmoid(u)
    scale = lax.rsqrt(jnp.mean(mix * mix, axis=-1, keepdims=True) + EPS)
    du_ref[...] = (dg * mix * scale * (sig * (1.0 + u * (1.0 - sig)))).astype(BF16)
    dn = dg * (u * sig)
    inner = jnp.mean(dn * mix, axis=-1, keepdims=True) * (scale * scale * scale)
    dm_ref[...] = (scale * dn - mix * inner).astype(BF16)


def in_back_body(order, x_ref, d_mid_ref, du_ref, d_ref, *refs):
    low, high, gates, (out, grad, held) = refs[:8], refs[8:16], refs[16:24], refs[24:]
    step = pl.program_id(0)

    @pl.when(step == 0)
    def _():
        grad[...] = dot(du_ref[...], stacked(gates), NT)

    grad[...] += dot(d_ref[0, 0], stacked(low), NT) + dot(d_ref[1, 0], stacked(high), NT)

    @pl.when(step == pl.num_programs(0) - 1)
    def _():
        restored(order, grad[...], held)
        g = held[...]
        x = x_ref[...].astype(F32)
        scale = lax.rsqrt(jnp.mean(x * x, axis=-1, keepdims=True) + EPS)
        inner = jnp.mean(g * x, axis=-1, keepdims=True) * (scale * scale * scale)
        out[...] = (d_mid_ref[...] + scale * g - x * inner).astype(BF16)


def weight_grads_body(order, h_ref, gated_ref, d_ref, du, db, *outs):
    held, sems = outs[4:8], outs[8]
    step = pl.program_id(0)

    def copies(side):
        return [
            pltpu.make_async_copy(held[2 * side + i], outs[2 * side + i], sems.at[2 * side + i])
            for i in range(2)
        ]

    def run(side):
        terms = [(h_ref, d_ref.at[0, i]) for i in range(3)] + [(h_ref, du), (gated_ref, db)]
        for i, (lhs, d) in enumerate(terms):
            g = dot(lhs[...], d[...], TN, BF16)
            cols = slice(i * g.shape[1], (i + 1) * g.shape[1])
            store_apart(g, held[2 * side], held[2 * side + 1], cols, side == 0)
        for copy in copies(side):
            copy.start()

    @pl.when(step == 0)
    def _():
        run(0)

    @pl.when(step == 1)
    def _():
        run(1)
        for copy in copies(0) + copies(1):
            copy.wait()


class Chain:
    def __init__(self, fresh, factor, forward, parts):
        self.fresh, self.factor, self.forward, self.parts = fresh, factor, forward, parts
        self.seqs = fresh.shape[0]
        self.now = [fresh[s] for s in range(self.seqs)]
        self.got = [[] for _ in range(self.seqs)]
        self.turns = self.seqs + parts - 2

    def pass_on(self, s, hop):
        pair = (hop - 1, hop) if self.forward else (self.parts - hop, self.parts - hop - 1)
        self.got[s].append(lax.ppermute(self.now[s], "heads", [pair]))

    def begin(self):
        for s in range(self.seqs):
            self.pass_on(s, 1)

    def at(self, turn):
        return [(s, turn - s) for s in range(self.seqs) if 1 <= turn - s < self.parts]

    def arrivals(self, turn):
        self.new = [self.got[s][hop - 1] for s, hop in self.at(turn)]
        return self, "new"

    def go_on(self, turn):
        for (s, hop), new in zip(self.at(turn), self.new):
            self.got[s][hop - 1] = new
            if hop + 1 < self.parts:
                arrived = new.astype(F32) * self.factor[s][:, None, None]
                self.now[s] = (self.fresh[s].astype(F32) + arrived).astype(BF16)
                self.pass_on(s, hop + 1)

    def result(self):
        return jnp.stack([functools.reduce(lambda a, b: a + b, g) for g in self.got])


class Layer:
    def __init__(self, tokens, doc_lengths, cotangent):
        seqs, length, width = tokens.shape
        self.seqs, self.length, self.width, self.count = seqs, length, width, seqs * length
        self.here = lax.axis_index("rows")
        self.place = lax.axis_index("heads")
        self.order = places(self.here, self.place)
        self.x = tokens.reshape(self.count, width)
        self.dy = cotangent.reshape(self.count, width)

        ends = jnp.cumsum(doc_lengths, axis=-1, dtype=jnp.int32)[:, :-1]

        def ids_at(where):
            return jnp.sum((where[None, :, None] >= ends[:, None, :]).astype(jnp.int32), axis=-1)

        start = self.place * length
        positions = start + jnp.arange(length, dtype=jnp.int32)
        ids = ids_at(positions)
        before = jnp.where(self.place > 0, ids_at(jnp.reshape(start - 1, (1,))), -1)
        final = ids[:, -1:]
        link = (ids == before).astype(F32)[:, :, None]
        tail = (ids == final).astype(F32)[:, :, None]
        slopes = jnp.array([slope_of(h) for h in range(HEADS)], F32)
        self.factor = (final == before).astype(F32) * jnp.exp(-slopes * length)[None, :]
        theta = jnp.exp(-math.log(10000.0) * jnp.arange(HEAD_DIM, dtype=F32) / HEAD_DIM)
        angle = positions.astype(F32)[:, None] * theta[None, :]

        table = pl.BlockSpec((length, HEAD_DIM), lambda s, *_: (0, 0))
        one_col = pl.BlockSpec((1, length, 1), lambda s, *_: (s, 0, 0))
        one_row = pl.BlockSpec((1, 1, length), lambda s, *_: (s, 0, 0))
        self.turn = [(jnp.cos(angle), table), (jnp.sin(angle), table)]
        self.link = link, one_col
        self.tail = tail, one_col
        self.masks = [(ids[:, :, None], one_col), (ids[:, None, :], one_row), self.link]
        self.seq = pl.BlockSpec((1, length, width), lambda s, *_: (s, 0, 0))
        self.state = pl.BlockSpec(
            (1, HEADS, 2 * HEAD_DIM, HEAD_DIM), lambda s, *_: (s, 0, 0, 0)
        )
        self.states = (seqs, HEADS, 2 * HEAD_DIM, HEAD_DIM), BF16, self.state
        step = min(self.count, 256)
        self.grid = (self.count // step,)
        self.wide = rows_spec(step, width)

    def rows(self, body, ins, types, order=None):
        return call(
            body, self.grid, self.order, [(a, self.wide) for a in ins],
            [((self.count, self.width), t, self.wide) for t in types],
        )

    def seqwise(self, body, ins, outs):
        shape = (self.seqs, self.length, self.width)
        ins = [i if isinstance(i, tuple) else (i.reshape(shape), self.seq) for i in ins]
        outs = [o if isinstance(o, tuple) else (shape, o, self.seq) for o in outs]
        got = call(body, (self.seqs,), self.order, ins, outs)
        return [g.reshape(self.count, self.width) if g.shape == shape else g for g in got]

    def norm(self):
        return self.rows(norm_body, [self.x], [BF16])

    def fresh(self, k_pre, v_pre):
        return self.seqwise(fresh_body, [k_pre, v_pre] + self.turn + [self.tail], [self.states])[0]

    def mix(self, q_pre, k_pre, v_pre, u_pre, state_in):
        ins = [q_pre, k_pre, v_pre, u_pre] + self.turn + self.masks + [(state_in, self.state)]
        return self.seqwise(mix_body, ins, [BF16, BF16])

    def mid(self, branch):
        return self.rows(mid_body, [self.x, branch], [F32, BF16])

    def mid_back(self, x_mid, grad):
        return self.rows(norm_back_body, [x_mid, self.dy, grad], [F32, BF16])

    def in_back(self, d_mid, grad):
        return self.rows(norm_back_body, [self.x, d_mid, grad], [F32])[0]

    def gate_back(self, q_pre, u_pre, mix, d_gated):
        ins = [q_pre, u_pre, mix, d_gated] + self.turn + [self.link]
        return self.seqwise(gate_back_body, ins, [BF16, BF16, self.states])

    def mix_back(self, q_pre, k_pre, v_pre, d_mix, state_in):
        ins = [q_pre, k_pre, v_pre, d_mix] + self.turn + self.masks + [(state_in, self.state)]
        return self.seqwise(mix_back_body, ins, [BF16, F32, F32])

    def state_back(self, k_pre, v_pre, dk_near, dv_near, d_state):
        ins = [k_pre, v_pre, dk_near, dv_near] + self.turn + [self.tail, (d_state, self.state)]
        return self.seqwise(state_back_body, ins, [BF16, BF16])


def plainly(layer, heads_count, weights):
    w_query, w_key, w_value, w_gate, w_out, w_left, w_right, w_down = (
        lax.all_gather(w, "rows", axis=0, tiled=True) for w in weights
    )

    def carried(fresh, forward):
        chain = Chain(fresh, layer.factor, forward, heads_count)
        chain.begin()
        for turn in range(1, chain.turns + 1):
            chain.arrivals(turn)
            chain.go_on(turn)
        return chain.result()

    def gradient(lhs, d):
        total = lax.psum_scatter(dot(lhs, d, TN, BF16), "rows", scatter_dimension=0, tiled=True)
        return lax.psum_scatter(total, "heads", scatter_dimension=1, tiled=True).astype(F32)

    (h_in,) = layer.norm()
    q_pre, k_pre, v_pre, u_pre = (
        dot(h_in, w, NN) for w in (w_query, w_key, w_value, w_gate)
    )
    state_in = carried(layer.fresh(k_pre, v_pre), True)
    mix, gated = layer.mix(q_pre, k_pre, v_pre, u_pre, state_in)
    x_mid, h_mid = layer.mid(dot(gated, w_out, NN))
    left, right = dot(h_mid, w_left, NN), dot(h_mid, w_right, NN)
    product = (left * right).astype(BF16)
    activations = (x_mid + dot(product, w_down, NN)).astype(BF16)
    grad_product = dot(layer.dy, w_down, NT)
    d_left = (grad_product * right).astype(BF16)
    d_right = (grad_product * left).astype(BF16)
    d_mid, d_branch = layer.mid_back(
        x_mid, dot(d_left, w_left, NT) + dot(d_right, w_right, NT)
    )
    d_u, d_mix, d_fresh = layer.gate_back(q_pre, u_pre, mix, dot(d_branch, w_out, NT))
    d_state = carried(d_fresh, False)
    d_q, dk_near, dv_near = layer.mix_back(q_pre, k_pre, v_pre, d_mix, state_in)
    d_k, d_v = layer.state_back(k_pre, v_pre, dk_near, dv_near, d_state)
    grad_in = (
        dot(d_q, w_query, NT) + dot(d_u, w_gate, NT) + dot(d_k, w_key, NT) + dot(d_v, w_value, NT)
    )
    input_grad = layer.in_back(d_mid, grad_in)
    pairs = (
        (h_in, d_q), (h_in, d_k), (h_in, d_v), (h_in, d_u), (gated, d_branch),
        (h_mid, d_left), (h_mid, d_right), (product, layer.dy),
    )
    return (activations, input_grad) + tuple(gradient(lhs, d) for lhs, d in pairs)


class Row:
    def __init__(self, doc_lengths, length, width, here, head):
        self.length, self.width = length, width
        self.order = places(here, head)
        lengths = lax.dynamic_index_in_dim(doc_lengths, head, 0, keepdims=False)
        ends = jnp.cumsum(lengths, dtype=jnp.int32)[:-1]
        positions = jnp.arange(length, dtype=jnp.int32)
        ids = jnp.sum((positions[:, None] >= ends[None, :]).astype(jnp.int32), axis=-1)
        theta = jnp.exp(-math.log(10000.0) * jnp.arange(HEAD_DIM, dtype=F32) / HEAD_DIM)
        angle = positions.astype(F32)[:, None] * theta[None, :]

        def whole(rows, cols):
            return pl.BlockSpec((rows, cols), lambda *_: (0, 0))

        table = whole(length, HEAD_DIM)
        self.extra = [
            (jnp.cos(angle), table), (jnp.sin(angle), table),
            (ids[:, None], whole(length, 1)), (ids[None, :], whole(1, length)),
        ]
        self.heads = pl.BlockSpec((length, 2 * HEAD_DIM), lambda h, *_: (0, h))
        self.wide = rows_spec(min(length, 256), width)
        self.all = whole(length, width)
        self.block = math.gcd(length, 256)
        self.flops = 2 * length * width * width

    def norm(self, x):
        return self.by_rows(row_norm_body, [(x, self.wide)], [], [BF16], [BF16])

    def pieces(self, group, half, width=None):
        rows, whole = group.pieces[half].shape
        spec = pl.BlockSpec((rows, width or whole), lambda i, *_: (0, i if width else 0))
        return [(a, spec) for a in group.all(half)]

    def thirds(self, which=None, dtype=F32):
        half = self.width // 2
        if which is None:
            return pl.BlockSpec((2, self.length, half), lambda i, *_: (0, 0, i))
        pair = 2 * HEAD_DIM
        each = half // pair
        return pl.BlockSpec(
            (1, self.length, pair), lambda i, *_: (i // each, 0, which * each + i % each)
        )

    def project(self, h, qkv):
        half = self.width // 2
        return call(
            project_body, (3,), self.order,
            [(h, self.all)] + self.pieces(qkv, 0, half) + self.pieces(qkv, 1, half),
            [((2, self.length, 3 * half), F32, self.thirds())], flops=3 * self.flops,
        )[0]

    def column(self, block, offset=0):
        return pl.BlockSpec((self.length, block), lambda i, *_: (0, offset + i))

    def mix(self, pre):
        return call(
            functools.partial(row_mix_body, self.block), (HEADS // 2,), self.order,
            [(pre, self.thirds(i)) for i in range(3)] + self.extra,
            [((self.length, self.width), BF16, self.heads)], flops=self.flops * 3 // 8,
        )[0]

    def mix_back(self, pre, d_mix):
        pair, half = 2 * HEAD_DIM, self.width // 2
        each = half // pair
        spec = pl.BlockSpec((1, 3, self.length, pair), lambda i, *_: (i // each, 0, 0, i % each))
        return call(
            functools.partial(row_mix_back_body, self.block), (HEADS // 2,), self.order,
            [(pre, self.thirds(i)) for i in range(3)] + [(d_mix, self.heads)] + self.extra,
            [((2, 3, self.length, half), BF16, spec)], flops=self.flops,
        )[0]

    def by_rows(self, body, ins, weights, types, scratch):
        step = self.wide.block_shape[0]
        return call(
            body, (self.length // step,), self.order, ins + weights,
            [((self.length, self.width), t, self.wide) for t in types],
            scratch=[pltpu.VMEM((step, self.width), t) for t in scratch], flops=self.flops,
        )

    def out_mid(self, mix, h, x, uo):
        return self.by_rows(
            out_mid_body, [(mix, self.wide), (h, self.wide), (x, self.wide)],
            self.pieces(uo, 0) + self.pieces(uo, 1),
            [F32, BF16, F32, BF16], [BF16],
        )

    def gate_out_back(self, d_branch, mix, u_pre, uo):
        return self.by_rows(
            gate_out_back_body, [(d_branch, self.wide), (mix, self.wide), (u_pre, self.wide)],
            self.pieces(uo, 1), [BF16, BF16], [F32],
        )

    def left_right(self, h, ff):
        inner = ff.pieces[0].shape[1]
        block = math.gcd(inner, 1408)
        return call(
            left_right_body, (inner // block,), self.order,
            [(h, self.all)] + self.pieces(ff, 0, block) + self.pieces(ff, 1, block),
            [((self.length, inner), BF16, self.column(block))] * 3,
            flops=2 * self.flops * inner // self.width,
        )

    def down_grad(self, product, c):
        inner, half = product.shape[1], self.width // 2
        block = math.gcd(inner, 1408)
        rows = inner // 8
        got = call(
            functools.partial(down_grad_body, rows), (inner // block,), self.order,
            [(product, self.column(block)), (c, self.all)], [((4 * rows, half), BF16, HBM)] * 4,
            scratch=[pltpu.VMEM((inner, self.width), BF16), pltpu.SemaphoreType.DMA((2, 8))],
            flops=self.flops * inner // self.width,
        )
        return Reduce(self.order, got[2:], got[:2], [2, 4])

    def feed_back(self, left, right, product, h, c, x_mid, ff, down):
        inner, rows = ff.pieces[0].shape[1], down.pieces[0].shape[0]
        block = math.gcd(inner, 256)
        steps = inner // block

        def now(rows):
            return pl.BlockSpec((rows, block), lambda i, *_: (0, jnp.minimum(i, steps - 1)))

        def before(rows):
            return pl.BlockSpec((rows, block), lambda i, *_: (0, jnp.maximum(i - 1, 0)))

        full = (self.length, self.width)
        weights = [(a, before(ff.pieces[0].shape[0])) for a in ff.all(0) + ff.all(1)]
        return call(
            functools.partial(feed_back_body, rows), (steps + 1,), self.order,
            [(left, now(self.length)), (right, now(self.length))]
            + [(product, whole_spec(self.length, inner))]
            + [(a, self.all) for a in (h, c, x_mid)]
            + weights + [(a, HBM) for a in down.all(0) + down.all(1)],
            [((self.width // 2, inner), BF16, before(self.width // 2))] * 4
            + [(full, F32, self.all), (full, BF16, self.all), (full, BF16, self.all)],
            scratch=[pltpu.VMEM((inner, self.width), BF16)] + [pltpu.VMEM(full, F32)] * 2
            + [pltpu.VMEM((self.length, 2 * block), BF16), pltpu.SemaphoreType.DMA((2, 8))],
            flops=6 * self.flops * inner // self.width,
        )

    def in_back(self, x, d_mid, d, d_u, qkv, uo):
        half = self.width // 2
        full = (self.length, self.width)
        third = pl.BlockSpec((2, 1, self.length, half), lambda i, *_: (0, i, 0, 0))
        return call(
            in_back_body, (3,), self.order,
            [(x, self.all), (d_mid, self.all), (d_u, self.all), (d, third)]
            + self.pieces(qkv, 0, half) + self.pieces(qkv, 1, half) + self.pieces(uo, 0),
            [(full, BF16, self.all)], scratch=[pltpu.VMEM(full, F32)] * 2, flops=4 * self.flops,
        )[0]

    def weight_grads(self, h, gated, d, d_u, d_branch):
        half = self.width // 2
        shape = (half, 5 * half)
        thirds = pl.BlockSpec((1, 3, self.length, half), lambda i, *_: (i, 0, 0, 0))
        got = call(
            weight_grads_body, (2,), self.order,
            [(h, self.all), (gated, self.all)]
            + [(d, thirds), (d_u, self.column(half)), (d_branch, self.column(half))],
            [(shape, BF16, HBM)] * 4,
            scratch=[pltpu.VMEM(shape, BF16)] * 4 + [pltpu.SemaphoreType.DMA((4,))],
            flops=5 * self.flops,
        )
        return Reduce(self.order, got[1::2], got[::2], [2, 4])


def stepwise(tokens, doc_lengths, cotangent, weights):
    w_query, w_key, w_value, w_gate, w_out, w_left, w_right, w_down = weights
    size, width = tokens.shape[1:]
    length, half = 4 * size, width // 2
    here, head = lax.axis_index("rows"), lax.axis_index("heads")
    row = Row(doc_lengths, length, width, here, head)
    order = row.order
    v = types.SimpleNamespace()
    clock = Clock(order)
    tick = clock.tick

    def exchanged(a):
        return lax.all_to_all(a.reshape(4, size, width), "heads", 0, 0, tiled=True)

    def whole_row(a):
        return exchanged(a).reshape(length, width)

    inner = w_left.shape[1]
    uo = Gather([w_gate, w_out])
    uo.first()
    qkv = Gather(
        pack(order, [w_query, w_key, w_value], [[(i, at, half) for i in range(3)] for at in (0, half)])
    )
    qkv.first()
    v.x = whole_row(after(tokens, uo.near_x[0]))
    v.extra = [a for a, _ in row.extra]
    ff = Gather([w_left, w_right])
    v.c = cotangent
    tick((qkv, "near_x"), (qkv, "near_y"), (uo, "near_x"), (uo, "near_y"), (uo, "pieces"), (v, "c"), (v, "extra"))
    row.extra = [(a, spec) for a, (_, spec) in zip(v.extra, row.extra)]
    qkv.second()
    uo.second()
    qkv.cross("pieces", "near_x", "near_y")
    uo.cross("pieces", "near_x", "near_y")
    (v.h,) = row.norm(v.x)
    tick((qkv, "far"), (uo, "far"), (v, "h"), (ff, "pieces"))
    ff.first()
    ff.cross("pieces")
    qkv.cross("far")
    uo.cross("far")
    v.pre = row.project(v.h, qkv)
    v.mix = row.mix(v.pre)
    v.u_pre, v.gated, v.x_mid, v.h_mid = row.out_mid(v.mix, v.h, v.x, uo)
    v.down = w_down
    tick((v, "x_mid"), (v, "h_mid"), (ff, "near_x"), (ff, "near_y"), (v, "down"), (v, "c"))
    ff.second()
    v.c = whole_row(v.c)
    ff.cross("near_x", "near_y")
    v.down = pack(order, [v.down], [[(0, 0, half)], [(0, half, half)]])
    tick((ff, "far"), (v, "down"))
    down = Gather(v.down)
    ff.cross("far")
    down.first()
    down.cross("pieces")

    v.left, v.right, v.product = row.left_right(v.h_mid, ff)
    tick((v, "left"), (v, "right"), (v, "product"), (down, "near_x"), (down, "near_y"), (v, "c"))
    down.second()
    down.cross("near_x", "near_y")
    v.g_down = dot(v.product, v.c, TN, BF16)
    tick((v, "g_down"), (down, "far"), (v, "left"))
    v.sum_down = lax.psum_scatter(v.g_down, "rows", scatter_dimension=0, tiled=True)
    down.cross("far")
    tick((down, "far_other"), (v, "left"))
    keep_l, send_l, keep_r, send_r, v.d_mid, v.d_branch, v.act = row.feed_back(
        v.left, v.right, v.product, v.h_mid, v.c, v.x_mid, ff, down
    )
    r_ff = Reduce(order, [send_l, send_r], [keep_l, keep_r], [2, 4])
    tick((r_ff, "sends"), (v, "d_mid"), (v, "d_branch"), (v, "act"))
    r_ff.core()
    v.d_u, v.d_mix = row.gate_out_back(v.d_branch, v.mix, v.u_pre, uo)
    tick((r_ff, "theirs"), (v, "d_u"), (v, "d_mix"))
    r_ff.join_far()
    tick((r_ff, "far"), (r_ff, "theirs"))
    r_ff.first_far()
    r_ff.join_near()
    tick((r_ff, "near"), (v, "act"), (v, "d_mix"))
    r_ff.first_near()
    v.act = exchanged(v.act)
    v.d = row.mix_back(v.pre, v.d_mix)
    tick((v, "d"), (r_ff, "got_far"))
    r_ff.join_first()
    tick((r_ff, "parts"), (v, "d"), (v, "sum_down"))
    r_ff.second()
    r_att = row.weight_grads(v.h, v.gated, v.d, v.d_u, v.d_branch)
    tick((r_att, "sends"), (r_ff, "got_near"), (v, "sum_down"))
    r_att.core()
    s_down = Settle(order, [[v.sum_down]], half // 2, [lambda z: z * (half // 2)])
    tick((r_att, "theirs"), (s_down, "out"), (v, "d"))
    s_down.first()
    r_att.join()
    v.back = row.in_back(v.x, v.d_mid, after(v.d, *r_att.both), v.d_u, qkv, uo)
    tick((r_att, "both"), (r_ff, "got_last"), (v, "back"), (s_down, "got"), (v, "act"))
    r_att.first()
    v.back = exchanged(v.back)
    quarter = inner // 4
    s_ff = r_ff.settle(quarter, [lambda z: z * quarter, lambda z: inner + z * quarter])
    s_down.join()
    tick((s_ff, "out"), (s_down, "out"))
    s_ff.first()
    tick((s_ff, "got"), (s_down, "out"), (s_down, "last"))
    s_ff.join()
    tick((s_ff, "out"), (s_ff, "last"), (s_down, "out"), (s_down, "last"))
    s_ff.second()
    s_down.second()
    tick((r_att, "got_near"))
    r_att.join_first_both()
    tick((r_att, "parts"))
    r_att.second()
    tick((s_down, "got_near"), (s_down, "got_far"))
    (v.g_down,) = s_down.result()
    tick((r_att, "got_last"), (v, "g_down"))
    s_att = r_att.settle(
        half // 2,
        [
            lambda z, i=i: (z // 2) * 5 * half + i * half + (z % 2) * (half // 2)
            for i in range(5)
        ],
    )
    tick((s_att, "out"), (v, "back"))
    s_att.first()
    v.back = v.back.astype(F32)
    tick((s_ff, "got_near"), (s_ff, "got_far"), (v, "back"))
    v.g_ff = s_ff.result()
    tick((s_att, "got"), (v, "g_ff"))
    s_att.join()
    tick((s_att, "out"), (s_att, "last"))
    s_att.second()
    g_query, g_key, g_value, g_gate, g_out = s_att.result()
    g_left, g_right = v.g_ff
    return (
        v.act, v.back, g_query, g_key, g_value, g_gate, g_out, g_left, g_right, v.g_down
    )


def on_device(rows_count, heads_count, tokens, doc_lengths, cotangent, *weights):
    if rows_count == 8 and heads_count == 4 and tokens.shape[0] == 4:
        return stepwise(tokens, doc_lengths, cotangent, weights)
    layer = Layer(tokens, doc_lengths, cotangent)
    activations, input_grad, *grads = plainly(layer, heads_count, weights)
    return (activations.reshape(tokens.shape), input_grad.reshape(tokens.shape), *grads)


def solution(mesh):
    sizes = dict(mesh.shape)
    tokens = P("rows", "heads", None)
    weights = P("rows", None)
    grads = P("rows", "heads")
    return jax.shard_map(
        functools.partial(on_device, sizes["rows"], sizes["heads"]),
        mesh=mesh,
        in_specs=(tokens, weights, tokens) + (weights,) * 8,
        out_specs=(tokens, tokens) + (grads,) * 8,
        check_vma=False,
    )
```
